32 devices in a mesh: node: 8 (over z, core), dev: 4 (over y, x).
Axes of the slice: x: 2, y: 2, z: 4, core: 2. Of those that a mesh axis runs over, the one named last changes fastest.
Arguments:
- density: float32 [192, 64, 4096], P(('node', 'dev')), may hold values from -18 to 18
- owner_counts: int32 [32], P(('node', 'dev')), may hold values from 1 to 6, as said below
Outputs:
- coefficients: float32 [192, 64, 4096], P(('node', 'dev'))
The draws below stay inside these ranges and needn't reach their ends.
Inputs may be any that keep to these rules, and one draw needn't show every extreme that they name: `owner_counts`: every device holds at least one block, the counts sum to 96, and some device holds exactly 6.
All inputs are finite; a program needn't handle non-finite values.
Results may differ from the reference program's by a relative error of at most 0.00002.
Values sent between devices are 32-bit elements; how exact they have to be, the bound alone decides.
No kernel may reach another device: no remote copies, remote signals or barrier semaphores. Data moves between devices by JAX's collectives and lax.ppermute only.
A program may use at most 128 MiB of HBM per device.

```python
import jax
import jax.numpy as jnp
from jax import lax

B = 64
BLK_DEV = 3
SLOTS = 6
NBLK = 96
Q = 16
M = 32
DEVICES = 32


def draw_density(key, part):
    rows_total = DEVICES * SLOTS
    shape_full = (rows_total, B, B, B)
    keys_all = jax.random.split(key, 8)
    summed = jax.random.truncated_normal(keys_all[0], -3.0, 3.0, shape_full, jnp.float32)
    for exponent in range(1, 6):
        cell_span = 2 ** exponent
        if cell_span <= B // 2:
            coarse_edge = B // cell_span
            coarse_shape = (rows_total, coarse_edge, 1, coarse_edge, 1, coarse_edge, 1)
            component = jax.random.truncated_normal(keys_all[exponent], -3.0, 3.0, coarse_shape, jnp.float32)
            wide_shape = (rows_total, coarse_edge, cell_span, coarse_edge, cell_span, coarse_edge, cell_span)
            summed = summed + jnp.broadcast_to(component, wide_shape).reshape(shape_full)
    return summed.reshape(rows_total, B, B * B)


def spread_even(total_sum, width):
    base_value = total_sum // width
    remainder = total_sum % width
    return (base_value + (jnp.arange(width, dtype=jnp.int32) < remainder).astype(jnp.int32)).astype(jnp.int32)


def draw_owner_counts(key, part):
    quad_total = DEVICES // 4
    per_device = BLK_DEV
    keys_all = jax.random.split(key, 8)
    pattern_kind = jax.random.randint(keys_all[0], (quad_total,), 0, 2)
    first_pick = jax.random.randint(keys_all[1], (quad_total,), 1, 2 * per_device - 1)
    room_left = 2 * per_device - 1 - first_pick
    second_pick = 1 + jax.random.randint(keys_all[2], (quad_total,), 0, 1 << 20) % room_left
    heavy_pattern = jnp.stack([jnp.full((quad_total,), 2 * per_device, jnp.int32), first_pick, second_pick, 2 * per_device - first_pick - second_pick], 1)
    spread_one = jax.random.randint(keys_all[3], (quad_total,), 1 - per_device, per_device)
    spread_two = jax.random.randint(keys_all[4], (quad_total,), 1 - per_device, per_device)
    even_pattern = jnp.stack([per_device + spread_one, per_device - spread_one, per_device + spread_two, per_device - spread_two], 1)
    chosen = jnp.where(pattern_kind[:, None] == 0, heavy_pattern, even_pattern)
    rotate_by = jax.random.randint(keys_all[5], (quad_total,), 0, 4)
    positions = (jnp.arange(4)[None, :] + rotate_by[:, None]) % 4
    counts = jnp.take_along_axis(chosen, positions, axis=1).reshape(DEVICES).astype(jnp.int32)
    window_start = DEVICES // 2 - 16
    prefix_sum = jnp.sum(counts[:window_start]).astype(jnp.int32)
    fill_total = 32 * per_device - 8
    extra_room = fill_total - 2 * per_device - 19 - 11
    base_head = 2 * per_device + 19 + extra_room * 12 // 23
    head_total = (base_head - (base_head + prefix_sum) % 8).astype(jnp.int32)
    head_rest = jnp.roll(spread_even(head_total - 2 * per_device, 12), jax.random.randint(keys_all[6], (), 0, 12))
    tail_fill = jnp.roll(spread_even(fill_total - head_total, 11), jax.random.randint(keys_all[7], (), 0, 11))
    singles = jnp.ones((8,), jnp.int32)
    window = jnp.concatenate([jnp.full((1,), 2 * per_device, jnp.int32), head_rest, singles, tail_fill]).astype(jnp.int32)
    counts = lax.dynamic_update_slice(counts, window, (window_start,))
    return counts.astype(jnp.int32)


def setup_inputs(seed: int = 0) -> dict:
    key_list = jax.random.split(jax.random.key(seed), 3)
    return {
        "density": draw_density(jax.random.fold_in(key_list[2], 71), 0),
        "owner_counts": draw_owner_counts(jax.random.fold_in(key_list[2], 71), 0),
    }


ALPHA_LIFT = -1.586134342059924
BETA_LIFT = -0.052980118572961
GAMMA_LIFT = 0.882911075530934
DELTA_LIFT = 0.443506852043971
SCALE_LIFT = 1.230174104914001
INVERSE_SCALE = 1.0 / SCALE_LIFT


def lift_front(values):
    length = values.shape[0]
    paired = values.reshape((length // 2, 2) + values.shape[1:])
    low_part = paired[:, 0]
    high_part = paired[:, 1]
    high_part = high_part + ALPHA_LIFT * (low_part + jnp.concatenate([low_part[1:], low_part[-1:]], 0))
    low_part = low_part + BETA_LIFT * (jnp.concatenate([high_part[:1], high_part[:-1]], 0) + high_part)
    high_part = high_part + GAMMA_LIFT * (low_part + jnp.concatenate([low_part[1:], low_part[-1:]], 0))
    low_part = low_part + DELTA_LIFT * (jnp.concatenate([high_part[:1], high_part[:-1]], 0) + high_part)
    return jnp.concatenate([low_part * INVERSE_SCALE, high_part * SCALE_LIFT], 0)


def one_level(volume):
    for axis_number in range(3):
        volume = jnp.moveaxis(lift_front(jnp.moveaxis(volume, axis_number, 0)), 0, axis_number)
    return volume


def corner_level(volume, corner_edge):
    inner = one_level(volume[:corner_edge, :corner_edge, :corner_edge])
    return volume.at[:corner_edge, :corner_edge, :corner_edge].set(inner)


def fine_levels(block_cube):
    return corner_level(one_level(block_cube), B // 2)


def coarse_levels(merged):
    return corner_level(corner_level(one_level(merged), M // 2), M // 4)


def assemble(pieces):
    return jnp.transpose(pieces.reshape(2, 2, 2, Q, Q, Q), (2, 3, 1, 4, 0, 5)).reshape(M, M, M)


def split_octet(merged):
    return jnp.transpose(merged.reshape(2, Q, 2, Q, 2, Q), (4, 2, 0, 1, 3, 5)).reshape(8, Q, Q, Q)


def reference(density, owner_counts):
    counts = owner_counts.astype(jnp.int32)
    starts = (jnp.cumsum(counts) - counts).astype(jnp.int32)
    blocks = density.reshape(DEVICES * SLOTS, B, B, B)
    lowpass = lax.map(lambda block_cube: fine_levels(block_cube)[:Q, :Q, :Q], blocks)
    block_ids = jnp.arange(NBLK, dtype=jnp.int32)
    owners = (jnp.sum((starts[None, :] <= block_ids[:, None]).astype(jnp.int32), axis=1) - 1).astype(jnp.int32)
    row_index = (owners * SLOTS + block_ids - starts[owners]).astype(jnp.int32)
    octets = jax.vmap(assemble)(lowpass[row_index].reshape(NBLK // 8, 8, Q, Q, Q))
    coarse = lax.map(coarse_levels, octets)
    corners = jax.vmap(split_octet)(coarse).reshape(NBLK, Q, Q, Q)
    slot_corner = jnp.zeros((DEVICES * SLOTS, Q, Q, Q), jnp.float32).at[row_index].set(corners)
    slot_ids = jnp.arange(DEVICES * SLOTS, dtype=jnp.int32)
    live_slots = (slot_ids % SLOTS) < counts[slot_ids // SLOTS]

    def finish_block(inputs):
        block_cube, corner_cube, is_live = inputs
        finished = fine_levels(block_cube).at[:Q, :Q, :Q].set(corner_cube)
        return jnp.where(is_live, finished, jnp.zeros_like(finished))

    result = lax.map(finish_block, (blocks, slot_corner, live_slots))
    return result.reshape(DEVICES * SLOTS, B, B * B)
```

```python
import functools

import jax
import jax.numpy as jnp
import numpy as np
from jax import lax
from jax.experimental import pallas as pl
from jax.experimental.pallas import tpu as pltpu
from jax.sharding import PartitionSpec as P

ALPHA = -1.586134342059924
BETA = -0.052980118572961
GAMMA = 0.882911075530934
DELTA = 0.443506852043971
SCALE = 1.230174104914001
SQUARE = SCALE * SCALE
F32 = jnp.float32
BF16 = jnp.bfloat16
AXES = ("node", "dev")
MIB = 1 << 20


def pass_matrix(n):
    low, high = np.eye(n)[0::2], np.eye(n)[1::2]

    def after(v):
        return np.concatenate([v[1:], v[-1:]], 0)

    def before(v):
        return np.concatenate([v[:1], v[:-1]], 0)

    high = high + ALPHA * (low + after(low))
    low = low + BETA * (before(high) + high)
    high = high + GAMMA * (low + after(low))
    low = low + DELTA * (before(high) + high)
    return np.concatenate([low / SCALE, high * SCALE], 0)


def two_terms(matrix):
    matrix = np.asarray(matrix, np.float32)
    first = matrix.astype(BF16)
    return first, (matrix - first.astype(np.float32)).astype(BF16)


def left_terms(matrix):
    first, second = two_terms(matrix)
    return np.concatenate([first, second, first], 1)


def split(value):
    first = value.astype(BF16)
    return first, (value - first.astype(F32)).astype(BF16)


def dot(left, right):
    return jnp.dot(left, right, preferred_element_type=F32)


def times(value, first, second):
    high, low = split(value)
    return dot(high, first) + dot(low, first) + dot(high, second)


def times_left(terms, value):
    high, low = split(value)
    return dot(terms, jnp.concatenate([high, high, low], 0))


def lowpass_kernel(x_ref, wh_ref, wl_ref, ax_ref, out_ref, acc_ref):
    step = pl.program_id(0)
    slots, edge, width = x_ref.shape
    part = times(x_ref[...].reshape(slots * edge, width), wh_ref[...], wl_ref[...])

    @pl.when(step == 0)
    def _():
        acc_ref[...] = part

    @pl.when(step > 0)
    def _():
        acc_ref[...] += part

    @pl.when(step == pl.num_programs(0) - 1)
    def _():
        for slot in range(slots):
            out_ref[slot] = times_left(ax_ref[...], acc_ref[pl.ds(slot * edge, edge), :])


def lowpass_call(density):
    slots, edge, plane = density.shape
    quarter = edge // 4
    two_levels = pass_matrix(edge // 2)[:quarter] @ pass_matrix(edge)[: edge // 2]
    first, second = two_terms(np.kron(two_levels.T, two_levels.T))
    terms = left_terms(two_levels)
    steps = 8
    width = plane // steps
    cols = quarter * quarter
    return pl.pallas_call(
        lowpass_kernel,
        grid=(steps,),
        in_specs=[
            pl.BlockSpec((slots, edge, width), lambda j: (0, 0, j)),
            pl.BlockSpec((width, cols), lambda j: (j, 0)),
            pl.BlockSpec((width, cols), lambda j: (j, 0)),
            pl.BlockSpec(terms.shape, lambda j: (0, 0)),
        ],
        out_specs=pl.BlockSpec((slots, quarter, cols), lambda j: (0, 0, 0)),
        out_shape=jax.ShapeDtypeStruct((slots, quarter, cols), F32),
        scratch_shapes=[pltpu.VMEM((slots * edge, cols), F32)],
        compiler_params=pltpu.CompilerParams(vmem_limit_bytes=24 * MIB),
        cost_estimate=pl.CostEstimate(
            flops=6 * slots * edge * plane * cols, bytes_accessed=10 * MIB, transcendentals=0
        ),
        name="lowpass",
    )(density, first, second, terms)


def lift(low, high, low_end, high_end, scaled):
    up = SQUARE if scaled else 1.0
    count = len(low)

    def raise_high(factor):
        last = low_end(low)
        for i in range(count):
            follow = low[i + 1] if i + 1 < count else last
            high[i] = high[i] + (factor * up) * (low[i] + follow)

    def raise_low(factor):
        previous = high_end(high)
        for i in range(count):
            low[i] = low[i] + (factor / up) * (previous + high[i])
            previous = high[i]

    raise_high(ALPHA)
    raise_low(BETA)
    raise_high(GAMMA)
    raise_low(DELTA)


def fine_kernel(
    count_ref, x_ref, w1h_ref, w1l_ref, w2h_ref, w2l_ref, out_ref, xh_ref, xl_ref, y_ref, z_ref, c_ref, d_ref
):
    slot = pl.program_id(0)
    edge = x_ref.shape[1]
    pairs = x_ref.shape[2] // 256
    half = edge // 2
    lane = lax.broadcasted_iota(jnp.int32, (8, 128), 1)
    row = lax.broadcasted_iota(jnp.int32, (8, 128), 0)
    front = lane < 64
    inner = (lane & 63) < half

    def turn(value):
        return pltpu.roll(value, 64, 1)

    def low_end_lanes(low):
        return jnp.where(front, turn(low[0]), low[-1])

    def high_end_lanes(high):
        return jnp.where(front, high[0], turn(high[-1]))

    def low_end_rows(low):
        return jnp.where(row < 7, pltpu.roll(low[0], 7, 0), low[-1])

    def high_end_rows(high):
        return jnp.where(row > 0, pltpu.roll(high[-1], 1, 0), high[0])

    @pl.when(slot >= count_ref[0])
    def _():
        out_ref[...] = jnp.zeros_like(out_ref)

    @pl.when(slot < count_ref[0])
    def _():
        for j in range(pairs):
            for q in range(2):
                tile = x_ref[0, :, pl.ds((j + q * pairs) * 128, 128)]
                high, low = split(tile)
                xh_ref[pl.ds(j * edge, edge), pl.ds(q * 128, 128)] = high
                xl_ref[pl.ds(j * edge, edge), pl.ds(q * 128, 128)] = low
        lifted = (
            dot(xh_ref[...], w1h_ref[...])
            + dot(xl_ref[...], w1h_ref[...])
            + dot(xh_ref[...], w1l_ref[...])
        )
        y_ref[0] = lifted[:, :128].reshape(pairs, edge, 128)
        y_ref[1] = lifted[:, 128:].reshape(pairs, edge, 128)

        @pl.loop(0, edge // 8)
        def _(r):
            rows = pl.ds(pl.multiple_of(r * 8, 8), 8)
            low = [y_ref[0, j, rows, :] for j in range(pairs)]
            high = [y_ref[1, j, rows, :] for j in range(pairs)]
            lift(low, high, low_end_lanes, high_end_lanes, True)
            for j in range(pairs):
                y_ref[0, j, rows, :] = low[j]
                y_ref[1, j, rows, :] = high[j]

        for part in range(2):

            @pl.loop(0, pairs // 2)
            def _(t):
                made = []
                for u in range(2):
                    j = 2 * t + u
                    low = [y_ref[part, j, pl.ds(2 * m, 8, stride=8), :] for m in range(4)]
                    high = [y_ref[part, j, pl.ds(2 * m + 1, 8, stride=8), :] for m in range(4)]
                    lift(low, high, low_end_rows, high_end_rows, False)
                    low = [v * (1.0 / SCALE) for v in low]
                    high = [v * SCALE for v in high]
                    if part == 0:
                        for m in range(4):
                            c_ref[u, t, pl.ds(8 * m, 8), :] = low[m]
                    made.append(low + high)
                for m in range(8):
                    a, b = made[0][m], made[1][m]
                    rows = pl.ds((m % 4) + half * (m // 4), 8, stride=4)
                    z_ref[part * pairs + t, rows, :] = jnp.where(front, a, turn(b))
                    z_ref[part * pairs + pairs // 2 + t, rows, :] = jnp.where(front, turn(a), b)

        corner = jnp.concatenate(
            [c_ref[0].reshape(pairs // 2 * 32, 128), c_ref[1].reshape(pairs // 2 * 32, 128)], 1
        )
        lifted = times(corner, w2h_ref[...], w2l_ref[...])
        c_ref[0] = lifted[:, :128].reshape(pairs // 2, 32, 128)
        c_ref[1] = lifted[:, 128:].reshape(pairs // 2, 32, 128)

        @pl.loop(0, 4)
        def _(r):
            rows = pl.ds(pl.multiple_of(r * 8, 8), 8)
            low = [c_ref[0, j, rows, :] for j in range(pairs // 2)]
            high = [c_ref[1, j, rows, :] for j in range(pairs // 2)]
            lift(low, high, low_end_lanes, high_end_lanes, True)
            for j in range(pairs // 2):
                c_ref[0, j, rows, :] = low[j]
                c_ref[1, j, rows, :] = high[j]

        for part in range(2):

            @pl.loop(0, pairs // 4)
            def _(t):
                made = []
                for u in range(2):
                    j = 2 * t + u
                    low = [c_ref[part, j, pl.ds(16 * m, 8), :] for m in range(2)]
                    high = [c_ref[part, j, pl.ds(16 * m + 8, 8), :] for m in range(2)]
                    lift(low, high, low_end_rows, high_end_rows, False)
                    low = [v * (1.0 / SCALE) for v in low]
                    high = [v * SCALE for v in high]
                    made.append(low + high)
                for m in range(4):
                    a, b = made[0][m], made[1][m]
                    rows = pl.ds((m % 2) + half // 2 * (m // 2), 8, stride=2)
                    d_ref[part * (pairs // 2) + t, rows, :] = jnp.where(front, a, turn(b))
                    d_ref[part * (pairs // 2) + pairs // 4 + t, rows, :] = jnp.where(front, turn(a), b)

        for t in range(2 * pairs):
            for r in range(edge // 8):
                rows = pl.ds(8 * r, 8)
                value = z_ref[t, rows, :]
                if t < pairs and r < half // 8:
                    value = jnp.where(inner, d_ref[t, rows, :], value)
                out_ref[0, rows, pl.ds(t * 128, 128)] = value


def fine_call(owner_counts, density):
    slots, edge, plane = density.shape
    half = edge // 2
    pairs = plane // 256
    one = pass_matrix(edge).T
    zero = np.zeros_like(one)
    w1 = np.block(
        [
            [one / SCALE, zero, zero, zero],
            [zero, zero, one * SCALE, zero],
            [zero, one / SCALE, zero, zero],
            [zero, zero, zero, one * SCALE],
        ]
    )
    two = np.zeros_like(one)
    two[:half, :half] = pass_matrix(half).T
    w2 = np.kron(np.diag([1 / SCALE, 1 / SCALE, SCALE, SCALE]), two)
    w1h, w1l = two_terms(w1)
    w2h, w2l = two_terms(w2)
    fixed = pl.BlockSpec((256, 256), lambda s: (0, 0))
    return pl.pallas_call(
        fine_kernel,
        grid=(slots,),
        in_specs=[
            pl.BlockSpec(memory_space=pltpu.SMEM),
            pl.BlockSpec((1, edge, plane), lambda s: (s, 0, 0)),
            fixed,
            fixed,
            fixed,
            fixed,
        ],
        out_specs=pl.BlockSpec((1, edge, plane), lambda s: (s, 0, 0)),
        out_shape=jax.ShapeDtypeStruct(density.shape, F32),
        scratch_shapes=[
            pltpu.VMEM((pairs * edge, 256), BF16),
            pltpu.VMEM((pairs * edge, 256), BF16),
            pltpu.VMEM((2, pairs, edge, 128), F32),
            pltpu.VMEM((2 * pairs, edge, 128), F32),
            pltpu.VMEM((2, pairs // 2, 32, 128), F32),
            pltpu.VMEM((pairs, 32, 128), F32),
        ],
        compiler_params=pltpu.CompilerParams(vmem_limit_bytes=32 * MIB),
        cost_estimate=pl.CostEstimate(
            flops=6 * slots * edge * plane * 256, bytes_accessed=12 * MIB, transcendentals=0
        ),
        name="fine",
    )(owner_counts, density, w1h, w1l, w2h, w2l)


def coarse_kernel(
    index_ref,
    table_ref,
    wx_ref,
    wzh_ref,
    wzl_ref,
    wyh_ref,
    wyl_ref,
    w23h_ref,
    w23l_ref,
    wx2_ref,
    wx3_ref,
    fine_ref,
    out_ref,
    piece_ref,
    block_ref,
    corner_ref,
    piece_sem,
    corner_sem,
    out_sem,
):
    slots = corner_ref.shape[0]
    lane = lax.broadcasted_iota(jnp.int32, (16, 128), 1)

    def piece_copy(i):
        return pltpu.make_async_copy(table_ref.at[index_ref[i]], piece_ref.at[i], piece_sem.at[i])

    def window(s):
        return out_ref.at[s, pl.ds(0, 16), pl.ds(0, 1024)]

    for i in range(16):
        piece_copy(i).start()
    for s in range(slots):
        pltpu.make_async_copy(window(s), corner_ref.at[s], corner_sem.at[s]).start()
    for i in range(16):
        piece_copy(i).wait()

    first = [
        [times_left(wx_ref[...], piece_ref[pl.ds(o * 8 + 2 * q, 2)].reshape(32, 256)) for q in range(4)]
        for o in range(2)
    ]
    stacked = []
    for o in range(2):
        for cy in range(2):
            for yh in range(2):
                part = slice(yh * 128, yh * 128 + 128)
                stacked.append(jnp.concatenate([first[o][cy][:, part], first[o][2 + cy][:, part]], 1))
    lifted = times(jnp.concatenate(stacked, 0), wzh_ref[...], wzl_ref[...])
    stacked = []
    for o in range(2):
        for tz in range(2):
            stacked.append(
                jnp.concatenate(
                    [lifted[(o * 4 + u) * 32 : (o * 4 + u + 1) * 32, tz * 128 : tz * 128 + 128] for u in range(4)],
                    1,
                )
            )
    lifted = times(jnp.concatenate(stacked, 0), wyh_ref[...], wyl_ref[...])
    corner = []
    for o in range(2):
        for tz in range(2):
            for ty in range(2):
                for tx in range(2):
                    at = (o * 2 + tz) * 32 + tx * 16
                    value = lifted[at : at + 16, ty * 256 : ty * 256 + 256]
                    if tx + ty + tz == 0:
                        corner.append(value)
                    else:
                        block_ref[o * 8 + tx + 2 * ty + 4 * tz] = value
    both = times(jnp.concatenate(corner, 0), w23h_ref[...], w23l_ref[...])
    spot = lax.broadcasted_iota(jnp.int32, (16, 256), 1)
    depth = lax.broadcasted_iota(jnp.int32, (16, 256), 0)
    small = (depth < 8) & (spot < 128) & ((spot & 15) < 8)
    for o in range(2):
        mine = both[o * 16 : o * 16 + 16]
        second = times_left(wx2_ref[...], mine[:, :256])
        third = times_left(wx3_ref[...], mine[:, 256:])
        block_ref[o * 8] = jnp.where(small, third, second)

    for s in range(slots):
        pltpu.make_async_copy(window(s), corner_ref.at[s], corner_sem.at[s]).wait()
    for s in range(slots):

        @pl.when(index_ref[16 + slots + s] > 0)
        def _():
            value = block_ref[index_ref[16 + s]]
            for t in range(8):
                tile = value[:, (t // 4) * 128 : (t // 4) * 128 + 128]
                near = pltpu.roll(tile, (128 - 32 * (t % 4)) % 128, 1)
                far = pltpu.roll(tile, (64 - 16 - 32 * (t % 4)) % 128, 1)
                old = corner_ref[s, :, pl.ds(t * 128, 128)]
                new = jnp.where(lane < 16, near, jnp.where((lane >= 64) & (lane < 80), far, old))
                corner_ref[s, :, pl.ds(t * 128, 128)] = new
            pltpu.make_async_copy(corner_ref.at[s], window(s), out_sem.at[s]).start()

    for s in range(slots):

        @pl.when(index_ref[16 + slots + s] > 0)
        def _():
            pltpu.make_async_copy(corner_ref.at[s], window(s), out_sem.at[s]).wait()


def coarse_call(index, table, fine):
    slots, edge, plane = fine.shape
    m32, m16, m8 = pass_matrix(32), pass_matrix(16), pass_matrix(8)
    deep = np.zeros((16, 16))
    deep[:8] = m8 @ m16[:8]
    eye8, eye16 = np.eye(8), np.eye(16)
    wz = np.zeros((256, 256))
    for cz in range(2):
        for tz in range(2):
            wz[cz * 128 : cz * 128 + 128, tz * 128 : tz * 128 + 128] = np.kron(
                eye8, m32[tz * 16 : tz * 16 + 16, cz * 16 : cz * 16 + 16].T
            )
    w23 = np.concatenate([np.kron(m16.T, m16.T), np.kron(deep.T, deep.T)], 1)
    weights = [
        left_terms(m32),
        *two_terms(wz),
        *two_terms(np.kron(m32.T, eye16)),
        *two_terms(w23),
        left_terms(m16),
        left_terms(deep),
    ]
    anywhere = pl.BlockSpec(memory_space=pl.ANY)
    vmem = pl.BlockSpec(memory_space=pltpu.VMEM)
    return pl.pallas_call(
        coarse_kernel,
        in_specs=[pl.BlockSpec(memory_space=pltpu.SMEM), anywhere] + [vmem] * len(weights) + [anywhere],
        out_specs=anywhere,
        out_shape=jax.ShapeDtypeStruct(fine.shape, F32),
        scratch_shapes=[
            pltpu.VMEM((16, 16, 256), F32),
            pltpu.VMEM((16, 16, 256), F32),
            pltpu.VMEM((slots, 16, 1024), F32),
            pltpu.SemaphoreType.DMA((16,)),
            pltpu.SemaphoreType.DMA((slots,)),
            pltpu.SemaphoreType.DMA((slots,)),
        ],
        input_output_aliases={2 + len(weights): 0},
        compiler_params=pltpu.CompilerParams(vmem_limit_bytes=16 * MIB),
        name="coarse",
    )(index, table, *weights, fine)


def find_pieces(counts, me, slots):
    starts = jnp.cumsum(counts) - counts
    devices = jnp.arange(counts.shape[0], dtype=jnp.int32)
    start = jnp.sum(jnp.where(devices < me, counts, 0))
    count = jnp.sum(jnp.where(devices == me, counts, 0))
    base = start // 8 * 8
    blocks = base + jnp.arange(16, dtype=jnp.int32)
    inside = (starts[None, :] <= blocks[:, None]) & (blocks[:, None] < (starts + counts)[None, :])
    rows = jnp.sum(
        jnp.where(inside, devices[None, :] * slots + blocks[:, None] - starts[None, :], 0), axis=1
    )
    slot_ids = jnp.arange(slots, dtype=jnp.int32)
    return jnp.concatenate([rows, start - base + slot_ids, (slot_ids < count).astype(jnp.int32)])


def gather_counts(owner_counts):
    sent = lax.optimization_barrier(jnp.broadcast_to(owner_counts[0], (8, 128)))
    every = lax.all_gather(sent, AXES, axis=0, tiled=True)
    return every.reshape(-1, 8, 128)[:, 0, 0]


def per_device(density, owner_counts):
    slots = density.shape[0]
    counts = gather_counts(owner_counts)
    index = find_pieces(counts, lax.axis_index(AXES), slots)
    lowpass = lowpass_call(density)
    table = lax.all_gather(lowpass, AXES, axis=0, tiled=True)
    fine = fine_call(owner_counts, density)
    return coarse_call(index, table, fine)


def solution(mesh):
    in_specs = (P(AXES, None, None), P(AXES))
    out_specs = P(AXES, None, None)
    return jax.shard_map(per_device, mesh=mesh, in_specs=in_specs, out_specs=out_specs, check_vma=False)
```

```python
import functools

import jax
import jax.numpy as jnp
import numpy as np
from jax import lax
from jax.experimental import pallas as pl
from jax.experimental.pallas import tpu as pltpu
from jax.sharding import PartitionSpec as P

ALPHA = -1.586134342059924
BETA = -0.052980118572961
GAMMA = 0.882911075530934
DELTA = 0.443506852043971
SCALE = 1.230174104914001
SQUARE = SCALE * SCALE
F32 = jnp.float32
BF16 = jnp.bfloat16
AXES = ("node", "dev")
MIB = 1 << 20
VMEM_LIMIT = 56 * MIB


def pass_matrix(n):
    low, high = np.eye(n)[0::2], np.eye(n)[1::2]

    def after(v):
        return np.concatenate([v[1:], v[-1:]], 0)

    def before(v):
        return np.concatenate([v[:1], v[:-1]], 0)

    high = high + ALPHA * (low + after(low))
    low = low + BETA * (before(high) + high)
    high = high + GAMMA * (low + after(low))
    low = low + DELTA * (before(high) + high)
    return np.concatenate([low / SCALE, high * SCALE], 0)


def two_terms(matrix):
    matrix = np.asarray(matrix, np.float32)
    first = matrix.astype(BF16)
    return first, (matrix - first.astype(np.float32)).astype(BF16)


def left_terms(matrix):
    first, second = two_terms(matrix)
    return np.concatenate([first, second, first], 1)


def split(value):
    first = value.astype(BF16)
    return first, (value - first.astype(F32)).astype(BF16)


def dot(left, right):
    return jnp.dot(left, right, preferred_element_type=F32)


def times(value, first, second):
    high, low = split(value)
    return dot(high, first) + dot(low, first) + dot(high, second)


def times_left(terms, value):
    high, low = split(value)
    return dot(terms, jnp.concatenate([high, high, low], 0))


def lowpass_kernel(count_ref, x_ref, wh_ref, wl_ref, ax_ref, out_ref, acc_ref):
    step = pl.program_id(0)
    slots, edge, width = x_ref.shape
    part = times(x_ref[...].reshape(slots * edge, width), wh_ref[...], wl_ref[...])

    @pl.when(step == 0)
    def _():
        acc_ref[...] = part

    @pl.when(step > 0)
    def _():
        acc_ref[...] += part

    @pl.when(step == pl.num_programs(0) - 1)
    def _():
        out_ref[...] = jnp.full(out_ref.shape, count_ref[0].astype(F32))
        for slot in range(slots):
            made = times_left(ax_ref[...], acc_ref[pl.ds(slot * edge, edge), :])
            for h in range(2):
                out_ref[pl.ds(8 * h + slot, edge // 4, stride=16), :] = made[:, h * 128 : h * 128 + 128]


def lowpass_call(owner_counts, density):
    slots, edge, plane = density.shape
    quarter = edge // 4
    two_levels = pass_matrix(edge // 2)[:quarter] @ pass_matrix(edge)[: edge // 2]
    first, second = two_terms(np.kron(two_levels.T, two_levels.T))
    terms = left_terms(two_levels)
    steps = 8
    width = plane // steps
    cols = quarter * quarter
    pieces = pl.pallas_call(
        lowpass_kernel,
        grid=(steps,),
        in_specs=[
            pl.BlockSpec(memory_space=pltpu.SMEM),
            pl.BlockSpec((slots, edge, width), lambda j: (0, 0, j)),
            pl.BlockSpec((width, cols), lambda j: (j, 0)),
            pl.BlockSpec((width, cols), lambda j: (j, 0)),
            pl.BlockSpec(terms.shape, lambda j: (0, 0)),
        ],
        out_specs=pl.BlockSpec((16 * quarter, 128), lambda j: (0, 0)),
        out_shape=jax.ShapeDtypeStruct((16 * quarter, 128), F32),
        scratch_shapes=[pltpu.VMEM((slots * edge, cols), F32)],
        compiler_params=pltpu.CompilerParams(vmem_limit_bytes=VMEM_LIMIT),
        cost_estimate=pl.CostEstimate(
            flops=6 * slots * edge * plane * cols, bytes_accessed=10 * MIB, transcendentals=0
        ),
        name="lowpass",
    )(owner_counts, density, first, second, terms)
    return pieces.reshape(2 * quarter, 8, 128)


def route_kernel(me_ref, got_ref, send_ref, index_ref, order_ref, count_ref, sem):
    devices = got_ref.shape[0]
    copy = pltpu.make_async_copy(got_ref.at[:, 7, :], count_ref, sem)
    copy.start()
    order_ref[...] = jnp.zeros_like(order_ref)
    copy.wait()
    start, my_start, my_count = 0, 0, 0
    starts = []
    for d in range(devices):
        count = count_ref[d, 0].astype(jnp.int32)
        starts.append(start)
        my_start = jnp.where(me_ref[0] == d, start, my_start)
        my_count = jnp.where(me_ref[0] == d, count, my_count)
        order_ref[pl.ds(start, 8), :] = got_ref[d]
        start = start + count
    for d in range(devices):
        at = pl.multiple_of(starts[d] // 8 * 8, 8) if d else 0
        send_ref[d] = order_ref[pl.ds(at, 16), :]
    index_ref[0] = my_start % 8
    index_ref[1] = my_count


def route_call(me, got, slots):
    devices = got.shape[0]
    return pl.pallas_call(
        route_kernel,
        in_specs=[
            pl.BlockSpec(memory_space=pltpu.SMEM),
            pl.BlockSpec(memory_space=pltpu.VMEM),
        ],
        out_specs=[pl.BlockSpec(memory_space=pltpu.VMEM), pl.BlockSpec(memory_space=pltpu.SMEM)],
        out_shape=[
            jax.ShapeDtypeStruct((devices, 16, 128), F32),
            jax.ShapeDtypeStruct((2,), jnp.int32),
        ],
        scratch_shapes=[
            pltpu.VMEM((devices * slots + 16, 128), F32),
            pltpu.SMEM((devices, 128), F32),
            pltpu.SemaphoreType.DMA,
        ],
        compiler_params=pltpu.CompilerParams(vmem_limit_bytes=VMEM_LIMIT),
        name="route",
    )(me, got)


def lift(low, high, n, halo, scaled):
    up = SQUARE if scaled else 1.0
    at = 2 if halo else 0
    first, second, third, fourth = ({} for _ in range(4))

    def get(values, i, is_low):
        if halo:
            return values[i]
        return values[min(i, n - 1)] if is_low else values[max(i, 0)]

    lows = {i - at: low[i] for i in range(len(low))}
    highs = {i - at: high[i] for i in range(len(high))}

    def make_first(i):
        first[i] = highs[i] + (ALPHA * up) * (lows[i] + get(lows, i + 1, True))

    def make_second(i):
        second[i] = lows[i] + (BETA / up) * (get(first, i - 1, False) + first[i])

    def make_third(i):
        third[i] = first[i] + (GAMMA * up) * (second[i] + get(second, i + 1, True))

    def make_fourth(i):
        fourth[i] = second[i] + (DELTA / up) * (get(third, i - 1, False) + third[i])

    if halo:
        for i in range(-2, n + 1):
            make_first(i)
            if i >= -1:
                make_second(i)
            if i >= 0:
                make_third(i - 1)
            if i >= 1:
                make_fourth(i - 1)
    else:
        for i in range(n):
            make_first(i)
            make_second(i)
            if i >= 1:
                make_third(i - 1)
                make_fourth(i - 1)
        make_third(n - 1)
        make_fourth(n - 1)
    return [fourth[i] for i in range(n)], [third[i] for i in range(n)]


def fine_kernel(
    count_ref, x_ref, w1_ref, w2_ref, out_ref, l_ref, y_ref, z_ref, c_ref, d_ref, e_ref
):
    slot = pl.program_id(0)
    edge = x_ref.shape[1]
    pairs = x_ref.shape[2] // 256
    half = edge // 2
    lane = lax.broadcasted_iota(jnp.int32, (8, 128), 1)
    front = lane < 64
    inner = (lane & 63) < half

    def turn(value):
        return pltpu.roll(value, 64, 1)

    def with_halo(low, high):
        def left(values, i):
            return jnp.where(front, values[i[0]], turn(values[i[1]]))

        def right(values, i):
            return jnp.where(front, turn(values[i[0]]), values[i[1]])

        low_all = [left(low, (2, -2)), left(low, (1, -1))] + low + [right(low, (0, -1)), right(low, (1, -2))]
        high_all = [left(high, (1, -2)), left(high, (0, -1))] + high + [right(high, (0, -2))]
        return low_all, high_all

    @pl.when(slot >= count_ref[0])
    def _():
        out_ref[...] = jnp.zeros_like(out_ref)

    @pl.when(slot < count_ref[0])
    def _():
        for j in range(pairs):
            for q in range(2):
                high, low = split(x_ref[0, :, pl.ds((j + q * pairs) * 128, 128)])
                rows = pl.ds(j * edge, edge)
                l_ref[rows, pl.ds(q * 128, 128)] = high
                l_ref[rows, pl.ds(256 + q * 128, 128)] = low
                l_ref[rows, pl.ds(512 + q * 128, 128)] = high
        lifted = dot(l_ref[...], w1_ref[...])
        y_ref[pl.ds(0, pairs * edge), :] = lifted[:, :128]
        y_ref[pl.ds(pairs * edge, pairs * edge), :] = lifted[:, 128:]

        for r in range(edge // 8):
            low = [y_ref[pl.ds(j * edge + r * 8, 8), :] for j in range(pairs)]
            high = [y_ref[pl.ds((pairs + j) * edge + r * 8, 8), :] for j in range(pairs)]
            low, high = lift(*with_halo(low, high), pairs, True, True)
            for j in range(pairs):
                y_ref[pl.ds(j * edge + r * 8, 8), :] = low[j]
                y_ref[pl.ds((pairs + j) * edge + r * 8, 8), :] = high[j]

        for part in range(2):
            made = []
            for u in range(2):
                at = (part * pairs + u) * edge
                rows = [y_ref[pl.ds(at + x, 8, stride=2 * edge), :] for x in range(edge)]
                low, high = lift(rows[0::2], rows[1::2], half, False, False)
                low = [v * (1.0 / SCALE) for v in low]
                high = [v * SCALE for v in high]
                if part == 0:
                    for x in range(half):
                        c_ref[pl.ds(8 * x, 8), pl.ds(u * 128, 128)] = low[x]
                made.append(low + high)
            for x in range(edge):
                a, b = made[0][x], made[1][x]
                at = part * pairs * edge + x
                z_ref[pl.ds(at, 8, stride=edge), :] = jnp.where(front, a, turn(b))
                z_ref[pl.ds(at + pairs // 2 * edge, 8, stride=edge), :] = jnp.where(front, turn(a), b)

        high, low = split(c_ref[...])
        lifted = dot(jnp.concatenate([high, low, high], 1), w2_ref[...])
        d_ref[pl.ds(0, 8 * half), :] = lifted[:, :128]
        d_ref[pl.ds(8 * half, 8 * half), :] = lifted[:, 128:]

        for r in range(half // 8):
            low = [d_ref[pl.ds(64 * r + i, 8, stride=8), :] for i in range(8)]
            high = [d_ref[pl.ds(8 * half + 64 * r + i, 8, stride=8), :] for i in range(8)]
            low, high = lift(*with_halo(low, high), 8, True, True)
            for i in range(8):
                d_ref[pl.ds(64 * r + i, 8, stride=8), :] = low[i]
                d_ref[pl.ds(8 * half + 64 * r + i, 8, stride=8), :] = high[i]

        for u in range(2):
            rows = [d_ref[pl.ds(8 * (u * half + x), 8), :] for x in range(half)]
            low, high = lift(rows[0::2], rows[1::2], half // 2, False, False)
            for x in range(half // 2):
                e_ref[pl.ds(u * 8 * half + x, 8, stride=half), :] = low[x] * (1.0 / SCALE)
                e_ref[pl.ds(u * 8 * half + half // 2 + x, 8, stride=half), :] = high[x] * SCALE

        for u in range(2):
            for t in range(4):
                for r in range(half // 8):
                    a = e_ref[pl.ds((u * 8 + 2 * t) * half + 8 * r, 8), :]
                    b = e_ref[pl.ds((u * 8 + 2 * t + 1) * half + 8 * r, 8), :]
                    for tile, value in (
                        (u * 8 + t, jnp.where(front, a, turn(b))),
                        (u * 8 + 4 + t, jnp.where(front, turn(a), b)),
                    ):
                        old = z_ref[pl.ds(tile * edge + 8 * r, 8), :]
                        out_ref[0, pl.ds(8 * r, 8), pl.ds(tile * 128, 128)] = jnp.where(inner, value, old)
        for t in range(2 * pairs):
            first = half if t < pairs else 0
            out_ref[0, pl.ds(first, edge - first), pl.ds(t * 128, 128)] = z_ref[
                pl.ds(t * edge + first, edge - first), :
            ]


def fine_call(owner_counts, density):
    slots, edge, plane = density.shape
    half = edge // 2
    pairs = plane // 256
    one = pass_matrix(edge).T
    zero = np.zeros_like(one)
    w1 = np.block(
        [
            [one / SCALE, zero, zero, zero],
            [zero, zero, one * SCALE, zero],
            [zero, one / SCALE, zero, zero],
            [zero, zero, zero, one * SCALE],
        ]
    )
    two = np.zeros_like(one)
    two[:half, :half] = pass_matrix(half).T
    w2 = np.kron(np.diag([1 / SCALE, 1 / SCALE, SCALE, SCALE]), two)
    def stacked(matrix):
        first, second = two_terms(matrix)
        return np.concatenate([first, first, second], 0)

    fixed = pl.BlockSpec((768, 256), lambda s: (0, 0))
    return pl.pallas_call(
        fine_kernel,
        grid=(slots,),
        in_specs=[
            pl.BlockSpec(memory_space=pltpu.SMEM),
            pl.BlockSpec((1, edge, plane), lambda s: (s, 0, 0)),
            fixed,
            fixed,
        ],
        out_specs=pl.BlockSpec((1, edge, plane), lambda s: (s, 0, 0)),
        out_shape=jax.ShapeDtypeStruct(density.shape, F32),
        scratch_shapes=[
            pltpu.VMEM((pairs * edge, 768), BF16),
            pltpu.VMEM((2 * pairs * edge, 128), F32),
            pltpu.VMEM((2 * pairs * edge, 128), F32),
            pltpu.VMEM((8 * half, 256), F32),
            pltpu.VMEM((16 * half, 128), F32),
            pltpu.VMEM((16 * half, 128), F32),
        ],
        compiler_params=pltpu.CompilerParams(vmem_limit_bytes=VMEM_LIMIT),
        cost_estimate=pl.CostEstimate(
            flops=6 * slots * edge * plane * 256, bytes_accessed=12 * MIB, transcendentals=0
        ),
        name="fine",
    )(owner_counts, density, stacked(w1), stacked(w2))


def coarse_kernel(
    index_ref,
    piece_ref,
    wx_ref,
    wzh_ref,
    wzl_ref,
    wyh_ref,
    wyl_ref,
    w23h_ref,
    w23l_ref,
    wx2_ref,
    wx3_ref,
    fine_ref,
    out_ref,
    block_ref,
    corner_ref,
    corner_sem,
    out_sem,
):
    slots = corner_ref.shape[0]
    lane = lax.broadcasted_iota(jnp.int32, (16, 128), 1)

    def window(s):
        return out_ref.at[s, pl.ds(0, 16), pl.ds(0, 1024)]

    def piece(i):
        return jnp.concatenate([piece_ref[pl.ds(16 * h + i, 16, stride=32), :] for h in range(2)], 1)

    for s in range(slots):
        pltpu.make_async_copy(window(s), corner_ref.at[s], corner_sem.at[s]).start()

    first = [
        [
            times_left(wx_ref[...], jnp.concatenate([piece(o * 8 + 2 * q), piece(o * 8 + 2 * q + 1)], 0))
            for q in range(4)
        ]
        for o in range(2)
    ]
    stacked = []
    for o in range(2):
        for cy in range(2):
            for yh in range(2):
                part = slice(yh * 128, yh * 128 + 128)
                stacked.append(jnp.concatenate([first[o][cy][:, part], first[o][2 + cy][:, part]], 1))
    lifted = times(jnp.concatenate(stacked, 0), wzh_ref[...], wzl_ref[...])
    stacked = []
    for o in range(2):
        for tz in range(2):
            stacked.append(
                jnp.concatenate(
                    [lifted[(o * 4 + u) * 32 : (o * 4 + u + 1) * 32, tz * 128 : tz * 128 + 128] for u in range(4)],
                    1,
                )
            )
    lifted = times(jnp.concatenate(stacked, 0), wyh_ref[...], wyl_ref[...])
    corner = []
    for o in range(2):
        for tz in range(2):
            for ty in range(2):
                for tx in range(2):
                    at = (o * 2 + tz) * 32 + tx * 16
                    value = lifted[at : at + 16, ty * 256 : ty * 256 + 256]
                    if tx + ty + tz == 0:
                        corner.append(value)
                    else:
                        block_ref[o * 8 + tx + 2 * ty + 4 * tz] = value
    both = times(jnp.concatenate(corner, 0), w23h_ref[...], w23l_ref[...])
    spot = lax.broadcasted_iota(jnp.int32, (16, 256), 1)
    depth = lax.broadcasted_iota(jnp.int32, (16, 256), 0)
    small = (depth < 8) & (spot < 128) & ((spot & 15) < 8)
    for o in range(2):
        mine = both[o * 16 : o * 16 + 16]
        second = times_left(wx2_ref[...], mine[:, :256])
        third = times_left(wx3_ref[...], mine[:, 256:])
        block_ref[o * 8] = jnp.where(small, third, second)

    for s in range(slots):
        pltpu.make_async_copy(window(s), corner_ref.at[s], corner_sem.at[s]).wait()
    for s in range(slots):

        @pl.when(s < index_ref[1])
        def _():
            value = block_ref[index_ref[0] + s]
            for t in range(8):
                tile = value[:, (t // 4) * 128 : (t // 4) * 128 + 128]
                near = pltpu.roll(tile, (128 - 32 * (t % 4)) % 128, 1)
                far = pltpu.roll(tile, (64 - 16 - 32 * (t % 4)) % 128, 1)
                old = corner_ref[s, :, pl.ds(t * 128, 128)]
                new = jnp.where(lane < 16, near, jnp.where((lane >= 64) & (lane < 80), far, old))
                corner_ref[s, :, pl.ds(t * 128, 128)] = new
            pltpu.make_async_copy(corner_ref.at[s], window(s), out_sem.at[s]).start()

    for s in range(slots):

        @pl.when(s < index_ref[1])
        def _():
            pltpu.make_async_copy(corner_ref.at[s], window(s), out_sem.at[s]).wait()


def coarse_call(index, pieces, fine):
    slots, edge, plane = fine.shape
    m32, m16, m8 = pass_matrix(32), pass_matrix(16), pass_matrix(8)
    deep = np.zeros((16, 16))
    deep[:8] = m8 @ m16[:8]
    eye8, eye16 = np.eye(8), np.eye(16)
    wz = np.zeros((256, 256))
    for cz in range(2):
        for tz in range(2):
            wz[cz * 128 : cz * 128 + 128, tz * 128 : tz * 128 + 128] = np.kron(
                eye8, m32[tz * 16 : tz * 16 + 16, cz * 16 : cz * 16 + 16].T
            )
    w23 = np.concatenate([np.kron(m16.T, m16.T), np.kron(deep.T, deep.T)], 1)
    weights = [
        left_terms(m32),
        *two_terms(wz),
        *two_terms(np.kron(m32.T, eye16)),
        *two_terms(w23),
        left_terms(m16),
        left_terms(deep),
    ]
    anywhere = pl.BlockSpec(memory_space=pl.ANY)
    vmem = pl.BlockSpec(memory_space=pltpu.VMEM)
    return pl.pallas_call(
        coarse_kernel,
        in_specs=[pl.BlockSpec(memory_space=pltpu.SMEM), vmem] + [vmem] * len(weights) + [anywhere],
        out_specs=anywhere,
        out_shape=jax.ShapeDtypeStruct(fine.shape, F32),
        scratch_shapes=[
            pltpu.VMEM((16, 16, 256), F32),
            pltpu.VMEM((slots, 16, 1024), F32),
            pltpu.SemaphoreType.DMA((slots,)),
            pltpu.SemaphoreType.DMA((slots,)),
        ],
        input_output_aliases={2 + len(weights): 0},
        compiler_params=pltpu.CompilerParams(vmem_limit_bytes=VMEM_LIMIT),
        name="coarse",
    )(index, pieces.reshape(-1, 128), *weights, fine)


def exchange(lowpass, slots):
    me = lax.axis_index(AXES)
    devices = lax.axis_size(AXES)
    if devices == lowpass.shape[0]:
        got = lax.all_to_all(lowpass, AXES, 0, 0, tiled=True)
        sent, index = route_call(me.reshape(1), got, slots)
        return lax.all_to_all(sent, AXES, 0, 0, tiled=True), index
    every = lax.all_gather(lowpass, AXES, axis=0)
    counts = every[:, 0, 7, 0].astype(jnp.int32)
    starts = jnp.cumsum(counts) - counts
    blocks = starts[me] // 8 * 8 + jnp.arange(16, dtype=jnp.int32)
    owners = jnp.sum((starts[None, :] <= blocks[:, None]).astype(jnp.int32), axis=1) - 1
    place = jnp.minimum(blocks - starts[owners], slots - 1)
    pieces = jnp.transpose(every[owners, :, place], (1, 0, 2))
    return pieces, jnp.stack([starts[me] % 8, counts[me]])


def per_device(density, owner_counts):
    lowpass = lowpass_call(owner_counts, density)
    pieces, index = exchange(lowpass, density.shape[0])
    fine = fine_call(owner_counts, density)
    return coarse_call(index, pieces, fine)


def solution(mesh):
    in_specs = (P(AXES, None, None), P(AXES))
    out_specs = P(AXES, None, None)
    return jax.shard_map(per_device, mesh=mesh, in_specs=in_specs, out_specs=out_specs, check_vma=False)
```

```python
import functools

import jax
import jax.numpy as jnp
import numpy as np
from jax import lax
from jax.experimental import pallas as pl
from jax.experimental.pallas import tpu as pltpu
from jax.sharding import PartitionSpec as P

ALPHA = -1.586134342059924
BETA = -0.052980118572961
GAMMA = 0.882911075530934
DELTA = 0.443506852043971
SCALE = 1.230174104914001
SQUARE = SCALE * SCALE
F32 = jnp.float32
BF16 = jnp.bfloat16
AXES = ("node", "dev")
MIB = 1 << 20
VMEM_LIMIT = 56 * MIB


def pass_matrix(n):
    low, high = np.eye(n)[0::2], np.eye(n)[1::2]

    def after(v):
        return np.concatenate([v[1:], v[-1:]], 0)

    def before(v):
        return np.concatenate([v[:1], v[:-1]], 0)

    high = high + ALPHA * (low + after(low))
    low = low + BETA * (before(high) + high)
    high = high + GAMMA * (low + after(low))
    low = low + DELTA * (before(high) + high)
    return np.concatenate([low / SCALE, high * SCALE], 0)


def two_terms(matrix):
    matrix = np.asarray(matrix, np.float32)
    first = matrix.astype(BF16)
    return first, (matrix - first.astype(np.float32)).astype(BF16)


def left_terms(matrix):
    first, second = two_terms(matrix)
    return np.concatenate([first, second, first], 1)


def split(value):
    first = value.astype(BF16)
    return first, (value - first.astype(F32)).astype(BF16)


def dot(left, right):
    return jnp.dot(left, right, preferred_element_type=F32)


def times(value, first, second):
    high, low = split(value)
    return dot(high, first) + dot(low, first) + dot(high, second)


def times_left(terms, value):
    high, low = split(value)
    return dot(terms, jnp.concatenate([high, high, low], 0))


def start_tiles(src_ref, dst_ref, sem, tiles):
    for t in tiles:
        pltpu.make_async_copy(src_ref.at[..., pl.ds(t * 128, 128)], dst_ref.at[..., t, :], sem).start()


def split_rows(rows):
    return [split(jnp.concatenate(rows[m : m + 2], 0)) for m in range(0, len(rows), 2)]


def lowpass_kernel(
    count_ref, x_ref, wz_any, wyh_any, wyl_any, out_ref, x_buf, wz_ref, wyh_ref, wyl_ref, l_ref, z_ref, sems, w_sems
):
    slots, edge = x_ref.shape[:2]
    quarter = edge // 4
    order = (0, 2, 1, 3)
    for g in order:
        start_tiles(x_ref, x_buf, sems.at[g], range(8 * g, 8 * g + 8))
    weights = [
        pltpu.make_async_copy(src, dst, w_sems.at[i])
        for i, (src, dst) in enumerate(((wz_any, wz_ref), (wyh_any, wyh_ref), (wyl_any, wyl_ref)))
    ]
    for copy in weights:
        copy.start()
    for g in order:
        part = x_buf.at[:, :, pl.ds(8 * g, 8), :]
        pltpu.make_async_copy(part, part, sems.at[g]).wait()
        at = (g % 2) * 256 + (g // 2) * 128

        @pl.loop(0, slots)
        def _(s):
            rows = [x_buf[s, x, pl.ds(8 * g, 8), :] for x in range(edge)]
            rows, _ = lift(rows[0::2], rows[1::2], edge // 2, False, False)
            rows, _ = lift(rows[0::2], rows[1::2], quarter, False, False)
            for m, (high, low) in enumerate(split_rows(rows)):
                place = pl.ds(pl.multiple_of(s * 8 * quarter + 16 * m, 16), 16)
                l_ref[place, pl.ds(at, 128)] = high
                l_ref[place, pl.ds(512 + at, 128)] = low
                l_ref[place, pl.ds(1024 + at, 128)] = high

    for copy in weights:
        copy.wait()
    z_ref[...] = dot(l_ref[...], wz_ref[...])
    wide = jnp.concatenate([z_ref[pl.ds(i, slots * quarter, stride=8), :] for i in range(8)], 1)
    made = times(wide, wyh_ref[...], wyl_ref[...])
    out_ref[...] = jnp.full(out_ref.shape, count_ref[0].astype(F32))
    for slot in range(slots):
        for h in range(2):
            out_ref[pl.ds(8 * h + slot, quarter, stride=16), :] = made[
                slot * quarter : (slot + 1) * quarter, h * 128 : h * 128 + 128
            ]


def stacked(matrix):
    first, second = two_terms(matrix)
    return np.concatenate([first, first, second], 0)


def lowpass_call(owner_counts, density):
    slots, edge, plane = density.shape
    quarter = edge // 4
    two_levels = pass_matrix(edge // 2)[:quarter] @ pass_matrix(edge)[: edge // 2]
    wz = stacked(np.kron(np.eye(8), two_levels.T))
    i, gp, q, p = np.meshgrid(np.arange(8), np.arange(2), np.arange(2), np.arange(2), indexing="ij")
    entry = (2 * (8 * gp + i) + p + 32 * q).reshape(-1)
    wy = np.kron(two_levels.T[entry] / SQUARE, np.eye(quarter))
    wyh, wyl = two_terms(wy)
    anywhere = pl.BlockSpec(memory_space=pl.ANY)
    pieces = pl.pallas_call(
        lowpass_kernel,
        in_specs=[pl.BlockSpec(memory_space=pltpu.SMEM)] + [anywhere] * 4,
        out_specs=pl.BlockSpec(memory_space=pltpu.VMEM),
        out_shape=jax.ShapeDtypeStruct((16 * quarter, 128), F32),
        scratch_shapes=[
            pltpu.VMEM((slots, edge, plane // 128, 128), F32),
            pltpu.VMEM(wz.shape, BF16),
            pltpu.VMEM(wyh.shape, BF16),
            pltpu.VMEM(wyl.shape, BF16),
            pltpu.VMEM((slots * 8 * quarter, 1536), BF16),
            pltpu.VMEM((slots * 8 * quarter, 128), F32),
            pltpu.SemaphoreType.DMA((4,)),
            pltpu.SemaphoreType.DMA((3,)),
        ],
        compiler_params=pltpu.CompilerParams(vmem_limit_bytes=VMEM_LIMIT),
        name="lowpass",
    )(owner_counts, density, wz, wyh, wyl)
    return pieces.reshape(2 * quarter, 8, 128)


def route_kernel(me_ref, got_ref, _, send_ref, index_ref, order_ref, count_ref, sem):
    devices = got_ref.shape[0]
    copy = pltpu.make_async_copy(got_ref.at[:, 7, :], count_ref, sem)
    copy.start()
    order_ref[...] = jnp.zeros_like(order_ref)
    copy.wait()
    start, my_start, my_count = 0, 0, 0
    starts = []
    for d in range(devices):
        count = count_ref[d, 0].astype(jnp.int32)
        starts.append(start)
        my_start = jnp.where(me_ref[0] == d, start, my_start)
        my_count = jnp.where(me_ref[0] == d, count, my_count)
        order_ref[pl.ds(start, 8), :] = got_ref[d]
        start = start + count
    for d in range(devices):
        at = pl.multiple_of(starts[d] // 8 * 8, 8) if d else 0
        send_ref[d] = order_ref[pl.ds(at, 16), :]
    index_ref[0] = my_start % 8
    index_ref[1] = my_count


def route_call(me, got, meanwhile, slots):
    devices = got.shape[0]
    return pl.pallas_call(
        route_kernel,
        in_specs=[
            pl.BlockSpec(memory_space=pltpu.SMEM),
            pl.BlockSpec(memory_space=pltpu.VMEM),
            pl.BlockSpec(memory_space=pl.ANY),
        ],
        out_specs=[pl.BlockSpec(memory_space=pltpu.VMEM), pl.BlockSpec(memory_space=pltpu.SMEM)],
        out_shape=[
            jax.ShapeDtypeStruct((devices, 16, 128), F32),
            jax.ShapeDtypeStruct((2,), jnp.int32),
        ],
        scratch_shapes=[
            pltpu.VMEM((devices * slots + 16, 128), F32),
            pltpu.SMEM((devices, 128), F32),
            pltpu.SemaphoreType.DMA,
        ],
        compiler_params=pltpu.CompilerParams(vmem_limit_bytes=VMEM_LIMIT),
        name="route",
    )(me, got, meanwhile)


def lift(low, high, n, halo, scaled):
    up = SQUARE if scaled else 1.0
    at = 2 if halo else 0
    first, second, third, fourth = ({} for _ in range(4))

    def get(values, i, is_low):
        if halo:
            return values[i]
        return values[min(i, n - 1)] if is_low else values[max(i, 0)]

    lows = {i - at: low[i] for i in range(len(low))}
    highs = {i - at: high[i] for i in range(len(high))}

    def make_first(i):
        first[i] = highs[i] + (ALPHA * up) * (lows[i] + get(lows, i + 1, True))

    def make_second(i):
        second[i] = lows[i] + (BETA / up) * (get(first, i - 1, False) + first[i])

    def make_third(i):
        third[i] = first[i] + (GAMMA * up) * (second[i] + get(second, i + 1, True))

    def make_fourth(i):
        fourth[i] = second[i] + (DELTA / up) * (get(third, i - 1, False) + third[i])

    if halo:
        for i in range(-2, n + 1):
            make_first(i)
            if i >= -1:
                make_second(i)
            if i >= 0:
                make_third(i - 1)
            if i >= 1:
                make_fourth(i - 1)
    else:
        for i in range(n):
            make_first(i)
            make_second(i)
            if i >= 1:
                make_third(i - 1)
                make_fourth(i - 1)
        make_third(n - 1)
        make_fourth(n - 1)
    return [fourth[i] for i in range(n)], [third[i] for i in range(n)]


def fine_kernel(count_ref, x_ref, w1_ref, w2_ref, *refs, offset):
    out_ref, x_buf, l_ref, y_ref, c_ref, m_ref, d_ref, sems = refs[-8:]
    step = pl.program_id(0)
    slot = step + offset
    edge = x_ref.shape[1]
    tiles = x_ref.shape[2] // 128
    pairs = tiles // 2
    half = edge // 2
    lane = lax.broadcasted_iota(jnp.int32, (8, 128), 1)
    front = lane < 64
    inner = (lane & 63) < half

    def turn(value):
        return pltpu.roll(value, 64, 1)

    def with_halo(low, high):
        def left(values, i):
            return jnp.where(front, values[i[0]], turn(values[i[1]]))

        def right(values, i):
            return jnp.where(front, turn(values[i[0]]), values[i[1]])

        low_all = [left(low, (2, -2)), left(low, (1, -1))] + low + [right(low, (0, -1)), right(low, (1, -2))]
        high_all = [left(high, (1, -2)), left(high, (0, -1))] + high + [right(high, (0, -2))]
        return low_all, high_all

    def fetch(which, place):
        start_tiles(x_ref.at[which], x_buf.at[place], sems.at[place], range(tiles))

    def scaled_rows(rows):
        low, high = lift(rows[0::2], rows[1::2], len(rows) // 2, False, False)
        return [v * (1.0 / SCALE) for v in low] + [v * SCALE for v in high]

    def store_terms(ref, row, col, rows):
        for m, (high, low) in enumerate(split_rows(rows)):
            place = pl.ds(row + 16 * m, 16)
            ref[place, pl.ds(col, 128)] = high
            ref[place, pl.ds(256 + col, 128)] = low
            ref[place, pl.ds(512 + col, 128)] = high

    @pl.when((step == 0) & (slot < count_ref[0]))
    def _():
        fetch(slot, 0)

    @pl.when((step + 1 < pl.num_programs(0)) & (slot + 1 < count_ref[0]))
    def _():
        fetch(slot + 1, (step + 1) % 2)

    @pl.when(slot >= count_ref[0])
    def _():
        out_ref[...] = jnp.zeros_like(out_ref)

    @pl.when(slot < count_ref[0])
    def _():
        x = x_buf.at[step % 2]
        pltpu.make_async_copy(x, x, sems.at[step % 2]).wait()
        for g in range(4):
            rows = scaled_rows([x[i, pl.ds(8 * g, 8), :] for i in range(edge)])
            store_terms(l_ref, (g % 2) * 8 * edge, (g // 2) * 128, rows)
        lifted = dot(l_ref[...], w1_ref[...])
        y_ref[pl.ds(0, pairs * edge), :] = lifted[:, :128]
        y_ref[pl.ds(pairs * edge, pairs * edge), :] = lifted[:, 128:]
        for r in range(edge // 8):
            rows = pl.ds(8 * r, 8)

            def tile(part, j):
                at = (part * 2 + j // 8) * 8 * edge + 64 * r + j % 8
                return y_ref[pl.ds(at, 8, stride=8), :]

            low = [tile(0, j) for j in range(pairs)]
            high = [tile(1, j) for j in range(pairs)]
            low, high = lift(*with_halo(low, high), pairs, True, True)
            for part, values in enumerate((low, high)):
                for t in range(pairs // 2):
                    a, b = values[2 * t], values[2 * t + 1]
                    at = part * pairs + t
                    out_ref[0, rows, pl.ds(at * 128, 128)] = jnp.where(front, a, turn(b))
                    out_ref[0, rows, pl.ds((at + pairs // 2) * 128, 128)] = jnp.where(front, turn(a), b)
            if r < half // 8:
                low, high = lift(*with_halo(low[0::2], low[1::2]), 8, True, False)
                for i in range(8):
                    c_ref[pl.ds(i * half + 8 * r, 8), :] = low[i]
                    c_ref[pl.ds((8 + i) * half + 8 * r, 8), :] = high[i]
        for u in range(2):
            rows = scaled_rows([c_ref[pl.ds(u * 8 * half + i, 8, stride=half), :] for i in range(half)])
            store_terms(m_ref, 0, u * 128, rows)
        lifted = dot(m_ref[...], w2_ref[...])
        d_ref[pl.ds(0, 8 * half), :] = lifted[:, :128]
        d_ref[pl.ds(8 * half, 8 * half), :] = lifted[:, 128:]
        for u in range(2):
            for t in range(4):
                for r in range(half // 8):
                    a = d_ref[pl.ds(u * 8 * half + 64 * r + 2 * t, 8, stride=8), :]
                    b = d_ref[pl.ds(u * 8 * half + 64 * r + 2 * t + 1, 8, stride=8), :]
                    for at, value in (
                        (u * 8 + t, jnp.where(front, a, turn(b))),
                        (u * 8 + 4 + t, jnp.where(front, turn(a), b)),
                    ):
                        rows, cols = pl.ds(8 * r, 8), pl.ds(at * 128, 128)
                        out_ref[0, rows, cols] = jnp.where(inner, value, out_ref[0, rows, cols])


def fine_call(owner_counts, density, first, last, before=None, after=None):
    slots, edge, plane = density.shape
    half = edge // 2
    pairs = plane // 256
    one = pass_matrix(edge).T
    zero = np.zeros_like(one)
    w1 = np.block(
        [
            [one / SCALE, zero, zero, zero],
            [zero, zero, one * SCALE, zero],
            [zero, one / SCALE, zero, zero],
            [zero, zero, zero, one * SCALE],
        ]
    )
    two = np.zeros_like(one)
    two[:half, :half] = pass_matrix(half).T
    w2 = np.kron(np.diag([1 / SCALE, 1 / SCALE, SCALE, SCALE]), two)
    anywhere = pl.BlockSpec(memory_space=pl.ANY)
    fixed = pl.BlockSpec((768, 256), lambda s: (0, 0))
    old = [after] if before is None else [before]
    return pl.pallas_call(
        functools.partial(fine_kernel, offset=first),
        grid=(last - first,),
        in_specs=[pl.BlockSpec(memory_space=pltpu.SMEM), anywhere, fixed, fixed] + [anywhere] * len(old),
        out_specs=pl.BlockSpec((1, edge, plane), lambda s: (s + first, 0, 0)),
        out_shape=jax.ShapeDtypeStruct(density.shape, F32),
        scratch_shapes=[
            pltpu.VMEM((2, edge, plane // 128, 128), F32),
            pltpu.VMEM((pairs * edge, 768), BF16),
            pltpu.VMEM((2 * pairs * edge, 128), F32),
            pltpu.VMEM((16 * half, 128), F32),
            pltpu.VMEM((8 * half, 768), BF16),
            pltpu.VMEM((16 * half, 128), F32),
            pltpu.SemaphoreType.DMA((2,)),
        ],
        input_output_aliases={} if before is None else {4: 0},
        compiler_params=pltpu.CompilerParams(vmem_limit_bytes=VMEM_LIMIT),
        cost_estimate=pl.CostEstimate(
            flops=6 * (last - first) * edge * plane * 256,
            bytes_accessed=2 * (last - first) * MIB,
            transcendentals=0,
        ),
        name="fine",
    )(owner_counts, density, stacked(w1), stacked(w2), *old)


def coarse_kernel(
    index_ref,
    piece_ref,
    wx_ref,
    wzh_ref,
    wzl_ref,
    wyh_ref,
    wyl_ref,
    w23h_ref,
    w23l_ref,
    wx2_ref,
    wx3_ref,
    fine_ref,
    out_ref,
    block_ref,
    corner_ref,
    corner_sem,
    out_sem,
):
    slots = corner_ref.shape[0]
    lane = lax.broadcasted_iota(jnp.int32, (16, 128), 1)

    def window(s):
        return out_ref.at[s, pl.ds(0, 16), pl.ds(0, 1024)]

    def piece(i):
        return jnp.concatenate([piece_ref[pl.ds(16 * h + i, 16, stride=32), :] for h in range(2)], 1)

    for s in range(slots):
        pltpu.make_async_copy(window(s), corner_ref.at[s], corner_sem.at[s]).start()

    first = [
        [
            times_left(wx_ref[...], jnp.concatenate([piece(o * 8 + 2 * q), piece(o * 8 + 2 * q + 1)], 0))
            for q in range(4)
        ]
        for o in range(2)
    ]
    stacked = []
    for o in range(2):
        for cy in range(2):
            for yh in range(2):
                part = slice(yh * 128, yh * 128 + 128)
                stacked.append(jnp.concatenate([first[o][cy][:, part], first[o][2 + cy][:, part]], 1))
    lifted = times(jnp.concatenate(stacked, 0), wzh_ref[...], wzl_ref[...])
    stacked = []
    for o in range(2):
        for tz in range(2):
            stacked.append(
                jnp.concatenate(
                    [lifted[(o * 4 + u) * 32 : (o * 4 + u + 1) * 32, tz * 128 : tz * 128 + 128] for u in range(4)],
                    1,
                )
            )
    lifted = times(jnp.concatenate(stacked, 0), wyh_ref[...], wyl_ref[...])
    corner = []
    for o in range(2):
        for tz in range(2):
            for ty in range(2):
                for tx in range(2):
                    at = (o * 2 + tz) * 32 + tx * 16
                    value = lifted[at : at + 16, ty * 256 : ty * 256 + 256]
                    if tx + ty + tz == 0:
                        corner.append(value)
                    else:
                        block_ref[o * 8 + tx + 2 * ty + 4 * tz] = value
    both = times(jnp.concatenate(corner, 0), w23h_ref[...], w23l_ref[...])
    spot = lax.broadcasted_iota(jnp.int32, (16, 256), 1)
    depth = lax.broadcasted_iota(jnp.int32, (16, 256), 0)
    small = (depth < 8) & (spot < 128) & ((spot & 15) < 8)
    for o in range(2):
        mine = both[o * 16 : o * 16 + 16]
        second = times_left(wx2_ref[...], mine[:, :256])
        third = times_left(wx3_ref[...], mine[:, 256:])
        block_ref[o * 8] = jnp.where(small, third, second)

    for s in range(slots):
        pltpu.make_async_copy(window(s), corner_ref.at[s], corner_sem.at[s]).wait()
    for s in range(slots):

        @pl.when(s < index_ref[1])
        def _():
            value = block_ref[index_ref[0] + s]
            for t in range(8):
                tile = value[:, (t // 4) * 128 : (t // 4) * 128 + 128]
                near = pltpu.roll(tile, (128 - 32 * (t % 4)) % 128, 1)
                far = pltpu.roll(tile, (64 - 16 - 32 * (t % 4)) % 128, 1)
                old = corner_ref[s, :, pl.ds(t * 128, 128)]
                new = jnp.where(lane < 16, near, jnp.where((lane >= 64) & (lane < 80), far, old))
                corner_ref[s, :, pl.ds(t * 128, 128)] = new
            pltpu.make_async_copy(corner_ref.at[s], window(s), out_sem.at[s]).start()

    for s in range(slots):

        @pl.when(s < index_ref[1])
        def _():
            pltpu.make_async_copy(corner_ref.at[s], window(s), out_sem.at[s]).wait()


def coarse_call(index, pieces, fine):
    slots, edge, plane = fine.shape
    m32, m16, m8 = pass_matrix(32), pass_matrix(16), pass_matrix(8)
    deep = np.zeros((16, 16))
    deep[:8] = m8 @ m16[:8]
    eye8, eye16 = np.eye(8), np.eye(16)
    wz = np.zeros((256, 256))
    for cz in range(2):
        for tz in range(2):
            wz[cz * 128 : cz * 128 + 128, tz * 128 : tz * 128 + 128] = np.kron(
                eye8, m32[tz * 16 : tz * 16 + 16, cz * 16 : cz * 16 + 16].T
            )
    w23 = np.concatenate([np.kron(m16.T, m16.T), np.kron(deep.T, deep.T)], 1)
    weights = [
        left_terms(m32),
        *two_terms(wz),
        *two_terms(np.kron(m32.T, eye16)),
        *two_terms(w23),
        left_terms(m16),
        left_terms(deep),
    ]
    anywhere = pl.BlockSpec(memory_space=pl.ANY)
    vmem = pl.BlockSpec(memory_space=pltpu.VMEM)
    return pl.pallas_call(
        coarse_kernel,
        in_specs=[pl.BlockSpec(memory_space=pltpu.SMEM), vmem] + [vmem] * len(weights) + [anywhere],
        out_specs=anywhere,
        out_shape=jax.ShapeDtypeStruct(fine.shape, F32),
        scratch_shapes=[
            pltpu.VMEM((16, 16, 256), F32),
            pltpu.VMEM((slots, 16, 1024), F32),
            pltpu.SemaphoreType.DMA((slots,)),
            pltpu.SemaphoreType.DMA((slots,)),
        ],
        input_output_aliases={2 + len(weights): 0},
        compiler_params=pltpu.CompilerParams(vmem_limit_bytes=VMEM_LIMIT),
        name="coarse",
    )(index, pieces.reshape(-1, 128), *weights, fine)


def exchange(lowpass, slots, meanwhile):
    me = lax.axis_index(AXES)
    devices = lax.axis_size(AXES)
    if devices == lowpass.shape[0]:
        got = lax.all_to_all(lowpass, AXES, 0, 0, tiled=True)
        sent, index = route_call(me.reshape(1), got, meanwhile, slots)
        return lax.all_to_all(sent, AXES, 0, 0, tiled=True), index
    every = lax.all_gather(lowpass, AXES, axis=0)
    counts = every[:, 0, 7, 0].astype(jnp.int32)
    starts = jnp.cumsum(counts) - counts
    blocks = starts[me] // 8 * 8 + jnp.arange(16, dtype=jnp.int32)
    owners = jnp.sum((starts[None, :] <= blocks[:, None]).astype(jnp.int32), axis=1) - 1
    place = jnp.minimum(blocks - starts[owners], slots - 1)
    pieces = jnp.transpose(every[owners, :, place], (1, 0, 2))
    return pieces, jnp.stack([starts[me] % 8, counts[me]])


def per_device(density, owner_counts):
    lowpass = lowpass_call(owner_counts, density)
    slots = density.shape[0]
    fine = fine_call(owner_counts, density, 0, slots // 2, after=lowpass)
    pieces, index = exchange(lowpass, slots, fine)
    fine = fine_call(owner_counts, density, slots // 2, slots, fine)
    return coarse_call(index, pieces, fine)


def solution(mesh):
    in_specs = (P(AXES, None, None), P(AXES))
    out_specs = P(AXES, None, None)
    return jax.shard_map(per_device, mesh=mesh, in_specs=in_specs, out_specs=out_specs, check_vma=False)
```

```python
import functools

import jax
import jax.numpy as jnp
import numpy as np
from jax import lax
from jax.experimental import pallas as pl
from jax.experimental.pallas import tpu as pltpu
from jax.sharding import PartitionSpec as P

ALPHA = -1.586134342059924
BETA = -0.052980118572961
GAMMA = 0.882911075530934
DELTA = 0.443506852043971
SCALE = 1.230174104914001
SQUARE = SCALE * SCALE
F32 = jnp.float32
BF16 = jnp.bfloat16
AXES = ("node", "dev")
MIB = 1 << 20
VMEM_LIMIT = 56 * MIB


def pass_matrix(n):
    low, high = np.eye(n)[0::2], np.eye(n)[1::2]

    def after(v):
        return np.concatenate([v[1:], v[-1:]], 0)

    def before(v):
        return np.concatenate([v[:1], v[:-1]], 0)

    high = high + ALPHA * (low + after(low))
    low = low + BETA * (before(high) + high)
    high = high + GAMMA * (low + after(low))
    low = low + DELTA * (before(high) + high)
    return np.concatenate([low / SCALE, high * SCALE], 0)


def two_terms(matrix):
    matrix = np.asarray(matrix, np.float32)
    first = matrix.astype(BF16)
    return first, (matrix - first.astype(np.float32)).astype(BF16)


def left_terms(matrix):
    first, second = two_terms(matrix)
    return np.concatenate([first, second, first], 1)


def split(value):
    first = value.astype(BF16)
    return first, (value - first.astype(F32)).astype(BF16)


def dot(left, right):
    return jnp.dot(left, right, preferred_element_type=F32)


def times(value, first, second):
    high, low = split(value)
    return dot(high, first) + dot(low, first) + dot(high, second)


def times_left(terms, value):
    high, low = split(value)
    return dot(terms, jnp.concatenate([high, high, low], 0))


def start_tiles(src_ref, dst_ref, sem, tiles):
    for t in tiles:
        pltpu.make_async_copy(src_ref.at[..., pl.ds(t * 128, 128)], dst_ref.at[..., t, :], sem).start()


def split_rows(rows):
    return [split(jnp.concatenate(rows[m : m + 2], 0)) for m in range(0, len(rows), 2)]


def lowpass_kernel(
    count_ref, x_ref, wz_any, wyh_any, wyl_any, out_ref, x_buf, wz_ref, wyh_ref, wyl_ref, l_ref, z_ref, sems, w_sems
):
    slots, edge = x_ref.shape[:2]
    quarter = edge // 4

    def copies(g):
        return [
            pltpu.make_async_copy(
                x_ref.at[:, :, pl.ds(t * 128, 128)],
                x_buf.at[pl.ds(t * slots, slots)],
                sems.at[g],
            )
            for t in range(8 * g, 8 * g + 8)
        ]

    weights = [
        pltpu.make_async_copy(src, dst, w_sems.at[i])
        for i, (src, dst) in enumerate(((wz_any, wz_ref), (wyh_any, wyh_ref), (wyl_any, wyl_ref)))
    ]
    order = (0, 2, 1, 3)
    for g in order[:2]:
        for copy in copies(g):
            copy.start()
    rows_ref = x_buf.reshape(x_buf.shape[0] * edge, 128)
    for n, g in enumerate(order):
        part = x_buf.at[pl.ds(8 * g * slots, 8 * slots)]
        pltpu.make_async_copy(part, part, sems.at[g]).wait()
        if n + 2 < len(order):
            for copy in copies(order[n + 2]):
                copy.start()
        if n == 0:
            for copy in weights:
                copy.start()
        at = (g // 2) * 128

        @pl.loop(0, slots)
        def _(s):
            base = (8 * g * slots + s) * edge
            rows = [rows_ref[pl.ds(base + x, 8, stride=slots * edge), :] for x in range(edge)]
            rows, _ = lift(rows[0::2], rows[1::2], edge // 2, False, False)
            rows, _ = lift(rows[0::2], rows[1::2], quarter, False, False)
            for m, (high, low) in enumerate(split_rows(rows)):
                place = pl.ds(pl.multiple_of(s * 8 * quarter + 16 * m, 16), 16)
                l_ref[g % 2, place, pl.ds(at, 128)] = high
                l_ref[g % 2, place, pl.ds(256 + at, 128)] = low
                l_ref[g % 2, place, pl.ds(512 + at, 128)] = high

        if n == 1:
            weights[0].wait()
            z_ref[...] = dot(l_ref[0], wz_ref[0])
        if n == 3:
            z_ref[...] += dot(l_ref[1], wz_ref[1])

    for copy in weights[1:]:
        copy.wait()
    wide = jnp.concatenate([z_ref[pl.ds(i, slots * quarter, stride=8), :] for i in range(8)], 1)
    made = times(wide, wyh_ref[...], wyl_ref[...])
    out_ref[...] = jnp.full(out_ref.shape, count_ref[0].astype(F32))
    for slot in range(slots):
        for h in range(2):
            out_ref[pl.ds(8 * h + slot, quarter, stride=16), :] = made[
                slot * quarter : (slot + 1) * quarter, h * 128 : h * 128 + 128
            ]


def stacked(matrix):
    first, second = two_terms(matrix)
    return np.concatenate([first, first, second], 0)


def lowpass_call(owner_counts, density):
    slots, edge, plane = density.shape
    quarter = edge // 4
    two_levels = pass_matrix(edge // 2)[:quarter] @ pass_matrix(edge)[: edge // 2]
    wide = np.kron(np.eye(8), two_levels.T)
    wz = np.stack([stacked(wide[:256]), stacked(wide[256:])])
    i, gp, q, p = np.meshgrid(np.arange(8), np.arange(2), np.arange(2), np.arange(2), indexing="ij")
    entry = (2 * (8 * gp + i) + p + 32 * q).reshape(-1)
    wy = np.kron(two_levels.T[entry] / SQUARE, np.eye(quarter))
    wyh, wyl = two_terms(wy)
    anywhere = pl.BlockSpec(memory_space=pl.ANY)
    pieces = pl.pallas_call(
        lowpass_kernel,
        in_specs=[pl.BlockSpec(memory_space=pltpu.SMEM)] + [anywhere] * 4,
        out_specs=pl.BlockSpec(memory_space=pltpu.VMEM),
        out_shape=jax.ShapeDtypeStruct((16 * quarter, 128), F32),
        scratch_shapes=[
            pltpu.VMEM((plane // 128 * slots, edge, 128), F32),
            pltpu.VMEM(wz.shape, BF16),
            pltpu.VMEM(wyh.shape, BF16),
            pltpu.VMEM(wyl.shape, BF16),
            pltpu.VMEM((2, slots * 8 * quarter, 768), BF16),
            pltpu.VMEM((slots * 8 * quarter, 128), F32),
            pltpu.SemaphoreType.DMA((4,)),
            pltpu.SemaphoreType.DMA((3,)),
        ],
        compiler_params=pltpu.CompilerParams(vmem_limit_bytes=VMEM_LIMIT),
        name="lowpass",
    )(owner_counts, density, wz, wyh, wyl)
    return pieces.reshape(2 * quarter, 8, 128)


def route_kernel(me_ref, got_any, _, send_ref, index_ref, got_ref, order_ref, count_ref, sems):
    devices = got_ref.shape[0]
    copies = [
        pltpu.make_async_copy(got_any.at[:, 7, :], count_ref, sems.at[0]),
        pltpu.make_async_copy(got_any, got_ref, sems.at[1]),
    ]
    for copy in copies:
        copy.start()
    order_ref[...] = jnp.zeros_like(order_ref)
    for copy in copies:
        copy.wait()
    start, my_start, my_count = 0, 0, 0
    starts = []
    for d in range(devices):
        count = count_ref[d, 0].astype(jnp.int32)
        starts.append(start)
        my_start = jnp.where(me_ref[0] == d, start, my_start)
        my_count = jnp.where(me_ref[0] == d, count, my_count)
        order_ref[pl.ds(start, 8), :] = got_ref[d]
        start = start + count
    for d in range(devices):
        at = pl.multiple_of(starts[d] // 8 * 8, 8) if d else 0
        send_ref[d] = order_ref[pl.ds(at, 16), :]
    index_ref[0] = my_start % 8
    index_ref[1] = my_count


def route_call(me, got, meanwhile, slots):
    devices = got.shape[0]
    return pl.pallas_call(
        route_kernel,
        in_specs=[
            pl.BlockSpec(memory_space=pltpu.SMEM),
            pl.BlockSpec(memory_space=pl.ANY),
            pl.BlockSpec(memory_space=pl.ANY),
        ],
        out_specs=[pl.BlockSpec(memory_space=pltpu.VMEM), pl.BlockSpec(memory_space=pltpu.SMEM)],
        out_shape=[
            jax.ShapeDtypeStruct((devices, 16, 128), F32),
            jax.ShapeDtypeStruct((2,), jnp.int32),
        ],
        scratch_shapes=[
            pltpu.VMEM(got.shape, F32),
            pltpu.VMEM((devices * slots + 16, 128), F32),
            pltpu.SMEM((devices, 128), F32),
            pltpu.SemaphoreType.DMA((2,)),
        ],
        compiler_params=pltpu.CompilerParams(vmem_limit_bytes=VMEM_LIMIT),
        name="route",
    )(me, got, meanwhile)


def lift(low, high, n, halo, scaled):
    up = SQUARE if scaled else 1.0
    at = 2 if halo else 0
    first, second, third, fourth = ({} for _ in range(4))

    def get(values, i, is_low):
        if halo:
            return values[i]
        return values[min(i, n - 1)] if is_low else values[max(i, 0)]

    lows = {i - at: low[i] for i in range(len(low))}
    highs = {i - at: high[i] for i in range(len(high))}

    def make_first(i):
        first[i] = highs[i] + (ALPHA * up) * (lows[i] + get(lows, i + 1, True))

    def make_second(i):
        second[i] = lows[i] + (BETA / up) * (get(first, i - 1, False) + first[i])

    def make_third(i):
        third[i] = first[i] + (GAMMA * up) * (second[i] + get(second, i + 1, True))

    def make_fourth(i):
        fourth[i] = second[i] + (DELTA / up) * (get(third, i - 1, False) + third[i])

    if halo:
        for i in range(-2, n + 1):
            make_first(i)
            if i >= -1:
                make_second(i)
            if i >= 0:
                make_third(i - 1)
            if i >= 1:
                make_fourth(i - 1)
    else:
        for i in range(n):
            make_first(i)
            make_second(i)
            if i >= 1:
                make_third(i - 1)
                make_fourth(i - 1)
        make_third(n - 1)
        make_fourth(n - 1)
    return [fourth[i] for i in range(n)], [third[i] for i in range(n)]


def fine_kernel(count_ref, x_ref, w1_ref, w2_ref, *refs, offset):
    out_ref, x_buf, l_ref, y_ref, c_ref, m_ref, d_ref, sems = refs[-8:]
    step = pl.program_id(0)
    slot = step + offset
    edge = x_ref.shape[1]
    tiles = x_ref.shape[2] // 128
    pairs = tiles // 2
    half = edge // 2
    lane = lax.broadcasted_iota(jnp.int32, (8, 128), 1)
    front = lane < 64
    inner = (lane & 63) < half

    def turn(value):
        return pltpu.roll(value, 64, 1)

    def with_halo(low, high):
        def left(values, i):
            return jnp.where(front, values[i[0]], turn(values[i[1]]))

        def right(values, i):
            return jnp.where(front, turn(values[i[0]]), values[i[1]])

        low_all = [left(low, (2, -2)), left(low, (1, -1))] + low + [right(low, (0, -1)), right(low, (1, -2))]
        high_all = [left(high, (1, -2)), left(high, (0, -1))] + high + [right(high, (0, -2))]
        return low_all, high_all

    def fetch(which, place, which_tiles):
        start_tiles(x_ref.at[which], x_buf.at[place], sems.at[place], which_tiles)

    def fetch_next(phase):
        @pl.when((step + 1 < pl.num_programs(0)) & (slot + 1 < count_ref[0]))
        def _():
            fetch(slot + 1, (step + 1) % 2, range(2 * phase, 2 * phase + 2))

    def scaled_rows(rows):
        low, high = lift(rows[0::2], rows[1::2], len(rows) // 2, False, False)
        return [v * (1.0 / SCALE) for v in low] + [v * SCALE for v in high]

    def store_terms(ref, row, col, rows):
        for m, (high, low) in enumerate(split_rows(rows)):
            place = pl.ds(row + 16 * m, 16)
            ref[place, pl.ds(col, 128)] = high
            ref[place, pl.ds(256 + col, 128)] = low
            ref[place, pl.ds(512 + col, 128)] = high

    @pl.when((step == 0) & (slot < count_ref[0]))
    def _():
        fetch(slot, 0, range(tiles))

    @pl.when(slot >= count_ref[0])
    def _():
        out_ref[...] = jnp.zeros_like(out_ref)

    @pl.when(slot < count_ref[0])
    def _():
        x = x_buf.at[step % 2]
        pltpu.make_async_copy(x, x, sems.at[step % 2]).wait()
        for g in range(4):
            rows = scaled_rows([x[i, pl.ds(8 * g, 8), :] for i in range(edge)])
            store_terms(l_ref, (g % 2) * 8 * edge, (g // 2) * 128, rows)
            fetch_next(2 * g)
            fetch_next(2 * g + 1)
        lifted = dot(l_ref[...], w1_ref[...])
        y_ref[pl.ds(0, pairs * edge), :] = lifted[:, :128]
        y_ref[pl.ds(pairs * edge, pairs * edge), :] = lifted[:, 128:]
        for r in range(edge // 8):
            rows = pl.ds(8 * r, 8)

            def tile(part, j):
                at = (part * 2 + j // 8) * 8 * edge + 64 * r + j % 8
                return y_ref[pl.ds(at, 8, stride=8), :]

            low = [tile(0, j) for j in range(pairs)]
            high = [tile(1, j) for j in range(pairs)]
            low, high = lift(*with_halo(low, high), pairs, True, True)
            for part, values in enumerate((low, high)):
                for t in range(pairs // 2):
                    a, b = values[2 * t], values[2 * t + 1]
                    at = part * pairs + t
                    out_ref[0, rows, pl.ds(at * 128, 128)] = jnp.where(front, a, turn(b))
                    out_ref[0, rows, pl.ds((at + pairs // 2) * 128, 128)] = jnp.where(front, turn(a), b)
            if r < half // 8:
                low, high = lift(*with_halo(low[0::2], low[1::2]), 8, True, False)
                for i in range(8):
                    c_ref[pl.ds(i * half + 8 * r, 8), :] = low[i]
                    c_ref[pl.ds((8 + i) * half + 8 * r, 8), :] = high[i]
            fetch_next(8 + r)
        for u in range(2):
            rows = scaled_rows([c_ref[pl.ds(u * 8 * half + i, 8, stride=half), :] for i in range(half)])
            store_terms(m_ref, 0, u * 128, rows)
        lifted = dot(m_ref[...], w2_ref[...])
        d_ref[pl.ds(0, 8 * half), :] = lifted[:, :128]
        d_ref[pl.ds(8 * half, 8 * half), :] = lifted[:, 128:]
        for u in range(2):
            for t in range(4):
                for r in range(half // 8):
                    a = d_ref[pl.ds(u * 8 * half + 64 * r + 2 * t, 8, stride=8), :]
                    b = d_ref[pl.ds(u * 8 * half + 64 * r + 2 * t + 1, 8, stride=8), :]
                    for at, value in (
                        (u * 8 + t, jnp.where(front, a, turn(b))),
                        (u * 8 + 4 + t, jnp.where(front, turn(a), b)),
                    ):
                        rows, cols = pl.ds(8 * r, 8), pl.ds(at * 128, 128)
                        out_ref[0, rows, cols] = jnp.where(inner, value, out_ref[0, rows, cols])


def fine_call(owner_counts, density, first, last, before=None, after=None):
    slots, edge, plane = density.shape
    half = edge // 2
    pairs = plane // 256
    one = pass_matrix(edge).T
    zero = np.zeros_like(one)
    w1 = np.block(
        [
            [one / SCALE, zero, zero, zero],
            [zero, zero, one * SCALE, zero],
            [zero, one / SCALE, zero, zero],
            [zero, zero, zero, one * SCALE],
        ]
    )
    two = np.zeros_like(one)
    two[:half, :half] = pass_matrix(half).T
    w2 = np.kron(np.diag([1 / SCALE, 1 / SCALE, SCALE, SCALE]), two)
    anywhere = pl.BlockSpec(memory_space=pl.ANY)
    fixed = pl.BlockSpec((768, 256), lambda s: (0, 0))
    old = [after] if before is None else [before]
    return pl.pallas_call(
        functools.partial(fine_kernel, offset=first),
        grid=(last - first,),
        in_specs=[pl.BlockSpec(memory_space=pltpu.SMEM), anywhere, fixed, fixed] + [anywhere] * len(old),
        out_specs=pl.BlockSpec((1, edge, plane), lambda s: (s + first, 0, 0)),
        out_shape=jax.ShapeDtypeStruct(density.shape, F32),
        scratch_shapes=[
            pltpu.VMEM((2, edge, plane // 128, 128), F32),
            pltpu.VMEM((pairs * edge, 768), BF16),
            pltpu.VMEM((2 * pairs * edge, 128), F32),
            pltpu.VMEM((16 * half, 128), F32),
            pltpu.VMEM((8 * half, 768), BF16),
            pltpu.VMEM((16 * half, 128), F32),
            pltpu.SemaphoreType.DMA((2,)),
        ],
        input_output_aliases={} if before is None else {4: 0},
        compiler_params=pltpu.CompilerParams(vmem_limit_bytes=VMEM_LIMIT),
        cost_estimate=pl.CostEstimate(
            flops=6 * (last - first) * edge * plane * 256,
            bytes_accessed=2 * (last - first) * MIB,
            transcendentals=0,
        ),
        name="fine",
    )(owner_counts, density, stacked(w1), stacked(w2), *old)


def coarse_kernel(
    index_ref,
    piece_any,
    wx_ref,
    wx2_ref,
    wx3_ref,
    wz_any,
    wy_any,
    w23_any,
    fine_ref,
    out_ref,
    wz_ref,
    wy_ref,
    w23_ref,
    piece_ref,
    block_ref,
    corner_ref,
    piece_sem,
    weight_sem,
    corner_sem,
    out_sem,
):
    slots = corner_ref.shape[0]
    lane = lax.broadcasted_iota(jnp.int32, (16, 128), 1)

    def window(s):
        return out_ref.at[s, pl.ds(0, 16), pl.ds(0, 1024)]

    def piece(i):
        return jnp.concatenate([piece_ref[pl.ds(16 * h + i, 16, stride=32), :] for h in range(2)], 1)

    pieces = pltpu.make_async_copy(piece_any, piece_ref, piece_sem)
    pieces.start()
    weights = [
        pltpu.make_async_copy(src, dst, weight_sem.at[i])
        for i, (src, dst) in enumerate(((wz_any, wz_ref), (wy_any, wy_ref), (w23_any, w23_ref)))
    ]
    for copy in weights:
        copy.start()
    for s in range(slots):
        pltpu.make_async_copy(window(s), corner_ref.at[s], corner_sem.at[s]).start()
    pieces.wait()

    first = [
        [
            times_left(wx_ref[...], jnp.concatenate([piece(o * 8 + 2 * q), piece(o * 8 + 2 * q + 1)], 0))
            for q in range(4)
        ]
        for o in range(2)
    ]
    stacked = []
    for o in range(2):
        for cy in range(2):
            for yh in range(2):
                part = slice(yh * 128, yh * 128 + 128)
                stacked.append(jnp.concatenate([first[o][cy][:, part], first[o][2 + cy][:, part]], 1))
    weights[0].wait()
    lifted = times(jnp.concatenate(stacked, 0), wz_ref[0], wz_ref[1])
    stacked = []
    for o in range(2):
        for tz in range(2):
            stacked.append(
                jnp.concatenate(
                    [lifted[(o * 4 + u) * 32 : (o * 4 + u + 1) * 32, tz * 128 : tz * 128 + 128] for u in range(4)],
                    1,
                )
            )
    weights[1].wait()
    lifted = times(jnp.concatenate(stacked, 0), wy_ref[0], wy_ref[1])
    corner = []
    for o in range(2):
        for tz in range(2):
            for ty in range(2):
                for tx in range(2):
                    at = (o * 2 + tz) * 32 + tx * 16
                    value = lifted[at : at + 16, ty * 256 : ty * 256 + 256]
                    if tx + ty + tz == 0:
                        corner.append(value)
                    else:
                        block_ref[o * 8 + tx + 2 * ty + 4 * tz] = value
    weights[2].wait()
    both = times(jnp.concatenate(corner, 0), w23_ref[0], w23_ref[1])
    spot = lax.broadcasted_iota(jnp.int32, (16, 256), 1)
    depth = lax.broadcasted_iota(jnp.int32, (16, 256), 0)
    small = (depth < 8) & (spot < 128) & ((spot & 15) < 8)
    for o in range(2):
        mine = both[o * 16 : o * 16 + 16]
        second = times_left(wx2_ref[...], mine[:, :256])
        third = times_left(wx3_ref[...], mine[:, 256:])
        block_ref[o * 8] = jnp.where(small, third, second)

    for s in range(slots):
        pltpu.make_async_copy(window(s), corner_ref.at[s], corner_sem.at[s]).wait()
    for s in range(slots):

        @pl.when(s < index_ref[1])
        def _():
            value = block_ref[index_ref[0] + s]
            for t in range(8):
                tile = value[:, (t // 4) * 128 : (t // 4) * 128 + 128]
                near = pltpu.roll(tile, (128 - 32 * (t % 4)) % 128, 1)
                far = pltpu.roll(tile, (64 - 16 - 32 * (t % 4)) % 128, 1)
                old = corner_ref[s, :, pl.ds(t * 128, 128)]
                new = jnp.where(lane < 16, near, jnp.where((lane >= 64) & (lane < 80), far, old))
                corner_ref[s, :, pl.ds(t * 128, 128)] = new
            pltpu.make_async_copy(corner_ref.at[s], window(s), out_sem.at[s]).start()

    for s in range(slots):

        @pl.when(s < index_ref[1])
        def _():
            pltpu.make_async_copy(corner_ref.at[s], window(s), out_sem.at[s]).wait()


def coarse_call(index, pieces, fine):
    slots, edge, plane = fine.shape
    m32, m16, m8 = pass_matrix(32), pass_matrix(16), pass_matrix(8)
    deep = np.zeros((16, 16))
    deep[:8] = m8 @ m16[:8]
    eye8, eye16 = np.eye(8), np.eye(16)
    wz = np.zeros((256, 256))
    for cz in range(2):
        for tz in range(2):
            wz[cz * 128 : cz * 128 + 128, tz * 128 : tz * 128 + 128] = np.kron(
                eye8, m32[tz * 16 : tz * 16 + 16, cz * 16 : cz * 16 + 16].T
            )
    w23 = np.concatenate([np.kron(m16.T, m16.T), np.kron(deep.T, deep.T)], 1)
    small = [left_terms(m32), left_terms(m16), left_terms(deep)]
    large = [np.stack(two_terms(w)) for w in (wz, np.kron(m32.T, eye16), w23)]
    weights = small + large
    anywhere = pl.BlockSpec(memory_space=pl.ANY)
    vmem = pl.BlockSpec(memory_space=pltpu.VMEM)
    return pl.pallas_call(
        coarse_kernel,
        in_specs=[pl.BlockSpec(memory_space=pltpu.SMEM), anywhere] + [vmem] * len(small) + [anywhere] * (len(large) + 1),
        out_specs=anywhere,
        out_shape=jax.ShapeDtypeStruct(fine.shape, F32),
        scratch_shapes=[
            *[pltpu.VMEM(w.shape, BF16) for w in large],
            pltpu.VMEM((32 * 16, 128), F32),
            pltpu.VMEM((16, 16, 256), F32),
            pltpu.VMEM((slots, 16, 1024), F32),
            pltpu.SemaphoreType.DMA,
            pltpu.SemaphoreType.DMA((3,)),
            pltpu.SemaphoreType.DMA((slots,)),
            pltpu.SemaphoreType.DMA((slots,)),
        ],
        input_output_aliases={2 + len(weights): 0},
        compiler_params=pltpu.CompilerParams(vmem_limit_bytes=VMEM_LIMIT),
        name="coarse",
    )(index, pieces.reshape(-1, 128), *weights, fine)


def exchange(lowpass, slots, meanwhile):
    me = lax.axis_index(AXES)
    devices = lax.axis_size(AXES)
    if devices == lowpass.shape[0]:
        got = lax.all_to_all(lowpass, AXES, 0, 0, tiled=True)
        sent, index = route_call(me.reshape(1), got, meanwhile, slots)
        return lax.all_to_all(sent, AXES, 0, 0, tiled=True), index
    every = lax.all_gather(lowpass, AXES, axis=0)
    counts = every[:, 0, 7, 0].astype(jnp.int32)
    starts = jnp.cumsum(counts) - counts
    blocks = starts[me] // 8 * 8 + jnp.arange(16, dtype=jnp.int32)
    owners = jnp.sum((starts[None, :] <= blocks[:, None]).astype(jnp.int32), axis=1) - 1
    place = jnp.minimum(blocks - starts[owners], slots - 1)
    pieces = jnp.transpose(every[owners, :, place], (1, 0, 2))
    return pieces, jnp.stack([starts[me] % 8, counts[me]])


def per_device(density, owner_counts):
    lowpass = lowpass_call(owner_counts, density)
    slots = density.shape[0]
    early = slots // 3
    fine = fine_call(owner_counts, density, 0, early, after=lowpass)
    pieces, index = exchange(lowpass, slots, fine)
    fine = fine_call(owner_counts, density, early, slots, fine)
    return coarse_call(index, pieces, fine)


def solution(mesh):
    in_specs = (P(AXES, None, None), P(AXES))
    out_specs = P(AXES, None, None)
    return jax.shard_map(per_device, mesh=mesh, in_specs=in_specs, out_specs=out_specs, check_vma=False)
```

```python
import functools

import jax
import jax.numpy as jnp
import numpy as np
from jax import lax
from jax.experimental import pallas as pl
from jax.experimental.pallas import tpu as pltpu
from jax.sharding import PartitionSpec as P

ALPHA = -1.586134342059924
BETA = -0.052980118572961
GAMMA = 0.882911075530934
DELTA = 0.443506852043971
SCALE = 1.230174104914001
SQUARE = SCALE * SCALE
F32 = jnp.float32
BF16 = jnp.bfloat16
AXES = ("node", "dev")
MIB = 1 << 20
VMEM_LIMIT = 40 * MIB
VMEM_SMALL = 16 * MIB
VMEM_LARGE = 45 * MIB


def pass_matrix(n):
    low, high = np.eye(n)[0::2], np.eye(n)[1::2]

    def after(v):
        return np.concatenate([v[1:], v[-1:]], 0)

    def before(v):
        return np.concatenate([v[:1], v[:-1]], 0)

    high = high + ALPHA * (low + after(low))
    low = low + BETA * (before(high) + high)
    high = high + GAMMA * (low + after(low))
    low = low + DELTA * (before(high) + high)
    return np.concatenate([low / SCALE, high * SCALE], 0)


def two_terms(matrix):
    matrix = np.asarray(matrix, np.float32)
    first = matrix.astype(BF16)
    return first, (matrix - first.astype(np.float32)).astype(BF16)


def left_terms(matrix):
    first, second = two_terms(matrix)
    return np.concatenate([first, second, first], 1)


def split(value):
    first = value.astype(BF16)
    return first, (value - first.astype(F32)).astype(BF16)


def dot(left, right):
    return jnp.dot(left, right, preferred_element_type=F32)


def times(value, first, second):
    high, low = split(value)
    both = dot(jnp.concatenate([high, low], 0), first)
    count = value.shape[0]
    return both[:count] + both[count:] + dot(high, second)


def times_left(terms, value):
    high, low = split(value)
    return dot(terms, jnp.concatenate([high, high, low], 0))


def split_rows(rows):
    return [split(jnp.concatenate(rows[m : m + 2], 0)) for m in range(0, len(rows), 2)]


def lowpass_kernel(
    count_ref, x_any, wz_any, wyh_any, wyl_any, out_ref, x_ref, wz_ref, wyh_ref, wyl_ref, l_ref, z_ref, sems, w_sems
):
    slots, edge = x_any.shape[:2]
    quarter = edge // 4
    rows_all = slots * 8 * quarter
    for t in range(x_ref.shape[2]):
        pltpu.make_async_copy(
            x_any.at[:, :, pl.ds(t * 128, 128)], x_ref.at[:, :, t, :], sems.at[t // 8]
        ).start()
    weights = [
        pltpu.make_async_copy(src, dst, w_sems.at[i])
        for i, (src, dst) in enumerate(((wz_any, wz_ref), (wyh_any, wyh_ref), (wyl_any, wyl_ref)))
    ]
    for copy in weights:
        copy.start()
    for g in range(4):
        part = x_ref.at[:, :, pl.ds(8 * g, 8), :]
        pltpu.make_async_copy(part, part, sems.at[g]).wait()

        @pl.loop(0, slots)
        def _(s):
            rows = [x_ref[s, x, pl.ds(8 * g, 8), :] for x in range(edge)]
            rows, _ = lift(rows[0::2], rows[1::2], edge // 2, False, False)
            rows, _ = lift(rows[0::2], rows[1::2], quarter, False, False)
            for m, (high, low) in enumerate(split_rows(rows)):
                at = pl.multiple_of(s * 8 * quarter + 16 * m, 16)
                cols = pl.ds((g // 2) * 128, 128)
                l_ref[g % 2, pl.ds(at, 16), cols] = high
                l_ref[g % 2, pl.ds(rows_all + at, 16), cols] = low

    for copy in weights:
        copy.wait()
    made = dot(l_ref[0], wz_ref[0]) + dot(l_ref[1], wz_ref[1])
    z_ref[...] = (made[:rows_all, :128] + made[rows_all:, :128]) + made[:rows_all, 128:]
    wide = jnp.concatenate([z_ref[pl.ds(i, slots * quarter, stride=8), :] for i in range(8)], 1)
    made = times(wide, wyh_ref[...], wyl_ref[...])
    out_ref[...] = jnp.full(out_ref.shape, count_ref[0].astype(F32))
    for slot in range(slots):
        for h in range(2):
            out_ref[pl.ds(8 * h + slot, quarter, stride=16), :] = made[
                slot * quarter : (slot + 1) * quarter, h * 128 : h * 128 + 128
            ]


def stacked(matrix):
    first, second = two_terms(matrix)
    return np.concatenate([first, first, second], 0)


def lowpass_call(owner_counts, density):
    slots, edge, plane = density.shape
    quarter = edge // 4
    two_levels = pass_matrix(edge // 2)[:quarter] @ pass_matrix(edge)[: edge // 2]
    wide = np.kron(np.eye(8), two_levels.T)
    wz = np.stack([np.concatenate(two_terms(w), 1) for w in (wide[:256], wide[256:])])
    i, gp, q, p = np.meshgrid(np.arange(8), np.arange(2), np.arange(2), np.arange(2), indexing="ij")
    entry = (2 * (8 * gp + i) + p + 32 * q).reshape(-1)
    wy = np.kron(two_levels.T[entry] / SQUARE, np.eye(quarter))
    wyh, wyl = two_terms(wy)
    anywhere = pl.BlockSpec(memory_space=pl.ANY)
    vmem = pl.BlockSpec(memory_space=pltpu.VMEM)
    rows_all = slots * 8 * quarter
    pieces, held = pl.pallas_call(
        lowpass_kernel,
        in_specs=[pl.BlockSpec(memory_space=pltpu.SMEM)] + [anywhere] * 4,
        out_specs=[vmem, vmem],
        out_shape=[
            jax.ShapeDtypeStruct((16 * quarter, 128), F32),
            jax.ShapeDtypeStruct((slots, edge, plane // 128, 128), F32),
        ],
        scratch_shapes=[
            pltpu.VMEM(wz.shape, BF16),
            pltpu.VMEM(wyh.shape, BF16),
            pltpu.VMEM(wyl.shape, BF16),
            pltpu.VMEM((2, 2 * rows_all, 256), BF16),
            pltpu.VMEM((rows_all, 128), F32),
            pltpu.SemaphoreType.DMA((4,)),
            pltpu.SemaphoreType.DMA((3,)),
        ],
        compiler_params=pltpu.CompilerParams(vmem_limit_bytes=VMEM_LARGE),
        name="lowpass",
    )(owner_counts, density, wz, wyh, wyl)
    return pieces.reshape(2 * quarter, 8, 128), held


def route_kernel(me_ref, got_any, _, send_ref, index_ref, got_ref, order_ref, count_ref, sems):
    devices = got_ref.shape[0]
    copies = [
        pltpu.make_async_copy(got_any.at[:, 7, :], count_ref, sems.at[0]),
        pltpu.make_async_copy(got_any, got_ref, sems.at[1]),
    ]
    for copy in copies:
        copy.start()
    order_ref[...] = jnp.zeros_like(order_ref)
    for copy in copies:
        copy.wait()
    start, my_start, my_count = 0, 0, 0
    starts = []
    for d in range(devices):
        count = count_ref[d, 0].astype(jnp.int32)
        starts.append(start)
        my_start = jnp.where(me_ref[0] == d, start, my_start)
        my_count = jnp.where(me_ref[0] == d, count, my_count)
        order_ref[pl.ds(start, 8), :] = got_ref[d]
        start = start + count
    for d in range(devices):
        at = pl.multiple_of(starts[d] // 8 * 8, 8) if d else 0
        send_ref[d] = order_ref[pl.ds(at, 16), :]
    index_ref[0] = my_start % 8
    index_ref[1] = my_count


def route_call(me, got, token, slots):
    devices = got.shape[0]
    return pl.pallas_call(
        route_kernel,
        in_specs=[
            pl.BlockSpec(memory_space=pltpu.SMEM),
            pl.BlockSpec(memory_space=pl.ANY),
            pl.BlockSpec(memory_space=pltpu.SMEM),
        ],
        out_specs=[pl.BlockSpec(memory_space=pltpu.VMEM), pl.BlockSpec(memory_space=pltpu.SMEM)],
        out_shape=[
            jax.ShapeDtypeStruct((devices, 16, 128), F32),
            jax.ShapeDtypeStruct((2,), jnp.int32),
        ],
        scratch_shapes=[
            pltpu.VMEM(got.shape, F32),
            pltpu.VMEM((devices * slots + 16, 128), F32),
            pltpu.SMEM((devices, 128), F32),
            pltpu.SemaphoreType.DMA((2,)),
        ],
        compiler_params=pltpu.CompilerParams(vmem_limit_bytes=VMEM_SMALL),
        name="route",
    )(me, got, token)


def lift(low, high, n, halo, scaled):
    up = SQUARE if scaled else 1.0
    at = 2 if halo else 0
    first, second, third, fourth = ({} for _ in range(4))

    def get(values, i, is_low):
        if halo:
            return values[i]
        return values[min(i, n - 1)] if is_low else values[max(i, 0)]

    lows = {i - at: low[i] for i in range(len(low))}
    highs = {i - at: high[i] for i in range(len(high))}

    def make_first(i):
        first[i] = highs[i] + (ALPHA * up) * (lows[i] + get(lows, i + 1, True))

    def make_second(i):
        second[i] = lows[i] + (BETA / up) * (get(first, i - 1, False) + first[i])

    def make_third(i):
        third[i] = first[i] + (GAMMA * up) * (second[i] + get(second, i + 1, True))

    def make_fourth(i):
        fourth[i] = second[i] + (DELTA / up) * (get(third, i - 1, False) + third[i])

    if halo:
        for i in range(-2, n + 1):
            make_first(i)
            if i >= -1:
                make_second(i)
            if i >= 0:
                make_third(i - 1)
            if i >= 1:
                make_fourth(i - 1)
    else:
        for i in range(n):
            make_first(i)
            make_second(i)
            if i >= 1:
                make_third(i - 1)
                make_fourth(i - 1)
        make_third(n - 1)
        make_fourth(n - 1)
    return [fourth[i] for i in range(n)], [third[i] for i in range(n)]


def fine_kernel(count_ref, _, x_ref, w1_ref, w2_ref, *refs, first):
    out_ref, token_ref, l_ref, y_ref, c_ref, m_ref, d_ref, o_ref, sems = refs[-9:]
    slots, edge = o_ref.shape[:2]
    tiles = x_ref.shape[2]
    pairs = tiles // 2
    half = edge // 2
    block = pairs * edge
    corner = 8 * half
    live = jnp.clip(count_ref[0] - first, 0, slots)
    lane = lax.broadcasted_iota(jnp.int32, (8, 128), 1)
    front = lane < 64
    inner = (lane & 63) < half
    token_ref[0] = live

    def turn(value):
        return pltpu.roll(value, 64, 1)

    def with_halo(low, high):
        def left(values, i):
            return jnp.where(front, values[i[0]], turn(values[i[1]]))

        def right(values, i):
            return jnp.where(front, turn(values[i[0]]), values[i[1]])

        low_all = [left(low, (2, -2)), left(low, (1, -1))] + low + [right(low, (0, -1)), right(low, (1, -2))]
        high_all = [left(high, (1, -2)), left(high, (0, -1))] + high + [right(high, (0, -2))]
        return low_all, high_all

    def scaled_rows(rows):
        low, high = lift(rows[0::2], rows[1::2], len(rows) // 2, False, False)
        return [v * (1.0 / SCALE) for v in low] + [v * SCALE for v in high]

    def store_terms(ref, row, col, rows):
        for m, (high, low) in enumerate(split_rows(rows)):
            place = pl.ds(pl.multiple_of(row + 16 * m, 16), 16)
            ref[place, pl.ds(col, 128)] = high
            ref[place, pl.ds(256 + col, 128)] = low
            ref[place, pl.ds(512 + col, 128)] = high

    def write(s):
        return pltpu.make_async_copy(o_ref.at[s], out_ref.at[first + s], sems.at[s])

    @pl.loop(live, slots)
    def _(s):
        o_ref[s] = jnp.zeros(o_ref.shape[1:], F32)
        write(s).start()

    @pl.loop(0, live)
    def _(s):
        for g in range(4):
            rows = scaled_rows([x_ref[first + s, i, pl.ds(8 * g, 8), :] for i in range(edge)])
            store_terms(l_ref, s * block + (g % 2) * 8 * edge, (g // 2) * 128, rows)

    lifted = dot(l_ref[...], w1_ref[...])
    y_ref[0] = lifted[:, :128]
    y_ref[1] = lifted[:, 128:]

    @pl.loop(0, live)
    def _(s):
        for r in range(edge // 8):
            rows = pl.ds(8 * r, 8)

            def tile(part, j):
                return y_ref[part, pl.ds(s * block + (j // 8) * 8 * edge + 64 * r + j % 8, 8, stride=8), :]

            low = [tile(0, j) for j in range(pairs)]
            high = [tile(1, j) for j in range(pairs)]
            low, high = lift(*with_halo(low, high), pairs, True, True)
            for part, values in enumerate((low, high)):
                for t in range(pairs // 2):
                    a, b = values[2 * t], values[2 * t + 1]
                    at = part * pairs + t
                    o_ref[s, rows, pl.ds(at * 128, 128)] = jnp.where(front, a, turn(b))
                    o_ref[s, rows, pl.ds((at + pairs // 2) * 128, 128)] = jnp.where(front, turn(a), b)
            if r < half // 8:
                low, high = lift(*with_halo(low[0::2], low[1::2]), 8, True, False)
                for i in range(8):
                    c_ref[pl.ds(64 * r + i, 8, stride=8), :] = low[i]
                    c_ref[pl.ds(corner + 64 * r + i, 8, stride=8), :] = high[i]
        for u in range(2):
            rows = scaled_rows([c_ref[pl.ds(u * corner + 8 * i, 8), :] for i in range(half)])
            store_terms(m_ref, s * corner, u * 128, rows)

    lifted = dot(m_ref[...], w2_ref[...])
    d_ref[0] = lifted[:, :128]
    d_ref[1] = lifted[:, 128:]

    @pl.loop(0, live)
    def _(s):
        for u in range(2):
            for t in range(4):
                for r in range(half // 8):
                    base = s * corner + 64 * r + 2 * t
                    a = d_ref[u, pl.ds(base, 8, stride=8), :]
                    b = d_ref[u, pl.ds(base + 1, 8, stride=8), :]
                    for at, value in (
                        (u * 8 + t, jnp.where(front, a, turn(b))),
                        (u * 8 + 4 + t, jnp.where(front, turn(a), b)),
                    ):
                        rows, cols = pl.ds(8 * r, 8), pl.ds(at * 128, 128)
                        o_ref[s, rows, cols] = jnp.where(inner, value, o_ref[s, rows, cols])
        write(s).start()

    for s in range(slots):
        write(s).wait()


def fine_call(owner_counts, token, held, first, last, before=None):
    slots, edge, tiles, _ = held.shape
    half = edge // 2
    pairs = tiles // 2
    count = last - first
    one = pass_matrix(edge).T
    zero = np.zeros_like(one)
    w1 = np.block(
        [
            [one / SCALE, zero, zero, zero],
            [zero, zero, one * SCALE, zero],
            [zero, one / SCALE, zero, zero],
            [zero, zero, zero, one * SCALE],
        ]
    )
    two = np.zeros_like(one)
    two[:half, :half] = pass_matrix(half).T
    w2 = np.kron(np.diag([1 / SCALE, 1 / SCALE, SCALE, SCALE]), two)
    anywhere = pl.BlockSpec(memory_space=pl.ANY)
    smem = pl.BlockSpec(memory_space=pltpu.SMEM)
    vmem = pl.BlockSpec(memory_space=pltpu.VMEM)
    old = [] if before is None else [before]
    return pl.pallas_call(
        functools.partial(fine_kernel, first=first),
        in_specs=[smem, smem, vmem, vmem, vmem] + [anywhere] * len(old),
        out_specs=[anywhere, smem],
        out_shape=[
            jax.ShapeDtypeStruct((slots, edge, tiles * 128), F32),
            jax.ShapeDtypeStruct((1,), jnp.int32),
        ],
        scratch_shapes=[
            pltpu.VMEM((count * pairs * edge, 768), BF16),
            pltpu.VMEM((2, count * pairs * edge, 128), F32),
            pltpu.VMEM((16 * half, 128), F32),
            pltpu.VMEM((count * 8 * half, 768), BF16),
            pltpu.VMEM((2, count * 8 * half, 128), F32),
            pltpu.VMEM((count, edge, tiles * 128), F32),
            pltpu.SemaphoreType.DMA((count,)),
        ],
        input_output_aliases={5: 0} if old else {},
        compiler_params=pltpu.CompilerParams(vmem_limit_bytes=VMEM_LIMIT),
        cost_estimate=pl.CostEstimate(
            flops=6 * count * edge * tiles * 128 * 256, bytes_accessed=2 * count * MIB, transcendentals=0
        ),
        name="fine",
    )(owner_counts, token, held, stacked(w1), stacked(w2), *old)


def coarse_kernel(
    index_ref,
    piece_ref,
    wx_ref,
    wzh_ref,
    wzl_ref,
    wyh_ref,
    wyl_ref,
    w23h_ref,
    w23l_ref,
    wx2_ref,
    wx3_ref,
    fine_ref,
    out_ref,
    block_ref,
    corner_ref,
    corner_sem,
    out_sem,
):
    slots = corner_ref.shape[0]
    lane = lax.broadcasted_iota(jnp.int32, (16, 128), 1)

    def window(s):
        return out_ref.at[s, pl.ds(0, 16), pl.ds(0, 1024)]

    def piece(i):
        return jnp.concatenate([piece_ref[pl.ds(16 * h + i, 16, stride=32), :] for h in range(2)], 1)

    for s in range(slots):
        pltpu.make_async_copy(window(s), corner_ref.at[s], corner_sem.at[s]).start()

    first = [
        [
            times_left(wx_ref[...], jnp.concatenate([piece(o * 8 + 2 * q), piece(o * 8 + 2 * q + 1)], 0))
            for q in range(4)
        ]
        for o in range(2)
    ]
    stacked = []
    for o in range(2):
        for cy in range(2):
            for yh in range(2):
                part = slice(yh * 128, yh * 128 + 128)
                stacked.append(jnp.concatenate([first[o][cy][:, part], first[o][2 + cy][:, part]], 1))
    lifted = times(jnp.concatenate(stacked, 0), wzh_ref[...], wzl_ref[...])
    stacked = []
    for o in range(2):
        for tz in range(2):
            stacked.append(
                jnp.concatenate(
                    [lifted[(o * 4 + u) * 32 : (o * 4 + u + 1) * 32, tz * 128 : tz * 128 + 128] for u in range(4)],
                    1,
                )
            )
    lifted = times(jnp.concatenate(stacked, 0), wyh_ref[...], wyl_ref[...])
    corner = []
    for o in range(2):
        for tz in range(2):
            for ty in range(2):
                for tx in range(2):
                    at = (o * 2 + tz) * 32 + tx * 16
                    value = lifted[at : at + 16, ty * 256 : ty * 256 + 256]
                    if tx + ty + tz == 0:
                        corner.append(value)
                    else:
                        block_ref[o * 8 + tx + 2 * ty + 4 * tz] = value
    both = times(jnp.concatenate(corner, 0), w23h_ref[...], w23l_ref[...])
    depth = lax.broadcasted_iota(jnp.int32, (16, 128), 0)
    small = (depth < 8) & ((lane & 15) < 8)
    for o in range(2):
        mine = both[o * 16 : o * 16 + 16]
        second = times_left(wx2_ref[...], mine[:, :256])
        third = times_left(wx3_ref[...], mine[:, 256:])
        block_ref[o * 8] = jnp.concatenate(
            [jnp.where(small, third, second[:, :128]), second[:, 128:]], 1
        )

    for s in range(slots):
        pltpu.make_async_copy(window(s), corner_ref.at[s], corner_sem.at[s]).wait()
    for s in range(slots):

        @pl.when(s < index_ref[1])
        def _():
            value = block_ref[index_ref[0] + s]
            for t in range(8):
                tile = value[:, (t // 4) * 128 : (t // 4) * 128 + 128]
                near = pltpu.roll(tile, (128 - 32 * (t % 4)) % 128, 1)
                far = pltpu.roll(tile, (64 - 16 - 32 * (t % 4)) % 128, 1)
                old = corner_ref[s, :, pl.ds(t * 128, 128)]
                new = jnp.where(lane < 16, near, jnp.where((lane >= 64) & (lane < 80), far, old))
                corner_ref[s, :, pl.ds(t * 128, 128)] = new
            pltpu.make_async_copy(corner_ref.at[s], window(s), out_sem.at[s]).start()

    for s in range(slots):

        @pl.when(s < index_ref[1])
        def _():
            pltpu.make_async_copy(corner_ref.at[s], window(s), out_sem.at[s]).wait()


def coarse_call(index, pieces, fine):
    slots, edge, plane = fine.shape
    m32, m16, m8 = pass_matrix(32), pass_matrix(16), pass_matrix(8)
    deep = np.zeros((16, 16))
    deep[:8] = m8 @ m16[:8]
    eye8, eye16 = np.eye(8), np.eye(16)
    wz = np.zeros((256, 256))
    for cz in range(2):
        for tz in range(2):
            wz[cz * 128 : cz * 128 + 128, tz * 128 : tz * 128 + 128] = np.kron(
                eye8, m32[tz * 16 : tz * 16 + 16, cz * 16 : cz * 16 + 16].T
            )
    w23 = np.concatenate([np.kron(m16.T, m16.T), np.kron(deep.T, deep.T)[:, :128]], 1)
    weights = [
        left_terms(m32),
        *two_terms(wz),
        *two_terms(np.kron(m32.T, eye16)),
        *two_terms(w23),
        left_terms(m16),
        left_terms(deep),
    ]
    anywhere = pl.BlockSpec(memory_space=pl.ANY)
    vmem = pl.BlockSpec(memory_space=pltpu.VMEM)
    return pl.pallas_call(
        coarse_kernel,
        in_specs=[pl.BlockSpec(memory_space=pltpu.SMEM), vmem] + [vmem] * len(weights) + [anywhere],
        out_specs=anywhere,
        out_shape=jax.ShapeDtypeStruct(fine.shape, F32),
        scratch_shapes=[
            pltpu.VMEM((16, 16, 256), F32),
            pltpu.VMEM((slots, 16, 1024), F32),
            pltpu.SemaphoreType.DMA((slots,)),
            pltpu.SemaphoreType.DMA((slots,)),
        ],
        input_output_aliases={2 + len(weights): 0},
        compiler_params=pltpu.CompilerParams(vmem_limit_bytes=VMEM_SMALL),
        name="coarse",
    )(index, pieces.reshape(-1, 128), *weights, fine)


def exchange(lowpass, slots, token):
    me = lax.axis_index(AXES)
    devices = lax.axis_size(AXES)
    if devices == lowpass.shape[0]:
        got = lax.all_to_all(lowpass, AXES, 0, 0, tiled=True)
        sent, index = route_call(me.reshape(1), got, token, slots)
        return lax.all_to_all(sent, AXES, 0, 0, tiled=True), index
    every = lax.all_gather(lowpass, AXES, axis=0)
    counts = every[:, 0, 7, 0].astype(jnp.int32)
    starts = jnp.cumsum(counts) - counts
    blocks = starts[me] // 8 * 8 + jnp.arange(16, dtype=jnp.int32)
    owners = jnp.sum((starts[None, :] <= blocks[:, None]).astype(jnp.int32), axis=1) - 1
    place = jnp.minimum(blocks - starts[owners], slots - 1)
    pieces = jnp.transpose(every[owners, :, place], (1, 0, 2))
    return pieces, jnp.stack([starts[me] % 8, counts[me]])


def per_device(density, owner_counts):
    slots = density.shape[0]
    early = slots // 3
    lowpass, held = lowpass_call(owner_counts, density)
    fine, token = fine_call(owner_counts, owner_counts, held, 0, early)
    pieces, index = exchange(lowpass, slots, token)
    fine, _ = fine_call(owner_counts, index, held, early, slots, fine)
    return coarse_call(index, pieces, fine)


def solution(mesh):
    in_specs = (P(AXES, None, None), P(AXES))
    out_specs = P(AXES, None, None)
    return jax.shard_map(per_device, mesh=mesh, in_specs=in_specs, out_specs=out_specs, check_vma=False)
```

```python
import functools

import jax
import jax.numpy as jnp
import numpy as np
from jax import lax
from jax.experimental import pallas as pl
from jax.experimental.pallas import tpu as pltpu
from jax.sharding import PartitionSpec as P

ALPHA = -1.586134342059924
BETA = -0.052980118572961
GAMMA = 0.882911075530934
DELTA = 0.443506852043971
SCALE = 1.230174104914001
SQUARE = SCALE * SCALE
F32 = jnp.float32
BF16 = jnp.bfloat16
AXES = ("node", "dev")
MIB = 1 << 20
VMEM_LIMIT = 48 * MIB
VMEM_SMALL = 16 * MIB
VMEM_LARGE = 56 * MIB


def pass_matrix(n):
    low, high = np.eye(n)[0::2], np.eye(n)[1::2]

    def after(v):
        return np.concatenate([v[1:], v[-1:]], 0)

    def before(v):
        return np.concatenate([v[:1], v[:-1]], 0)

    high = high + ALPHA * (low + after(low))
    low = low + BETA * (before(high) + high)
    high = high + GAMMA * (low + after(low))
    low = low + DELTA * (before(high) + high)
    return np.concatenate([low / SCALE, high * SCALE], 0)


def two_terms(matrix):
    matrix = np.asarray(matrix, np.float32)
    first = matrix.astype(BF16)
    return first, (matrix - first.astype(np.float32)).astype(BF16)


def left_terms(matrix):
    first, second = two_terms(matrix)
    return np.concatenate([first, second, first], 1)


def split(value):
    first = value.astype(BF16)
    return first, (value - first.astype(F32)).astype(BF16)


def dot(left, right):
    return jnp.dot(left, right, preferred_element_type=F32)


def times(value, first, second):
    high, low = split(value)
    both = dot(jnp.concatenate([high, low], 0), first)
    count = value.shape[0]
    return both[:count] + both[count:] + dot(high, second)


def times_left(terms, value):
    high, low = split(value)
    return dot(terms, jnp.concatenate([high, high, low], 0))


def split_rows(rows):
    return [split(jnp.concatenate(rows[m : m + 2], 0)) for m in range(0, len(rows), 2)]


def start_tiles(src_ref, dst_ref, sems):
    for t in range(dst_ref.shape[2]):
        pltpu.make_async_copy(
            src_ref.at[:, :, pl.ds(t * 128, 128)], dst_ref.at[:, :, t, :], sems.at[t // 8]
        ).start()


def wait_tiles(dst_ref, sems, group):
    part = dst_ref.at[:, :, pl.ds(8 * group, 8), :]
    pltpu.make_async_copy(part, part, sems.at[group]).wait()


def lowpass_kernel(
    count_ref, x_any, wz_any, wyh_any, wyl_any, out_ref, token_ref, x_ref, wz_ref, wyh_ref, wyl_ref, l_ref, z_ref, sems, w_sems
):
    slots, edge = x_any.shape[:2]
    quarter = edge // 4
    rows_all = slots * 8 * quarter
    token_ref[0] = count_ref[0]
    start_tiles(x_any, x_ref, sems)
    weights = [
        pltpu.make_async_copy(src, dst, w_sems.at[i])
        for i, (src, dst) in enumerate(((wz_any, wz_ref), (wyh_any, wyh_ref), (wyl_any, wyl_ref)))
    ]
    for copy in weights:
        copy.start()
    for g in range(4):
        wait_tiles(x_ref, sems, g)

        @pl.loop(0, slots)
        def _(s):
            rows = [x_ref[s, x, pl.ds(8 * g, 8), :] for x in range(edge)]
            rows, _ = lift(rows[0::2], rows[1::2], edge // 2, False, False)
            rows, _ = lift(rows[0::2], rows[1::2], quarter, False, False)
            for m, (high, low) in enumerate(split_rows(rows)):
                at = pl.multiple_of(s * 8 * quarter + 16 * m, 16)
                cols = pl.ds((g // 2) * 128, 128)
                l_ref[g % 2, pl.ds(at, 16), cols] = high
                l_ref[g % 2, pl.ds(rows_all + at, 16), cols] = low

    for copy in weights:
        copy.wait()
    made = dot(l_ref[0], wz_ref[0]) + dot(l_ref[1], wz_ref[1])
    z_ref[...] = (made[:rows_all, :128] + made[rows_all:, :128]) + made[:rows_all, 128:]
    wide = jnp.concatenate([z_ref[pl.ds(i, slots * quarter, stride=8), :] for i in range(8)], 1)
    made = times(wide, wyh_ref[...], wyl_ref[...])
    out_ref[...] = jnp.full(out_ref.shape, count_ref[0].astype(F32))
    for slot in range(slots):
        for h in range(2):
            out_ref[pl.ds(8 * h + slot, quarter, stride=16), :] = made[
                slot * quarter : (slot + 1) * quarter, h * 128 : h * 128 + 128
            ]


def stacked(matrix):
    first, second = two_terms(matrix)
    return np.concatenate([first, first, second], 0)


def lowpass_call(owner_counts, density):
    slots, edge, plane = density.shape
    quarter = edge // 4
    two_levels = pass_matrix(edge // 2)[:quarter] @ pass_matrix(edge)[: edge // 2]
    wide = np.kron(np.eye(8), two_levels.T)
    wz = np.stack([np.concatenate(two_terms(w), 1) for w in (wide[:256], wide[256:])])
    i, gp, q, p = np.meshgrid(np.arange(8), np.arange(2), np.arange(2), np.arange(2), indexing="ij")
    entry = (2 * (8 * gp + i) + p + 32 * q).reshape(-1)
    wy = np.kron(two_levels.T[entry] / SQUARE, np.eye(quarter))
    wyh, wyl = two_terms(wy)
    anywhere = pl.BlockSpec(memory_space=pl.ANY)
    vmem = pl.BlockSpec(memory_space=pltpu.VMEM)
    rows_all = slots * 8 * quarter
    pieces, token = pl.pallas_call(
        lowpass_kernel,
        in_specs=[pl.BlockSpec(memory_space=pltpu.SMEM)] + [anywhere] * 4,
        out_specs=[vmem, pl.BlockSpec(memory_space=pltpu.SMEM)],
        out_shape=[
            jax.ShapeDtypeStruct((16 * quarter, 128), F32),
            jax.ShapeDtypeStruct((1,), jnp.int32),
        ],
        scratch_shapes=[
            pltpu.VMEM((slots, edge, plane // 128, 128), F32),
            pltpu.VMEM(wz.shape, BF16),
            pltpu.VMEM(wyh.shape, BF16),
            pltpu.VMEM(wyl.shape, BF16),
            pltpu.VMEM((2, 2 * rows_all, 256), BF16),
            pltpu.VMEM((rows_all, 128), F32),
            pltpu.SemaphoreType.DMA((4,)),
            pltpu.SemaphoreType.DMA((3,)),
        ],
        compiler_params=pltpu.CompilerParams(vmem_limit_bytes=VMEM_LARGE),
        name="lowpass",
    )(owner_counts, density, wz, wyh, wyl)
    return pieces.reshape(2 * quarter, 8, 128), token


def route_kernel(me_ref, got_any, _, send_ref, index_ref, got_ref, order_ref, count_ref, sems):
    devices = got_ref.shape[0]
    copies = [
        pltpu.make_async_copy(got_any.at[:, 7, :], count_ref, sems.at[0]),
        pltpu.make_async_copy(got_any, got_ref, sems.at[1]),
    ]
    for copy in copies:
        copy.start()
    order_ref[...] = jnp.zeros_like(order_ref)
    for copy in copies:
        copy.wait()
    start, my_start, my_count = 0, 0, 0
    starts = []
    for d in range(devices):
        count = count_ref[d, 0].astype(jnp.int32)
        starts.append(start)
        my_start = jnp.where(me_ref[0] == d, start, my_start)
        my_count = jnp.where(me_ref[0] == d, count, my_count)
        order_ref[pl.ds(start, 8), :] = got_ref[d]
        start = start + count
    for d in range(devices):
        at = pl.multiple_of(starts[d] // 8 * 8, 8) if d else 0
        send_ref[d] = order_ref[pl.ds(at, 16), :]
    index_ref[0] = my_start % 8
    index_ref[1] = my_count


def route_call(me, got, token, slots):
    devices = got.shape[0]
    return pl.pallas_call(
        route_kernel,
        in_specs=[
            pl.BlockSpec(memory_space=pltpu.SMEM),
            pl.BlockSpec(memory_space=pl.ANY),
            pl.BlockSpec(memory_space=pltpu.SMEM),
        ],
        out_specs=[pl.BlockSpec(memory_space=pltpu.VMEM), pl.BlockSpec(memory_space=pltpu.SMEM)],
        out_shape=[
            jax.ShapeDtypeStruct((devices, 16, 128), F32),
            jax.ShapeDtypeStruct((2,), jnp.int32),
        ],
        scratch_shapes=[
            pltpu.VMEM(got.shape, F32),
            pltpu.VMEM((devices * slots + 16, 128), F32),
            pltpu.SMEM((devices, 128), F32),
            pltpu.SemaphoreType.DMA((2,)),
        ],
        compiler_params=pltpu.CompilerParams(vmem_limit_bytes=VMEM_SMALL),
        name="route",
    )(me, got, token)


def lift(low, high, n, halo, scaled):
    up = SQUARE if scaled else 1.0
    at = 2 if halo else 0
    first, second, third, fourth = ({} for _ in range(4))

    def get(values, i, is_low):
        if halo:
            return values[i]
        return values[min(i, n - 1)] if is_low else values[max(i, 0)]

    lows = {i - at: low[i] for i in range(len(low))}
    highs = {i - at: high[i] for i in range(len(high))}

    def make_first(i):
        first[i] = highs[i] + (ALPHA * up) * (lows[i] + get(lows, i + 1, True))

    def make_second(i):
        second[i] = lows[i] + (BETA / up) * (get(first, i - 1, False) + first[i])

    def make_third(i):
        third[i] = first[i] + (GAMMA * up) * (second[i] + get(second, i + 1, True))

    def make_fourth(i):
        fourth[i] = second[i] + (DELTA / up) * (get(third, i - 1, False) + third[i])

    if halo:
        for i in range(-2, n + 1):
            make_first(i)
            if i >= -1:
                make_second(i)
            if i >= 0:
                make_third(i - 1)
            if i >= 1:
                make_fourth(i - 1)
    else:
        for i in range(n):
            make_first(i)
            make_second(i)
            if i >= 1:
                make_third(i - 1)
                make_fourth(i - 1)
        make_third(n - 1)
        make_fourth(n - 1)
    return [fourth[i] for i in range(n)], [third[i] for i in range(n)]


def fine_kernel(count_ref, _, x_any, w1_ref, w2_ref, *refs, first):
    out_ref, token_ref, x_ref, l_ref, y_ref, c_ref, m_ref, d_ref, o_ref, x_sems, sems = refs[-11:]
    slots, edge = o_ref.shape[:2]
    tiles = x_ref.shape[2]
    pairs = tiles // 2
    half = edge // 2
    block = pairs * edge
    corner = 8 * half
    live = jnp.clip(count_ref[0] - first, 0, slots)
    lane = lax.broadcasted_iota(jnp.int32, (8, 128), 1)
    front = lane < 64
    inner = (lane & 63) < half
    token_ref[0] = live
    start_tiles(x_any.at[pl.ds(first, slots)], x_ref, x_sems)

    def turn(value):
        return pltpu.roll(value, 64, 1)

    def with_halo(low, high):
        def left(values, i):
            return jnp.where(front, values[i[0]], turn(values[i[1]]))

        def right(values, i):
            return jnp.where(front, turn(values[i[0]]), values[i[1]])

        low_all = [left(low, (2, -2)), left(low, (1, -1))] + low + [right(low, (0, -1)), right(low, (1, -2))]
        high_all = [left(high, (1, -2)), left(high, (0, -1))] + high + [right(high, (0, -2))]
        return low_all, high_all

    def scaled_rows(rows):
        low, high = lift(rows[0::2], rows[1::2], len(rows) // 2, False, False)
        return [v * (1.0 / SCALE) for v in low] + [v * SCALE for v in high]

    def store_terms(ref, row, col, rows):
        for m, (high, low) in enumerate(split_rows(rows)):
            place = pl.ds(pl.multiple_of(row + 16 * m, 16), 16)
            ref[place, pl.ds(col, 128)] = high
            ref[place, pl.ds(256 + col, 128)] = low
            ref[place, pl.ds(512 + col, 128)] = high

    def write(s):
        return pltpu.make_async_copy(o_ref.at[s], out_ref.at[first + s], sems.at[s])

    @pl.loop(live, slots)
    def _(s):
        o_ref[s] = jnp.zeros(o_ref.shape[1:], F32)
        write(s).start()

    for g in range(4):
        wait_tiles(x_ref, x_sems, g)

        @pl.loop(0, live)
        def _(s):
            rows = scaled_rows([x_ref[s, i, pl.ds(8 * g, 8), :] for i in range(edge)])
            store_terms(l_ref, s * block + (g % 2) * 8 * edge, (g // 2) * 128, rows)

    lifted = dot(l_ref[...], w1_ref[...])
    y_ref[0] = lifted[:, :128]
    y_ref[1] = lifted[:, 128:]

    @pl.loop(0, live)
    def _(s):
        for r in range(edge // 8):
            rows = pl.ds(8 * r, 8)

            def tile(part, j):
                return y_ref[part, pl.ds(s * block + (j // 8) * 8 * edge + 64 * r + j % 8, 8, stride=8), :]

            low = [tile(0, j) for j in range(pairs)]
            high = [tile(1, j) for j in range(pairs)]
            low, high = lift(*with_halo(low, high), pairs, True, True)
            for part, values in enumerate((low, high)):
                for t in range(pairs // 2):
                    a, b = values[2 * t], values[2 * t + 1]
                    at = part * pairs + t
                    o_ref[s, rows, pl.ds(at * 128, 128)] = jnp.where(front, a, turn(b))
                    o_ref[s, rows, pl.ds((at + pairs // 2) * 128, 128)] = jnp.where(front, turn(a), b)
            if r < half // 8:
                low, high = lift(*with_halo(low[0::2], low[1::2]), 8, True, False)
                for i in range(8):
                    c_ref[pl.ds(64 * r + i, 8, stride=8), :] = low[i]
                    c_ref[pl.ds(corner + 64 * r + i, 8, stride=8), :] = high[i]
        for u in range(2):
            rows = scaled_rows([c_ref[pl.ds(u * corner + 8 * i, 8), :] for i in range(half)])
            store_terms(m_ref, s * corner, u * 128, rows)

    lifted = dot(m_ref[...], w2_ref[...])
    d_ref[0] = lifted[:, :128]
    d_ref[1] = lifted[:, 128:]

    @pl.loop(0, live)
    def _(s):
        for u in range(2):
            for t in range(4):
                for r in range(half // 8):
                    base = s * corner + 64 * r + 2 * t
                    a = d_ref[u, pl.ds(base, 8, stride=8), :]
                    b = d_ref[u, pl.ds(base + 1, 8, stride=8), :]
                    for at, value in (
                        (u * 8 + t, jnp.where(front, a, turn(b))),
                        (u * 8 + 4 + t, jnp.where(front, turn(a), b)),
                    ):
                        rows, cols = pl.ds(8 * r, 8), pl.ds(at * 128, 128)
                        o_ref[s, rows, cols] = jnp.where(inner, value, o_ref[s, rows, cols])
        write(s).start()

    for s in range(slots):
        write(s).wait()


def fine_call(owner_counts, token, density, first, last, before=None):
    slots, edge, plane = density.shape
    tiles = plane // 128
    half = edge // 2
    pairs = tiles // 2
    count = last - first
    one = pass_matrix(edge).T
    zero = np.zeros_like(one)
    w1 = np.block(
        [
            [one / SCALE, zero, zero, zero],
            [zero, zero, one * SCALE, zero],
            [zero, one / SCALE, zero, zero],
            [zero, zero, zero, one * SCALE],
        ]
    )
    two = np.zeros_like(one)
    two[:half, :half] = pass_matrix(half).T
    w2 = np.kron(np.diag([1 / SCALE, 1 / SCALE, SCALE, SCALE]), two)
    anywhere = pl.BlockSpec(memory_space=pl.ANY)
    smem = pl.BlockSpec(memory_space=pltpu.SMEM)
    vmem = pl.BlockSpec(memory_space=pltpu.VMEM)
    old = [] if before is None else [before]
    return pl.pallas_call(
        functools.partial(fine_kernel, first=first),
        in_specs=[smem, smem, anywhere, vmem, vmem] + [anywhere] * len(old),
        out_specs=[anywhere, smem],
        out_shape=[
            jax.ShapeDtypeStruct(density.shape, F32),
            jax.ShapeDtypeStruct((1,), jnp.int32),
        ],
        scratch_shapes=[
            pltpu.VMEM((count, edge, tiles, 128), F32),
            pltpu.VMEM((count * pairs * edge, 768), BF16),
            pltpu.VMEM((2, count * pairs * edge, 128), F32),
            pltpu.VMEM((16 * half, 128), F32),
            pltpu.VMEM((count * 8 * half, 768), BF16),
            pltpu.VMEM((2, count * 8 * half, 128), F32),
            pltpu.VMEM((count, edge, tiles * 128), F32),
            pltpu.SemaphoreType.DMA((4,)),
            pltpu.SemaphoreType.DMA((count,)),
        ],
        input_output_aliases={5: 0} if old else {},
        compiler_params=pltpu.CompilerParams(vmem_limit_bytes=VMEM_LIMIT),
        cost_estimate=pl.CostEstimate(
            flops=6 * count * edge * tiles * 128 * 256, bytes_accessed=2 * count * MIB, transcendentals=0
        ),
        name="fine",
    )(owner_counts, token, density, stacked(w1), stacked(w2), *old)


def coarse_kernel(
    index_ref,
    piece_ref,
    wx_ref,
    wzh_ref,
    wzl_ref,
    wyh_ref,
    wyl_ref,
    w23h_ref,
    w23l_ref,
    wx2_ref,
    wx3_ref,
    fine_ref,
    out_ref,
    block_ref,
    corner_ref,
    corner_sem,
    out_sem,
):
    slots = corner_ref.shape[0]
    lane = lax.broadcasted_iota(jnp.int32, (16, 128), 1)

    def window(s):
        return out_ref.at[s, pl.ds(0, 16), pl.ds(0, 1024)]

    def piece(i):
        return jnp.concatenate([piece_ref[pl.ds(16 * h + i, 16, stride=32), :] for h in range(2)], 1)

    for s in range(slots):
        pltpu.make_async_copy(window(s), corner_ref.at[s], corner_sem.at[s]).start()

    first = [
        [
            times_left(wx_ref[...], jnp.concatenate([piece(o * 8 + 2 * q), piece(o * 8 + 2 * q + 1)], 0))
            for q in range(4)
        ]
        for o in range(2)
    ]
    stacked = []
    for o in range(2):
        for cy in range(2):
            for yh in range(2):
                part = slice(yh * 128, yh * 128 + 128)
                stacked.append(jnp.concatenate([first[o][cy][:, part], first[o][2 + cy][:, part]], 1))
    lifted = times(jnp.concatenate(stacked, 0), wzh_ref[...], wzl_ref[...])
    stacked = []
    for o in range(2):
        for tz in range(2):
            stacked.append(
                jnp.concatenate(
                    [lifted[(o * 4 + u) * 32 : (o * 4 + u + 1) * 32, tz * 128 : tz * 128 + 128] for u in range(4)],
                    1,
                )
            )
    lifted = times(jnp.concatenate(stacked, 0), wyh_ref[...], wyl_ref[...])
    corner = []
    for o in range(2):
        for tz in range(2):
            for ty in range(2):
                for tx in range(2):
                    at = (o * 2 + tz) * 32 + tx * 16
                    value = lifted[at : at + 16, ty * 256 : ty * 256 + 256]
                    if tx + ty + tz == 0:
                        corner.append(value)
                    else:
                        block_ref[o * 8 + tx + 2 * ty + 4 * tz] = value
    both = times(jnp.concatenate(corner, 0), w23h_ref[...], w23l_ref[...])
    depth = lax.broadcasted_iota(jnp.int32, (16, 128), 0)
    small = (depth < 8) & ((lane & 15) < 8)
    for o in range(2):
        mine = both[o * 16 : o * 16 + 16]
        second = times_left(wx2_ref[...], mine[:, :256])
        third = times_left(wx3_ref[...], mine[:, 256:])
        block_ref[o * 8] = jnp.concatenate(
            [jnp.where(small, third, second[:, :128]), second[:, 128:]], 1
        )

    for s in range(slots):
        pltpu.make_async_copy(window(s), corner_ref.at[s], corner_sem.at[s]).wait()
    for s in range(slots):

        @pl.when(s < index_ref[1])
        def _():
            value = block_ref[index_ref[0] + s]
            for t in range(8):
                tile = value[:, (t // 4) * 128 : (t // 4) * 128 + 128]
                near = pltpu.roll(tile, (128 - 32 * (t % 4)) % 128, 1)
                far = pltpu.roll(tile, (64 - 16 - 32 * (t % 4)) % 128, 1)
                old = corner_ref[s, :, pl.ds(t * 128, 128)]
                new = jnp.where(lane < 16, near, jnp.where((lane >= 64) & (lane < 80), far, old))
                corner_ref[s, :, pl.ds(t * 128, 128)] = new
            pltpu.make_async_copy(corner_ref.at[s], window(s), out_sem.at[s]).start()

    for s in range(slots):

        @pl.when(s < index_ref[1])
        def _():
            pltpu.make_async_copy(corner_ref.at[s], window(s), out_sem.at[s]).wait()


def coarse_call(index, pieces, fine):
    slots, edge, plane = fine.shape
    m32, m16, m8 = pass_matrix(32), pass_matrix(16), pass_matrix(8)
    deep = np.zeros((16, 16))
    deep[:8] = m8 @ m16[:8]
    eye8, eye16 = np.eye(8), np.eye(16)
    wz = np.zeros((256, 256))
    for cz in range(2):
        for tz in range(2):
            wz[cz * 128 : cz * 128 + 128, tz * 128 : tz * 128 + 128] = np.kron(
                eye8, m32[tz * 16 : tz * 16 + 16, cz * 16 : cz * 16 + 16].T
            )
    w23 = np.concatenate([np.kron(m16.T, m16.T), np.kron(deep.T, deep.T)[:, :128]], 1)
    weights = [
        left_terms(m32),
        *two_terms(wz),
        *two_terms(np.kron(m32.T, eye16)),
        *two_terms(w23),
        left_terms(m16),
        left_terms(deep),
    ]
    anywhere = pl.BlockSpec(memory_space=pl.ANY)
    vmem = pl.BlockSpec(memory_space=pltpu.VMEM)
    return pl.pallas_call(
        coarse_kernel,
        in_specs=[pl.BlockSpec(memory_space=pltpu.SMEM), vmem] + [vmem] * len(weights) + [anywhere],
        out_specs=anywhere,
        out_shape=jax.ShapeDtypeStruct(fine.shape, F32),
        scratch_shapes=[
            pltpu.VMEM((16, 16, 256), F32),
            pltpu.VMEM((slots, 16, 1024), F32),
            pltpu.SemaphoreType.DMA((slots,)),
            pltpu.SemaphoreType.DMA((slots,)),
        ],
        input_output_aliases={2 + len(weights): 0},
        compiler_params=pltpu.CompilerParams(vmem_limit_bytes=VMEM_SMALL),
        name="coarse",
    )(index, pieces.reshape(-1, 128), *weights, fine)


def exchange(lowpass, slots, token):
    me = lax.axis_index(AXES)
    devices = lax.axis_size(AXES)
    if devices == lowpass.shape[0]:
        got = lax.all_to_all(lowpass, AXES, 0, 0, tiled=True)
        sent, index = route_call(me.reshape(1), got, token, slots)
        return lax.all_to_all(sent, AXES, 0, 0, tiled=True), index
    every = lax.all_gather(lowpass, AXES, axis=0)
    counts = every[:, 0, 7, 0].astype(jnp.int32)
    starts = jnp.cumsum(counts) - counts
    blocks = starts[me] // 8 * 8 + jnp.arange(16, dtype=jnp.int32)
    owners = jnp.sum((starts[None, :] <= blocks[:, None]).astype(jnp.int32), axis=1) - 1
    place = jnp.minimum(blocks - starts[owners], slots - 1)
    pieces = jnp.transpose(every[owners, :, place], (1, 0, 2))
    return pieces, jnp.stack([starts[me] % 8, counts[me]])


def per_device(density, owner_counts):
    slots = density.shape[0]
    early = slots // 3
    lowpass, token = lowpass_call(owner_counts, density)
    fine, token = fine_call(owner_counts, token, density, 0, early)
    pieces, index = exchange(lowpass, slots, token)
    fine, _ = fine_call(owner_counts, index, density, early, slots, fine)
    return coarse_call(index, pieces, fine)


def solution(mesh):
    in_specs = (P(AXES, None, None), P(AXES))
    out_specs = P(AXES, None, None)
    return jax.shard_map(per_device, mesh=mesh, in_specs=in_specs, out_specs=out_specs, check_vma=False)
```

```python
import functools

import jax
import jax.numpy as jnp
import numpy as np
from jax import lax
from jax.experimental import pallas as pl
from jax.experimental.pallas import tpu as pltpu
from jax.sharding import PartitionSpec as P

ALPHA = -1.586134342059924
BETA = -0.052980118572961
GAMMA = 0.882911075530934
DELTA = 0.443506852043971
SCALE = 1.230174104914001
SQUARE = SCALE * SCALE
F32 = jnp.float32
BF16 = jnp.bfloat16
AXES = ("node", "dev")
MIB = 1 << 20
VMEM_LIMIT = 48 * MIB
VMEM_SMALL = 16 * MIB
VMEM_LARGE = 56 * MIB


def pass_matrix(n):
    low, high = np.eye(n)[0::2], np.eye(n)[1::2]

    def after(v):
        return np.concatenate([v[1:], v[-1:]], 0)

    def before(v):
        return np.concatenate([v[:1], v[:-1]], 0)

    high = high + ALPHA * (low + after(low))
    low = low + BETA * (before(high) + high)
    high = high + GAMMA * (low + after(low))
    low = low + DELTA * (before(high) + high)
    return np.concatenate([low / SCALE, high * SCALE], 0)


def two_terms(matrix):
    matrix = np.asarray(matrix, np.float32)
    first = matrix.astype(BF16)
    return first, (matrix - first.astype(np.float32)).astype(BF16)


def left_terms(matrix):
    first, second = two_terms(matrix)
    return np.concatenate([first, second, first], 1)


def split(value):
    first = value.astype(BF16)
    return first, (value - first.astype(F32)).astype(BF16)


def dot(left, right):
    return jnp.dot(left, right, preferred_element_type=F32)


def times(value, first, second):
    high, low = split(value)
    both = dot(jnp.concatenate([high, low], 0), first)
    count = value.shape[0]
    return both[:count] + both[count:] + dot(high, second)


def times_left(terms, value):
    high, low = split(value)
    return dot(terms, jnp.concatenate([high, high, low], 0))


def split_rows(rows):
    return [split(jnp.concatenate(rows[m : m + 2], 0)) for m in range(0, len(rows), 2)]


def tile_buffer(tiles, slots, edge):
    return pltpu.VMEM((tiles, slots | 1, edge + 8, 128), F32)


def start_tiles(src_ref, dst_ref, sems):
    slots, edge = src_ref.shape[:2]
    for t in range(dst_ref.shape[0]):
        pltpu.make_async_copy(
            src_ref.at[:, :, pl.ds(t * 128, 128)],
            dst_ref.at[t, pl.ds(0, slots), pl.ds(0, edge), :],
            sems.at[t // 8],
        ).start()


def wait_tiles(src_ref, dst_ref, sems, group):
    slots, edge = src_ref.shape[:2]
    part = dst_ref.at[pl.ds(8 * group, 8), pl.ds(0, slots), pl.ds(0, edge), :]
    pltpu.make_async_copy(part, part, sems.at[group]).wait()


def tile_rows(ref, slot, group, edge):
    tiles, slots, pitch, lanes = ref.shape
    flat = ref.reshape(tiles * slots * pitch, lanes)
    base = 8 * group * slots * pitch + slot * pitch
    return [flat[pl.ds(base + x, 8, stride=slots * pitch), :] for x in range(edge)]


def lowpass_kernel(
    count_ref, x_any, wz_any, wyh_any, wyl_any, out_ref, token_ref, x_ref, wz_ref, wyh_ref, wyl_ref, l_ref, z_ref, sems, w_sems
):
    slots, edge = x_any.shape[:2]
    quarter = edge // 4
    rows_all = slots * 8 * quarter
    token_ref[0] = count_ref[0]
    start_tiles(x_any, x_ref, sems)
    weights = [
        pltpu.make_async_copy(src, dst, w_sems.at[i])
        for i, (src, dst) in enumerate(((wz_any, wz_ref), (wyh_any, wyh_ref), (wyl_any, wyl_ref)))
    ]
    for copy in weights:
        copy.start()
    for g in range(4):
        wait_tiles(x_any, x_ref, sems, g)

        @pl.loop(0, slots)
        def _(s):
            rows = tile_rows(x_ref, s, g, edge)
            rows, _ = lift(rows[0::2], rows[1::2], edge // 2, False, False)
            rows, _ = lift(rows[0::2], rows[1::2], quarter, False, False)
            for m, (high, low) in enumerate(split_rows(rows)):
                at = pl.multiple_of(s * 8 * quarter + 16 * m, 16)
                cols = pl.ds((g // 2) * 128, 128)
                l_ref[g % 2, pl.ds(at, 16), cols] = high
                l_ref[g % 2, pl.ds(rows_all + at, 16), cols] = low

    for copy in weights:
        copy.wait()
    made = dot(l_ref[0], wz_ref[0]) + dot(l_ref[1], wz_ref[1])
    z_ref[...] = (made[:rows_all, :128] + made[rows_all:, :128]) + made[:rows_all, 128:]
    wide = jnp.concatenate([z_ref[pl.ds(i, slots * quarter, stride=8), :] for i in range(8)], 1)
    made = times(wide, wyh_ref[...], wyl_ref[...])
    out_ref[...] = jnp.full(out_ref.shape, count_ref[0].astype(F32))
    for slot in range(slots):
        for h in range(2):
            out_ref[pl.ds(8 * h + slot, quarter, stride=16), :] = made[
                slot * quarter : (slot + 1) * quarter, h * 128 : h * 128 + 128
            ]


def stacked(matrix):
    first, second = two_terms(matrix)
    return np.concatenate([first, first, second], 0)


def lowpass_call(owner_counts, density):
    slots, edge, plane = density.shape
    quarter = edge // 4
    two_levels = pass_matrix(edge // 2)[:quarter] @ pass_matrix(edge)[: edge // 2]
    wide = np.kron(np.eye(8), two_levels.T)
    wz = np.stack([np.concatenate(two_terms(w), 1) for w in (wide[:256], wide[256:])])
    i, gp, q, p = np.meshgrid(np.arange(8), np.arange(2), np.arange(2), np.arange(2), indexing="ij")
    entry = (2 * (8 * gp + i) + p + 32 * q).reshape(-1)
    wy = np.kron(two_levels.T[entry] / SQUARE, np.eye(quarter))
    wyh, wyl = two_terms(wy)
    anywhere = pl.BlockSpec(memory_space=pl.ANY)
    vmem = pl.BlockSpec(memory_space=pltpu.VMEM)
    rows_all = slots * 8 * quarter
    pieces, token = pl.pallas_call(
        lowpass_kernel,
        in_specs=[pl.BlockSpec(memory_space=pltpu.SMEM)] + [anywhere] * 4,
        out_specs=[vmem, pl.BlockSpec(memory_space=pltpu.SMEM)],
        out_shape=[
            jax.ShapeDtypeStruct((16 * quarter, 128), F32),
            jax.ShapeDtypeStruct((1,), jnp.int32),
        ],
        scratch_shapes=[
            tile_buffer(plane // 128, slots, edge),
            pltpu.VMEM(wz.shape, BF16),
            pltpu.VMEM(wyh.shape, BF16),
            pltpu.VMEM(wyl.shape, BF16),
            pltpu.VMEM((2, 2 * rows_all, 256), BF16),
            pltpu.VMEM((rows_all, 128), F32),
            pltpu.SemaphoreType.DMA((4,)),
            pltpu.SemaphoreType.DMA((3,)),
        ],
        compiler_params=pltpu.CompilerParams(vmem_limit_bytes=VMEM_LARGE),
        name="lowpass",
    )(owner_counts, density, wz, wyh, wyl)
    return pieces.reshape(2 * quarter, 8, 128), token


def route_kernel(me_ref, got_ref, _, send_ref, index_ref, order_ref, count_ref, sem):
    devices = got_ref.shape[0]
    copy = pltpu.make_async_copy(got_ref.at[:, 7, :], count_ref, sem)
    copy.start()
    order_ref[...] = jnp.zeros_like(order_ref)
    copy.wait()
    start, my_start, my_count = 0, 0, 0
    starts = []
    for d in range(devices):
        count = count_ref[d, 0].astype(jnp.int32)
        starts.append(start)
        my_start = jnp.where(me_ref[0] == d, start, my_start)
        my_count = jnp.where(me_ref[0] == d, count, my_count)
        order_ref[pl.ds(start, 8), :] = got_ref[d]
        start = start + count
    for d in range(devices):
        at = pl.multiple_of(starts[d] // 8 * 8, 8) if d else 0
        send_ref[d] = order_ref[pl.ds(at, 16), :]
    index_ref[0] = my_start % 8
    index_ref[1] = my_count


def route_call(me, got, token, slots):
    devices = got.shape[0]
    return pl.pallas_call(
        route_kernel,
        in_specs=[
            pl.BlockSpec(memory_space=pltpu.SMEM),
            pl.BlockSpec(memory_space=pltpu.VMEM),
            pl.BlockSpec(memory_space=pltpu.SMEM),
        ],
        out_specs=[pl.BlockSpec(memory_space=pltpu.VMEM), pl.BlockSpec(memory_space=pltpu.SMEM)],
        out_shape=[
            jax.ShapeDtypeStruct((devices, 16, 128), F32),
            jax.ShapeDtypeStruct((2,), jnp.int32),
        ],
        scratch_shapes=[
            pltpu.VMEM((devices * slots + 16, 128), F32),
            pltpu.SMEM((devices, 128), F32),
            pltpu.SemaphoreType.DMA,
        ],
        compiler_params=pltpu.CompilerParams(vmem_limit_bytes=VMEM_SMALL),
        name="route",
    )(me, got, token)


def lift(low, high, n, halo, scaled):
    up = SQUARE if scaled else 1.0
    at = 2 if halo else 0
    first, second, third, fourth = ({} for _ in range(4))

    def get(values, i, is_low):
        if halo:
            return values[i]
        return values[min(i, n - 1)] if is_low else values[max(i, 0)]

    lows = {i - at: low[i] for i in range(len(low))}
    highs = {i - at: high[i] for i in range(len(high))}

    def make_first(i):
        first[i] = highs[i] + (ALPHA * up) * (lows[i] + get(lows, i + 1, True))

    def make_second(i):
        second[i] = lows[i] + (BETA / up) * (get(first, i - 1, False) + first[i])

    def make_third(i):
        third[i] = first[i] + (GAMMA * up) * (second[i] + get(second, i + 1, True))

    def make_fourth(i):
        fourth[i] = second[i] + (DELTA / up) * (get(third, i - 1, False) + third[i])

    if halo:
        for i in range(-2, n + 1):
            make_first(i)
            if i >= -1:
                make_second(i)
            if i >= 0:
                make_third(i - 1)
            if i >= 1:
                make_fourth(i - 1)
    else:
        for i in range(n):
            make_first(i)
            make_second(i)
            if i >= 1:
                make_third(i - 1)
                make_fourth(i - 1)
        make_third(n - 1)
        make_fourth(n - 1)
    return [fourth[i] for i in range(n)], [third[i] for i in range(n)]


def fine_kernel(count_ref, _, x_any, w1_ref, w2_ref, *refs, first):
    out_ref, token_ref, x_ref, l_ref, y_ref, c_ref, m_ref, d_ref, o_ref, x_sems, sems = refs[-11:]
    slots, edge = o_ref.shape[:2]
    tiles = x_ref.shape[0]
    pairs = tiles // 2
    half = edge // 2
    block = pairs * edge
    corner = 8 * half
    live = jnp.clip(count_ref[0] - first, 0, slots)
    lane = lax.broadcasted_iota(jnp.int32, (8, 128), 1)
    front = lane < 64
    inner = (lane & 63) < half
    token_ref[0] = live
    x_any = x_any.at[pl.ds(first, slots)]
    start_tiles(x_any, x_ref, x_sems)

    def cross(a, b):
        return pltpu.roll(jnp.where(front, b, a), 64, 1)

    def exchange(a, b):
        crossed = cross(a, b)
        return jnp.where(front, a, crossed), jnp.where(front, crossed, b)

    def with_halo(low, high):
        one, two = cross(low[0], low[-1]), cross(low[1], low[-2])
        low_all = [jnp.where(front, low[2], two), jnp.where(front, low[1], one)] + low
        low_all += [jnp.where(front, one, low[-1]), jnp.where(front, two, low[-2])]
        one, two = cross(high[0], high[-1]), cross(high[1], high[-2])
        high_all = [jnp.where(front, high[1], two), jnp.where(front, high[0], one)] + high
        return low_all, high_all + [jnp.where(front, one, high[-2])]

    def scaled_rows(rows):
        low, high = lift(rows[0::2], rows[1::2], len(rows) // 2, False, False)
        return [v * (1.0 / SCALE) for v in low] + [v * SCALE for v in high]

    def store_terms(ref, row, col, rows):
        for m, (high, low) in enumerate(split_rows(rows)):
            place = pl.ds(pl.multiple_of(row + 16 * m, 16), 16)
            ref[place, pl.ds(col, 128)] = high
            ref[place, pl.ds(256 + col, 128)] = low
            ref[place, pl.ds(512 + col, 128)] = high

    def write(s):
        return pltpu.make_async_copy(o_ref.at[s], out_ref.at[first + s], sems.at[s])

    @pl.loop(live, slots)
    def _(s):
        o_ref[s] = jnp.zeros(o_ref.shape[1:], F32)
        write(s).start()

    for g in range(4):
        wait_tiles(x_any, x_ref, x_sems, g)

        @pl.loop(0, live)
        def _(s):
            rows = scaled_rows(tile_rows(x_ref, s, g, edge))
            store_terms(l_ref, s * block + (g % 2) * 8 * edge, (g // 2) * 128, rows)

    lifted = dot(l_ref[...], w1_ref[...])
    y_ref[0] = lifted[:, :128]
    y_ref[1] = lifted[:, 128:]

    @pl.loop(0, live)
    def _(s):
        for r in range(edge // 8):
            rows = pl.ds(8 * r, 8)

            def tile(part, j):
                return y_ref[part, pl.ds(s * block + (j // 8) * 8 * edge + 64 * r + j % 8, 8, stride=8), :]

            low = [tile(0, j) for j in range(pairs)]
            high = [tile(1, j) for j in range(pairs)]
            low, high = lift(*with_halo(low, high), pairs, True, True)
            for part, values in enumerate((low, high)):
                for t in range(pairs // 2):
                    a, b = exchange(values[2 * t], values[2 * t + 1])
                    at = part * pairs + t
                    o_ref[s, rows, pl.ds(at * 128, 128)] = a
                    o_ref[s, rows, pl.ds((at + pairs // 2) * 128, 128)] = b
            if r < half // 8:
                low, high = lift(*with_halo(low[0::2], low[1::2]), 8, True, False)
                for i in range(8):
                    c_ref[pl.ds(64 * r + i, 8, stride=8), :] = low[i]
                    c_ref[pl.ds(corner + 64 * r + i, 8, stride=8), :] = high[i]
        for u in range(2):
            rows = scaled_rows([c_ref[pl.ds(u * corner + 8 * i, 8), :] for i in range(half)])
            store_terms(m_ref, s * corner, u * 128, rows)

    lifted = dot(m_ref[...], w2_ref[...])
    d_ref[0] = lifted[:, :128]
    d_ref[1] = lifted[:, 128:]

    @pl.loop(0, live)
    def _(s):
        for u in range(2):
            for t in range(4):
                for r in range(half // 8):
                    base = s * corner + 64 * r + 2 * t
                    a = d_ref[u, pl.ds(base, 8, stride=8), :]
                    b = d_ref[u, pl.ds(base + 1, 8, stride=8), :]
                    for at, value in zip((u * 8 + t, u * 8 + 4 + t), exchange(a, b)):
                        rows, cols = pl.ds(8 * r, 8), pl.ds(at * 128, 128)
                        o_ref[s, rows, cols] = jnp.where(inner, value, o_ref[s, rows, cols])
        write(s).start()

    for s in range(slots):
        write(s).wait()


def fine_call(owner_counts, token, density, first, last, before=None):
    slots, edge, plane = density.shape
    tiles = plane // 128
    half = edge // 2
    pairs = tiles // 2
    count = last - first
    one = pass_matrix(edge).T
    zero = np.zeros_like(one)
    w1 = np.block(
        [
            [one / SCALE, zero, zero, zero],
            [zero, zero, one * SCALE, zero],
            [zero, one / SCALE, zero, zero],
            [zero, zero, zero, one * SCALE],
        ]
    )
    two = np.zeros_like(one)
    two[:half, :half] = pass_matrix(half).T
    w2 = np.kron(np.diag([1 / SCALE, 1 / SCALE, SCALE, SCALE]), two)
    anywhere = pl.BlockSpec(memory_space=pl.ANY)
    smem = pl.BlockSpec(memory_space=pltpu.SMEM)
    vmem = pl.BlockSpec(memory_space=pltpu.VMEM)
    old = [] if before is None else [before]
    return pl.pallas_call(
        functools.partial(fine_kernel, first=first),
        in_specs=[smem, smem, anywhere, vmem, vmem] + [anywhere] * len(old),
        out_specs=[anywhere, smem],
        out_shape=[
            jax.ShapeDtypeStruct(density.shape, F32),
            jax.ShapeDtypeStruct((1,), jnp.int32),
        ],
        scratch_shapes=[
            tile_buffer(tiles, count, edge),
            pltpu.VMEM((count * pairs * edge, 768), BF16),
            pltpu.VMEM((2, count * pairs * edge, 128), F32),
            pltpu.VMEM((16 * half, 128), F32),
            pltpu.VMEM((count * 8 * half, 768), BF16),
            pltpu.VMEM((2, count * 8 * half, 128), F32),
            pltpu.VMEM((count, edge, tiles * 128), F32),
            pltpu.SemaphoreType.DMA((4,)),
            pltpu.SemaphoreType.DMA((count,)),
        ],
        input_output_aliases={5: 0} if old else {},
        compiler_params=pltpu.CompilerParams(vmem_limit_bytes=VMEM_LIMIT),
        cost_estimate=pl.CostEstimate(
            flops=6 * count * edge * tiles * 128 * 256, bytes_accessed=2 * count * MIB, transcendentals=0
        ),
        name="fine",
    )(owner_counts, token, density, stacked(w1), stacked(w2), *old)


def coarse_kernel(
    index_ref,
    piece_ref,
    wx_ref,
    wzh_ref,
    wzl_ref,
    wyh_ref,
    wyl_ref,
    w23h_ref,
    w23l_ref,
    wx2_ref,
    wx3_ref,
    fine_ref,
    out_ref,
    block_ref,
    corner_ref,
    corner_sem,
    out_sem,
):
    slots = corner_ref.shape[0]
    lane = lax.broadcasted_iota(jnp.int32, (16, 128), 1)

    def window(s):
        return out_ref.at[s, pl.ds(0, 16), pl.ds(0, 1024)]

    def piece(i):
        return jnp.concatenate([piece_ref[pl.ds(16 * h + i, 16, stride=32), :] for h in range(2)], 1)

    for s in range(slots):
        pltpu.make_async_copy(window(s), corner_ref.at[s], corner_sem.at[s]).start()

    first = [
        [
            times_left(wx_ref[...], jnp.concatenate([piece(o * 8 + 2 * q), piece(o * 8 + 2 * q + 1)], 0))
            for q in range(4)
        ]
        for o in range(2)
    ]
    stacked = []
    for o in range(2):
        for cy in range(2):
            for yh in range(2):
                part = slice(yh * 128, yh * 128 + 128)
                stacked.append(jnp.concatenate([first[o][cy][:, part], first[o][2 + cy][:, part]], 1))
    lifted = times(jnp.concatenate(stacked, 0), wzh_ref[...], wzl_ref[...])
    stacked = []
    for o in range(2):
        for tz in range(2):
            stacked.append(
                jnp.concatenate(
                    [lifted[(o * 4 + u) * 32 : (o * 4 + u + 1) * 32, tz * 128 : tz * 128 + 128] for u in range(4)],
                    1,
                )
            )
    lifted = times(jnp.concatenate(stacked, 0), wyh_ref[...], wyl_ref[...])
    corner = []
    for o in range(2):
        for tz in range(2):
            for ty in range(2):
                for tx in range(2):
                    at = (o * 2 + tz) * 32 + tx * 16
                    value = lifted[at : at + 16, ty * 256 : ty * 256 + 256]
                    if tx + ty + tz == 0:
                        corner.append(value)
                    else:
                        block_ref[o * 8 + tx + 2 * ty + 4 * tz] = value
    both = times(jnp.concatenate(corner, 0), w23h_ref[...], w23l_ref[...])
    depth = lax.broadcasted_iota(jnp.int32, (16, 128), 0)
    small = (depth < 8) & ((lane & 15) < 8)
    for o in range(2):
        mine = both[o * 16 : o * 16 + 16]
        second = times_left(wx2_ref[...], mine[:, :256])
        third = times_left(wx3_ref[...], mine[:, 256:])
        block_ref[o * 8] = jnp.concatenate(
            [jnp.where(small, third, second[:, :128]), second[:, 128:]], 1
        )

    for s in range(slots):
        pltpu.make_async_copy(window(s), corner_ref.at[s], corner_sem.at[s]).wait()
    for s in range(slots):

        @pl.when(s < index_ref[1])
        def _():
            value = block_ref[index_ref[0] + s]
            for t in range(8):
                tile = value[:, (t // 4) * 128 : (t // 4) * 128 + 128]
                near = pltpu.roll(tile, (128 - 32 * (t % 4)) % 128, 1)
                far = pltpu.roll(tile, (64 - 16 - 32 * (t % 4)) % 128, 1)
                old = corner_ref[s, :, pl.ds(t * 128, 128)]
                new = jnp.where(lane < 16, near, jnp.where((lane >= 64) & (lane < 80), far, old))
                corner_ref[s, :, pl.ds(t * 128, 128)] = new
            pltpu.make_async_copy(corner_ref.at[s], window(s), out_sem.at[s]).start()

    for s in range(slots):

        @pl.when(s < index_ref[1])
        def _():
            pltpu.make_async_copy(corner_ref.at[s], window(s), out_sem.at[s]).wait()


def coarse_call(index, pieces, fine):
    slots, edge, plane = fine.shape
    m32, m16, m8 = pass_matrix(32), pass_matrix(16), pass_matrix(8)
    deep = np.zeros((16, 16))
    deep[:8] = m8 @ m16[:8]
    eye8, eye16 = np.eye(8), np.eye(16)
    wz = np.zeros((256, 256))
    for cz in range(2):
        for tz in range(2):
            wz[cz * 128 : cz * 128 + 128, tz * 128 : tz * 128 + 128] = np.kron(
                eye8, m32[tz * 16 : tz * 16 + 16, cz * 16 : cz * 16 + 16].T
            )
    w23 = np.concatenate([np.kron(m16.T, m16.T), np.kron(deep.T, deep.T)[:, :128]], 1)
    weights = [
        left_terms(m32),
        *two_terms(wz),
        *two_terms(np.kron(m32.T, eye16)),
        *two_terms(w23),
        left_terms(m16),
        left_terms(deep),
    ]
    anywhere = pl.BlockSpec(memory_space=pl.ANY)
    vmem = pl.BlockSpec(memory_space=pltpu.VMEM)
    return pl.pallas_call(
        coarse_kernel,
        in_specs=[pl.BlockSpec(memory_space=pltpu.SMEM), vmem] + [vmem] * len(weights) + [anywhere],
        out_specs=anywhere,
        out_shape=jax.ShapeDtypeStruct(fine.shape, F32),
        scratch_shapes=[
            pltpu.VMEM((16, 16, 256), F32),
            pltpu.VMEM((slots, 16, 1024), F32),
            pltpu.SemaphoreType.DMA((slots,)),
            pltpu.SemaphoreType.DMA((slots,)),
        ],
        input_output_aliases={2 + len(weights): 0},
        compiler_params=pltpu.CompilerParams(vmem_limit_bytes=VMEM_SMALL),
        name="coarse",
    )(index, pieces.reshape(-1, 128), *weights, fine)


def exchange(lowpass, slots, token):
    me = lax.axis_index(AXES)
    devices = lax.axis_size(AXES)
    if devices == lowpass.shape[0]:
        got = lax.all_to_all(lowpass, AXES, 0, 0, tiled=True)
        sent, index = route_call(me.reshape(1), got, token, slots)
        return lax.all_to_all(sent, AXES, 0, 0, tiled=True), index
    every = lax.all_gather(lowpass, AXES, axis=0)
    counts = every[:, 0, 7, 0].astype(jnp.int32)
    starts = jnp.cumsum(counts) - counts
    blocks = starts[me] // 8 * 8 + jnp.arange(16, dtype=jnp.int32)
    owners = jnp.sum((starts[None, :] <= blocks[:, None]).astype(jnp.int32), axis=1) - 1
    place = jnp.minimum(blocks - starts[owners], slots - 1)
    pieces = jnp.transpose(every[owners, :, place], (1, 0, 2))
    return pieces, jnp.stack([starts[me] % 8, counts[me]])


def per_device(density, owner_counts):
    slots = density.shape[0]
    early = slots // 3
    lowpass, token = lowpass_call(owner_counts, density)
    fine, token = fine_call(owner_counts, token, density, 0, early)
    pieces, index = exchange(lowpass, slots, token)
    fine, _ = fine_call(owner_counts, index, density, early, slots, fine)
    return coarse_call(index, pieces, fine)


def solution(mesh):
    in_specs = (P(AXES, None, None), P(AXES))
    out_specs = P(AXES, None, None)
    return jax.shard_map(per_device, mesh=mesh, in_specs=in_specs, out_specs=out_specs, check_vma=False)
```

```python
import functools

import jax
import jax.numpy as jnp
import numpy as np
from jax import lax
from jax.experimental import pallas as pl
from jax.experimental.pallas import tpu as pltpu
from jax.sharding import PartitionSpec as P

ALPHA = -1.586134342059924
BETA = -0.052980118572961
GAMMA = 0.882911075530934
DELTA = 0.443506852043971
SCALE = 1.230174104914001
SQUARE = SCALE * SCALE
F32 = jnp.float32
BF16 = jnp.bfloat16
AXES = ("node", "dev")
MIB = 1 << 20
VMEM_LIMIT = 48 * MIB
VMEM_SMALL = 16 * MIB
VMEM_LARGE = 56 * MIB


def pass_matrix(n):
    low, high = np.eye(n)[0::2], np.eye(n)[1::2]

    def after(v):
        return np.concatenate([v[1:], v[-1:]], 0)

    def before(v):
        return np.concatenate([v[:1], v[:-1]], 0)

    high = high + ALPHA * (low + after(low))
    low = low + BETA * (before(high) + high)
    high = high + GAMMA * (low + after(low))
    low = low + DELTA * (before(high) + high)
    return np.concatenate([low / SCALE, high * SCALE], 0)


def two_terms(matrix):
    matrix = np.asarray(matrix, np.float32)
    first = matrix.astype(BF16)
    return first, (matrix - first.astype(np.float32)).astype(BF16)


def left_terms(matrix):
    first, second = two_terms(matrix)
    return np.concatenate([first, second, first], 1)


def split(value):
    first = value.astype(BF16)
    return first, (value - first.astype(F32)).astype(BF16)


def dot(left, right):
    return jnp.dot(left, right, preferred_element_type=F32)


def times(value, first, second):
    high, low = split(value)
    both = dot(jnp.concatenate([high, low], 0), first)
    count = value.shape[0]
    return both[:count] + both[count:] + dot(high, second)


def times_left(terms, value):
    high, low = split(value)
    return dot(terms, jnp.concatenate([high, high, low], 0))


def split_rows(rows):
    return [split(jnp.concatenate(rows[m : m + 2], 0)) for m in range(0, len(rows), 2)]


def start_tiles(src_ref, dst_ref, sems):
    for t in range(dst_ref.shape[2]):
        pltpu.make_async_copy(
            src_ref.at[:, :, pl.ds(t * 128, 128)], dst_ref.at[:, :, t, :], sems.at[t // 8]
        ).start()


def wait_tiles(dst_ref, sems, group):
    part = dst_ref.at[:, :, pl.ds(8 * group, 8), :]
    pltpu.make_async_copy(part, part, sems.at[group]).wait()


def lowpass_kernel(
    count_ref, x_any, wz_any, wyh_any, wyl_any, out_ref, token_ref, x_ref, wz_ref, wyh_ref, wyl_ref, l_ref, z_ref, sems, w_sems
):
    slots, edge = x_any.shape[:2]
    quarter = edge // 4
    rows_all = slots * 8 * quarter
    token_ref[0] = count_ref[0]
    start_tiles(x_any, x_ref, sems)
    weights = [
        pltpu.make_async_copy(src, dst, w_sems.at[i])
        for i, (src, dst) in enumerate(((wz_any, wz_ref), (wyh_any, wyh_ref), (wyl_any, wyl_ref)))
    ]
    for copy in weights:
        copy.start()
    for g in range(4):
        wait_tiles(x_ref, sems, g)

        @pl.loop(0, slots)
        def _(s):
            rows = [x_ref[s, x, pl.ds(8 * g, 8), :] for x in range(edge)]
            rows, _ = lift(rows[0::2], rows[1::2], edge // 2, False, False)
            rows, _ = lift(rows[0::2], rows[1::2], quarter, False, False)
            for m, (high, low) in enumerate(split_rows(rows)):
                at = pl.multiple_of(s * 8 * quarter + 16 * m, 16)
                cols = pl.ds((g // 2) * 128, 128)
                l_ref[g % 2, pl.ds(at, 16), cols] = high
                l_ref[g % 2, pl.ds(rows_all + at, 16), cols] = low

    for copy in weights:
        copy.wait()
    made = dot(l_ref[0], wz_ref[0]) + dot(l_ref[1], wz_ref[1])
    z_ref[...] = (made[:rows_all, :128] + made[rows_all:, :128]) + made[:rows_all, 128:]
    wide = jnp.concatenate([z_ref[pl.ds(i, slots * quarter, stride=8), :] for i in range(8)], 1)
    made = times(wide, wyh_ref[...], wyl_ref[...])
    out_ref[...] = jnp.full(out_ref.shape, count_ref[0].astype(F32))
    for slot in range(slots):
        for h in range(2):
            out_ref[pl.ds(8 * h + slot, quarter, stride=16), :] = made[
                slot * quarter : (slot + 1) * quarter, h * 128 : h * 128 + 128
            ]


def stacked(matrix):
    first, second = two_terms(matrix)
    return np.concatenate([first, first, second], 0)


def lowpass_call(owner_counts, density):
    slots, edge, plane = density.shape
    quarter = edge // 4
    two_levels = pass_matrix(edge // 2)[:quarter] @ pass_matrix(edge)[: edge // 2]
    wide = np.kron(np.eye(8), two_levels.T)
    wz = np.stack([np.concatenate(two_terms(w), 1) for w in (wide[:256], wide[256:])])
    i, gp, q, p = np.meshgrid(np.arange(8), np.arange(2), np.arange(2), np.arange(2), indexing="ij")
    entry = (2 * (8 * gp + i) + p + 32 * q).reshape(-1)
    wy = np.kron(two_levels.T[entry] / SQUARE, np.eye(quarter))
    wyh, wyl = two_terms(wy)
    anywhere = pl.BlockSpec(memory_space=pl.ANY)
    vmem = pl.BlockSpec(memory_space=pltpu.VMEM)
    rows_all = slots * 8 * quarter
    pieces, token = pl.pallas_call(
        lowpass_kernel,
        in_specs=[pl.BlockSpec(memory_space=pltpu.SMEM)] + [anywhere] * 4,
        out_specs=[vmem, pl.BlockSpec(memory_space=pltpu.SMEM)],
        out_shape=[
            jax.ShapeDtypeStruct((16 * quarter, 128), F32),
            jax.ShapeDtypeStruct((1,), jnp.int32),
        ],
        scratch_shapes=[
            pltpu.VMEM((slots, edge, plane // 128, 128), F32),
            pltpu.VMEM(wz.shape, BF16),
            pltpu.VMEM(wyh.shape, BF16),
            pltpu.VMEM(wyl.shape, BF16),
            pltpu.VMEM((2, 2 * rows_all, 256), BF16),
            pltpu.VMEM((rows_all, 128), F32),
            pltpu.SemaphoreType.DMA((4,)),
            pltpu.SemaphoreType.DMA((3,)),
        ],
        compiler_params=pltpu.CompilerParams(vmem_limit_bytes=VMEM_LARGE),
        name="lowpass",
    )(owner_counts, density, wz, wyh, wyl)
    return pieces.reshape(2 * quarter, 8, 128), token


def route_kernel(me_ref, got_ref, _, send_ref, index_ref, order_ref, count_ref, sem):
    devices = got_ref.shape[0]
    copy = pltpu.make_async_copy(got_ref.at[:, 7, :], count_ref, sem)
    copy.start()
    order_ref[...] = jnp.zeros_like(order_ref)
    copy.wait()
    start, my_start, my_count = 0, 0, 0
    starts = []
    for d in range(devices):
        count = count_ref[d, 0].astype(jnp.int32)
        starts.append(start)
        my_start = jnp.where(me_ref[0] == d, start, my_start)
        my_count = jnp.where(me_ref[0] == d, count, my_count)
        order_ref[pl.ds(start, 8), :] = got_ref[d]
        start = start + count
    for d in range(devices):
        at = pl.multiple_of(starts[d] // 8 * 8, 8) if d else 0
        send_ref[d] = order_ref[pl.ds(at, 16), :]
    index_ref[0] = my_start % 8
    index_ref[1] = my_count


def route_call(me, got, token, slots):
    devices = got.shape[0]
    return pl.pallas_call(
        route_kernel,
        in_specs=[
            pl.BlockSpec(memory_space=pltpu.SMEM),
            pl.BlockSpec(memory_space=pltpu.VMEM),
            pl.BlockSpec(memory_space=pltpu.SMEM),
        ],
        out_specs=[pl.BlockSpec(memory_space=pltpu.VMEM), pl.BlockSpec(memory_space=pltpu.SMEM)],
        out_shape=[
            jax.ShapeDtypeStruct((devices, 16, 128), F32),
            jax.ShapeDtypeStruct((2,), jnp.int32),
        ],
        scratch_shapes=[
            pltpu.VMEM((devices * slots + 16, 128), F32),
            pltpu.SMEM((devices, 128), F32),
            pltpu.SemaphoreType.DMA,
        ],
        compiler_params=pltpu.CompilerParams(vmem_limit_bytes=VMEM_SMALL),
        name="route",
    )(me, got, token)


def lift(low, high, n, halo, scaled):
    up = SQUARE if scaled else 1.0
    at = 2 if halo else 0
    first, second, third, fourth = ({} for _ in range(4))

    def get(values, i, is_low):
        if halo:
            return values[i]
        return values[min(i, n - 1)] if is_low else values[max(i, 0)]

    lows = {i - at: low[i] for i in range(len(low))}
    highs = {i - at: high[i] for i in range(len(high))}

    def make_first(i):
        first[i] = highs[i] + (ALPHA * up) * (lows[i] + get(lows, i + 1, True))

    def make_second(i):
        second[i] = lows[i] + (BETA / up) * (get(first, i - 1, False) + first[i])

    def make_third(i):
        third[i] = first[i] + (GAMMA * up) * (second[i] + get(second, i + 1, True))

    def make_fourth(i):
        fourth[i] = second[i] + (DELTA / up) * (get(third, i - 1, False) + third[i])

    if halo:
        for i in range(-2, n + 1):
            make_first(i)
            if i >= -1:
                make_second(i)
            if i >= 0:
                make_third(i - 1)
            if i >= 1:
                make_fourth(i - 1)
    else:
        for i in range(n):
            make_first(i)
            make_second(i)
            if i >= 1:
                make_third(i - 1)
                make_fourth(i - 1)
        make_third(n - 1)
        make_fourth(n - 1)
    return [fourth[i] for i in range(n)], [third[i] for i in range(n)]


def fine_kernel(count_ref, _, x_any, w1_ref, w2_ref, *refs, first):
    out_ref, token_ref, x_buf, l_ref, y_ref, c_ref, m_ref, d_ref, sems = refs[-9:]
    step = pl.program_id(0)
    slot = step + first
    edge = x_any.shape[1]
    tiles = x_buf.shape[2]
    pairs = tiles // 2
    half = edge // 2
    corner = 8 * half
    live = slot < count_ref[0]
    lane = lax.broadcasted_iota(jnp.int32, (8, 128), 1)
    front = lane < 64
    inner = (lane & 63) < half
    token_ref[0] = step

    def cross(a, b):
        return pltpu.roll(jnp.where(front, b, a), 64, 1)

    def exchange(a, b):
        crossed = cross(a, b)
        return jnp.where(front, a, crossed), jnp.where(front, crossed, b)

    def with_halo(low, high):
        one, two = cross(low[0], low[-1]), cross(low[1], low[-2])
        low_all = [jnp.where(front, low[2], two), jnp.where(front, low[1], one)] + low
        low_all += [jnp.where(front, one, low[-1]), jnp.where(front, two, low[-2])]
        one, two = cross(high[0], high[-1]), cross(high[1], high[-2])
        high_all = [jnp.where(front, high[1], two), jnp.where(front, high[0], one)] + high
        return low_all, high_all + [jnp.where(front, one, high[-2])]

    def scaled_rows(rows):
        low, high = lift(rows[0::2], rows[1::2], len(rows) // 2, False, False)
        return [v * (1.0 / SCALE) for v in low] + [v * SCALE for v in high]

    def store_terms(ref, row, col, rows):
        for m, (high, low) in enumerate(split_rows(rows)):
            place = pl.ds(pl.multiple_of(row + 16 * m, 16), 16)
            ref[place, pl.ds(col, 128)] = high
            ref[place, pl.ds(256 + col, 128)] = low
            ref[place, pl.ds(512 + col, 128)] = high

    def fetch(which, place):
        for t in range(tiles):
            pltpu.make_async_copy(
                x_any.at[which, :, pl.ds(t * 128, 128)], x_buf.at[place, :, t, :], sems.at[place]
            ).start()

    @pl.when((step == 0) & live)
    def _():
        fetch(slot, 0)

    @pl.when((step + 1 < pl.num_programs(0)) & (slot + 1 < count_ref[0]))
    def _():
        fetch(slot + 1, (step + 1) % 2)

    @pl.when(jnp.logical_not(live))
    def _():
        out_ref[...] = jnp.zeros_like(out_ref)

    @pl.when(live)
    def _():
        x = x_buf.at[step % 2]
        pltpu.make_async_copy(x, x, sems.at[step % 2]).wait()
        for g in range(4):
            rows = scaled_rows([x[i, pl.ds(8 * g, 8), :] for i in range(edge)])
            store_terms(l_ref, (g % 2) * 8 * edge, (g // 2) * 128, rows)
        lifted = dot(l_ref[...], w1_ref[...])
        y_ref[0] = lifted[:, :128]
        y_ref[1] = lifted[:, 128:]
        for r in range(edge // 8):
            rows = pl.ds(8 * r, 8)

            def tile(part, j):
                return y_ref[part, pl.ds((j // 8) * 8 * edge + 64 * r + j % 8, 8, stride=8), :]

            low = [tile(0, j) for j in range(pairs)]
            high = [tile(1, j) for j in range(pairs)]
            low, high = lift(*with_halo(low, high), pairs, True, True)
            for part, values in enumerate((low, high)):
                for t in range(pairs // 2):
                    a, b = exchange(values[2 * t], values[2 * t + 1])
                    at = part * pairs + t
                    out_ref[0, rows, pl.ds(at * 128, 128)] = a
                    out_ref[0, rows, pl.ds((at + pairs // 2) * 128, 128)] = b
            if r < half // 8:
                low, high = lift(*with_halo(low[0::2], low[1::2]), 8, True, False)
                for i in range(8):
                    c_ref[pl.ds(64 * r + i, 8, stride=8), :] = low[i]
                    c_ref[pl.ds(corner + 64 * r + i, 8, stride=8), :] = high[i]
        for u in range(2):
            rows = scaled_rows([c_ref[pl.ds(u * corner + 8 * i, 8), :] for i in range(half)])
            store_terms(m_ref, 0, u * 128, rows)
        lifted = dot(m_ref[...], w2_ref[...])
        d_ref[0] = lifted[:, :128]
        d_ref[1] = lifted[:, 128:]
        for u in range(2):
            for t in range(4):
                for r in range(half // 8):
                    a = d_ref[u, pl.ds(64 * r + 2 * t, 8, stride=8), :]
                    b = d_ref[u, pl.ds(64 * r + 2 * t + 1, 8, stride=8), :]
                    for at, value in zip((u * 8 + t, u * 8 + 4 + t), exchange(a, b)):
                        rows, cols = pl.ds(8 * r, 8), pl.ds(at * 128, 128)
                        out_ref[0, rows, cols] = jnp.where(inner, value, out_ref[0, rows, cols])


def fine_call(owner_counts, token, density, first, last, before=None):
    slots, edge, plane = density.shape
    tiles = plane // 128
    half = edge // 2
    pairs = tiles // 2
    count = last - first
    one = pass_matrix(edge).T
    zero = np.zeros_like(one)
    w1 = np.block(
        [
            [one / SCALE, zero, zero, zero],
            [zero, zero, one * SCALE, zero],
            [zero, one / SCALE, zero, zero],
            [zero, zero, zero, one * SCALE],
        ]
    )
    two = np.zeros_like(one)
    two[:half, :half] = pass_matrix(half).T
    w2 = np.kron(np.diag([1 / SCALE, 1 / SCALE, SCALE, SCALE]), two)
    anywhere = pl.BlockSpec(memory_space=pl.ANY)
    smem = pl.BlockSpec(memory_space=pltpu.SMEM)
    old = [] if before is None else [before]
    fixed = pl.BlockSpec((768, 256), lambda s: (0, 0))
    return pl.pallas_call(
        functools.partial(fine_kernel, first=first),
        grid=(count,),
        in_specs=[smem, smem, anywhere, fixed, fixed] + [anywhere] * len(old),
        out_specs=[pl.BlockSpec((1, edge, plane), lambda s: (s + first, 0, 0)), smem],
        out_shape=[
            jax.ShapeDtypeStruct(density.shape, F32),
            jax.ShapeDtypeStruct((1,), jnp.int32),
        ],
        scratch_shapes=[
            pltpu.VMEM((2, edge, tiles, 128), F32),
            pltpu.VMEM((pairs * edge, 768), BF16),
            pltpu.VMEM((2, pairs * edge, 128), F32),
            pltpu.VMEM((16 * half, 128), F32),
            pltpu.VMEM((8 * half, 768), BF16),
            pltpu.VMEM((2, 8 * half, 128), F32),
            pltpu.SemaphoreType.DMA((2,)),
        ],
        input_output_aliases={5: 0} if old else {},
        compiler_params=pltpu.CompilerParams(vmem_limit_bytes=VMEM_LIMIT),
        cost_estimate=pl.CostEstimate(
            flops=6 * count * edge * plane * 256, bytes_accessed=2 * count * MIB, transcendentals=0
        ),
        name="fine",
    )(owner_counts, token, density, stacked(w1), stacked(w2), *old)


def coarse_kernel(
    index_ref,
    piece_ref,
    wx_ref,
    wzh_ref,
    wzl_ref,
    wyh_ref,
    wyl_ref,
    w23h_ref,
    w23l_ref,
    wx2_ref,
    wx3_ref,
    fine_ref,
    out_ref,
    block_ref,
    corner_ref,
    corner_sem,
    out_sem,
):
    slots = corner_ref.shape[0]
    lane = lax.broadcasted_iota(jnp.int32, (16, 128), 1)

    def window(s):
        return out_ref.at[s, pl.ds(0, 16), pl.ds(0, 1024)]

    def piece(i):
        return jnp.concatenate([piece_ref[pl.ds(16 * h + i, 16, stride=32), :] for h in range(2)], 1)

    for s in range(slots):
        pltpu.make_async_copy(window(s), corner_ref.at[s], corner_sem.at[s]).start()

    first = [
        [
            times_left(wx_ref[...], jnp.concatenate([piece(o * 8 + 2 * q), piece(o * 8 + 2 * q + 1)], 0))
            for q in range(4)
        ]
        for o in range(2)
    ]
    stacked = []
    for o in range(2):
        for cy in range(2):
            for yh in range(2):
                part = slice(yh * 128, yh * 128 + 128)
                stacked.append(jnp.concatenate([first[o][cy][:, part], first[o][2 + cy][:, part]], 1))
    lifted = times(jnp.concatenate(stacked, 0), wzh_ref[...], wzl_ref[...])
    stacked = []
    for o in range(2):
        for tz in range(2):
            stacked.append(
                jnp.concatenate(
                    [lifted[(o * 4 + u) * 32 : (o * 4 + u + 1) * 32, tz * 128 : tz * 128 + 128] for u in range(4)],
                    1,
                )
            )
    lifted = times(jnp.concatenate(stacked, 0), wyh_ref[...], wyl_ref[...])
    corner = []
    for o in range(2):
        for tz in range(2):
            for ty in range(2):
                for tx in range(2):
                    at = (o * 2 + tz) * 32 + tx * 16
                    value = lifted[at : at + 16, ty * 256 : ty * 256 + 256]
                    if tx + ty + tz == 0:
                        corner.append(value)
                    else:
                        block_ref[o * 8 + tx + 2 * ty + 4 * tz] = value
    both = times(jnp.concatenate(corner, 0), w23h_ref[...], w23l_ref[...])
    depth = lax.broadcasted_iota(jnp.int32, (16, 128), 0)
    small = (depth < 8) & ((lane & 15) < 8)
    for o in range(2):
        mine = both[o * 16 : o * 16 + 16]
        second = times_left(wx2_ref[...], mine[:, :256])
        third = times_left(wx3_ref[...], mine[:, 256:])
        block_ref[o * 8] = jnp.concatenate(
            [jnp.where(small, third, second[:, :128]), second[:, 128:]], 1
        )

    for s in range(slots):
        pltpu.make_async_copy(window(s), corner_ref.at[s], corner_sem.at[s]).wait()
    for s in range(slots):

        @pl.when(s < index_ref[1])
        def _():
            value = block_ref[index_ref[0] + s]
            for t in range(8):
                tile = value[:, (t // 4) * 128 : (t // 4) * 128 + 128]
                near = pltpu.roll(tile, (128 - 32 * (t % 4)) % 128, 1)
                far = pltpu.roll(tile, (64 - 16 - 32 * (t % 4)) % 128, 1)
                old = corner_ref[s, :, pl.ds(t * 128, 128)]
                new = jnp.where(lane < 16, near, jnp.where((lane >= 64) & (lane < 80), far, old))
                corner_ref[s, :, pl.ds(t * 128, 128)] = new
            pltpu.make_async_copy(corner_ref.at[s], window(s), out_sem.at[s]).start()

    for s in range(slots):

        @pl.when(s < index_ref[1])
        def _():
            pltpu.make_async_copy(corner_ref.at[s], window(s), out_sem.at[s]).wait()


def coarse_call(index, pieces, fine):
    slots, edge, plane = fine.shape
    m32, m16, m8 = pass_matrix(32), pass_matrix(16), pass_matrix(8)
    deep = np.zeros((16, 16))
    deep[:8] = m8 @ m16[:8]
    eye8, eye16 = np.eye(8), np.eye(16)
    wz = np.zeros((256, 256))
    for cz in range(2):
        for tz in range(2):
            wz[cz * 128 : cz * 128 + 128, tz * 128 : tz * 128 + 128] = np.kron(
                eye8, m32[tz * 16 : tz * 16 + 16, cz * 16 : cz * 16 + 16].T
            )
    w23 = np.concatenate([np.kron(m16.T, m16.T), np.kron(deep.T, deep.T)[:, :128]], 1)
    weights = [
        left_terms(m32),
        *two_terms(wz),
        *two_terms(np.kron(m32.T, eye16)),
        *two_terms(w23),
        left_terms(m16),
        left_terms(deep),
    ]
    anywhere = pl.BlockSpec(memory_space=pl.ANY)
    vmem = pl.BlockSpec(memory_space=pltpu.VMEM)
    return pl.pallas_call(
        coarse_kernel,
        in_specs=[pl.BlockSpec(memory_space=pltpu.SMEM), vmem] + [vmem] * len(weights) + [anywhere],
        out_specs=anywhere,
        out_shape=jax.ShapeDtypeStruct(fine.shape, F32),
        scratch_shapes=[
            pltpu.VMEM((16, 16, 256), F32),
            pltpu.VMEM((slots, 16, 1024), F32),
            pltpu.SemaphoreType.DMA((slots,)),
            pltpu.SemaphoreType.DMA((slots,)),
        ],
        input_output_aliases={2 + len(weights): 0},
        compiler_params=pltpu.CompilerParams(vmem_limit_bytes=VMEM_SMALL),
        name="coarse",
    )(index, pieces.reshape(-1, 128), *weights, fine)


def exchange(lowpass, slots, token):
    me = lax.axis_index(AXES)
    devices = lax.axis_size(AXES)
    if devices == lowpass.shape[0]:
        got = lax.all_to_all(lowpass, AXES, 0, 0, tiled=True)
        sent, index = route_call(me.reshape(1), got, token, slots)
        return lax.all_to_all(sent, AXES, 0, 0, tiled=True), index
    every = lax.all_gather(lowpass, AXES, axis=0)
    counts = every[:, 0, 7, 0].astype(jnp.int32)
    starts = jnp.cumsum(counts) - counts
    blocks = starts[me] // 8 * 8 + jnp.arange(16, dtype=jnp.int32)
    owners = jnp.sum((starts[None, :] <= blocks[:, None]).astype(jnp.int32), axis=1) - 1
    place = jnp.minimum(blocks - starts[owners], slots - 1)
    pieces = jnp.transpose(every[owners, :, place], (1, 0, 2))
    return pieces, jnp.stack([starts[me] % 8, counts[me]])


def per_device(density, owner_counts):
    slots = density.shape[0]
    early = slots // 3
    lowpass, token = lowpass_call(owner_counts, density)
    fine, token = fine_call(owner_counts, token, density, 0, early)
    pieces, index = exchange(lowpass, slots, token)
    fine, _ = fine_call(owner_counts, index, density, early, slots, fine)
    return coarse_call(index, pieces, fine)


def solution(mesh):
    in_specs = (P(AXES, None, None), P(AXES))
    out_specs = P(AXES, None, None)
    return jax.shard_map(per_device, mesh=mesh, in_specs=in_specs, out_specs=out_specs, check_vma=False)
```

```python
import functools

import jax
import jax.numpy as jnp
import numpy as np
from jax import lax
from jax.experimental import pallas as pl
from jax.experimental.pallas import tpu as pltpu
from jax.sharding import PartitionSpec as P

ALPHA = -1.586134342059924
BETA = -0.052980118572961
GAMMA = 0.882911075530934
DELTA = 0.443506852043971
SCALE = 1.230174104914001
SQUARE = SCALE * SCALE
F32 = jnp.float32
BF16 = jnp.bfloat16
AXES = ("node", "dev")
MIB = 1 << 20
VMEM_LIMIT = 48 * MIB
VMEM_SMALL = 16 * MIB
VMEM_LARGE = 56 * MIB


def pass_matrix(n):
    low, high = np.eye(n)[0::2], np.eye(n)[1::2]

    def after(v):
        return np.concatenate([v[1:], v[-1:]], 0)

    def before(v):
        return np.concatenate([v[:1], v[:-1]], 0)

    high = high + ALPHA * (low + after(low))
    low = low + BETA * (before(high) + high)
    high = high + GAMMA * (low + after(low))
    low = low + DELTA * (before(high) + high)
    return np.concatenate([low / SCALE, high * SCALE], 0)


def two_terms(matrix):
    matrix = np.asarray(matrix, np.float32)
    first = matrix.astype(BF16)
    return first, (matrix - first.astype(np.float32)).astype(BF16)


def left_terms(matrix):
    first, second = two_terms(matrix)
    return np.concatenate([first, second, first], 1)


def split(value):
    first = value.astype(BF16)
    return first, (value - first.astype(F32)).astype(BF16)


def dot(left, right):
    return jnp.dot(left, right, preferred_element_type=F32)


def times(value, first, second):
    high, low = split(value)
    both = dot(jnp.concatenate([high, low], 0), first)
    count = value.shape[0]
    return both[:count] + both[count:] + dot(high, second)


def times_left(terms, value):
    high, low = split(value)
    return dot(terms, jnp.concatenate([high, high, low], 0))


def split_rows(rows):
    return [split(jnp.concatenate(rows[m : m + 2], 0)) for m in range(0, len(rows), 2)]


def start_tiles(src_ref, dst_ref, sems):
    for t in range(dst_ref.shape[2]):
        pltpu.make_async_copy(
            src_ref.at[:, :, pl.ds(t * 128, 128)], dst_ref.at[:, :, t, :], sems.at[t // 8]
        ).start()


def wait_tiles(dst_ref, sems, group):
    part = dst_ref.at[:, :, pl.ds(8 * group, 8), :]
    pltpu.make_async_copy(part, part, sems.at[group]).wait()


def lowpass_kernel(
    count_ref, x_any, wz_any, wyh_any, wyl_any, out_ref, token_ref, x_ref, wz_ref, wyh_ref, wyl_ref, l_ref, z_ref, sems, w_sems
):
    slots, edge = x_any.shape[:2]
    quarter = edge // 4
    rows_all = slots * 8 * quarter
    token_ref[0] = count_ref[0]
    start_tiles(x_any, x_ref, sems)
    weights = [
        pltpu.make_async_copy(src, dst, w_sems.at[i])
        for i, (src, dst) in enumerate(((wz_any, wz_ref), (wyh_any, wyh_ref), (wyl_any, wyl_ref)))
    ]
    for copy in weights:
        copy.start()
    for g in range(4):
        wait_tiles(x_ref, sems, g)

        @pl.loop(0, slots)
        def _(s):
            rows = [x_ref[s, x, pl.ds(8 * g, 8), :] for x in range(edge)]
            rows, _ = lift(rows[0::2], rows[1::2], edge // 2, False, False)
            rows, _ = lift(rows[0::2], rows[1::2], quarter, False, False)
            for m, (high, low) in enumerate(split_rows(rows)):
                at = pl.multiple_of(s * 8 * quarter + 16 * m, 16)
                cols = pl.ds((g % 2) * 256 + (g // 2) * 128, 128)
                l_ref[pl.ds(at, 16), cols] = high
                l_ref[pl.ds(rows_all + at, 16), cols] = low

    for copy in weights:
        copy.wait()
    made = dot(l_ref[...], wz_ref[...])
    z_ref[...] = (made[:rows_all, :128] + made[rows_all:, :128]) + made[:rows_all, 128:]
    wide = jnp.concatenate([z_ref[pl.ds(i, slots * quarter, stride=8), :] for i in range(8)], 1)
    made = times(wide, wyh_ref[...], wyl_ref[...])
    out_ref[...] = jnp.full(out_ref.shape, count_ref[0].astype(F32))
    for slot in range(slots):
        for h in range(2):
            out_ref[pl.ds(8 * h + slot, quarter, stride=16), :] = made[
                slot * quarter : (slot + 1) * quarter, h * 128 : h * 128 + 128
            ]


def stacked(matrix):
    first, second = two_terms(matrix)
    return np.concatenate([first, first, second], 0)


def lowpass_call(owner_counts, density):
    slots, edge, plane = density.shape
    quarter = edge // 4
    two_levels = pass_matrix(edge // 2)[:quarter] @ pass_matrix(edge)[: edge // 2]
    wz = np.concatenate(two_terms(np.kron(np.eye(8), two_levels.T)), 1)
    i, gp, q, p = np.meshgrid(np.arange(8), np.arange(2), np.arange(2), np.arange(2), indexing="ij")
    entry = (2 * (8 * gp + i) + p + 32 * q).reshape(-1)
    wy = np.kron(two_levels.T[entry] / SQUARE, np.eye(quarter))
    wyh, wyl = two_terms(wy)
    anywhere = pl.BlockSpec(memory_space=pl.ANY)
    vmem = pl.BlockSpec(memory_space=pltpu.VMEM)
    rows_all = slots * 8 * quarter
    pieces, token = pl.pallas_call(
        lowpass_kernel,
        in_specs=[pl.BlockSpec(memory_space=pltpu.SMEM)] + [anywhere] * 4,
        out_specs=[vmem, pl.BlockSpec(memory_space=pltpu.SMEM)],
        out_shape=[
            jax.ShapeDtypeStruct((16 * quarter, 128), F32),
            jax.ShapeDtypeStruct((1,), jnp.int32),
        ],
        scratch_shapes=[
            pltpu.VMEM((slots, edge, plane // 128, 128), F32),
            pltpu.VMEM(wz.shape, BF16),
            pltpu.VMEM(wyh.shape, BF16),
            pltpu.VMEM(wyl.shape, BF16),
            pltpu.VMEM((2 * rows_all, 512), BF16),
            pltpu.VMEM((rows_all, 128), F32),
            pltpu.SemaphoreType.DMA((4,)),
            pltpu.SemaphoreType.DMA((3,)),
        ],
        compiler_params=pltpu.CompilerParams(vmem_limit_bytes=VMEM_LARGE),
        name="lowpass",
    )(owner_counts, density, wz, wyh, wyl)
    return pieces.reshape(2 * quarter, 8, 128), token


def route_kernel(me_ref, got_ref, _, send_ref, index_ref, order_ref, count_ref, sem):
    devices = got_ref.shape[0]
    copy = pltpu.make_async_copy(got_ref.at[:, 7, :], count_ref, sem)
    copy.start()
    order_ref[...] = jnp.zeros_like(order_ref)
    copy.wait()
    start, my_start, my_count = 0, 0, 0
    starts = []
    for d in range(devices):
        count = count_ref[d, 0].astype(jnp.int32)
        starts.append(start)
        my_start = jnp.where(me_ref[0] == d, start, my_start)
        my_count = jnp.where(me_ref[0] == d, count, my_count)
        order_ref[pl.ds(start, 8), :] = got_ref[d]
        start = start + count
    for d in range(devices):
        at = pl.multiple_of(starts[d] // 8 * 8, 8) if d else 0
        send_ref[d] = order_ref[pl.ds(at, 16), :]
    index_ref[0] = my_start % 8
    index_ref[1] = my_count


def route_call(me, got, token, slots):
    devices = got.shape[0]
    return pl.pallas_call(
        route_kernel,
        in_specs=[
            pl.BlockSpec(memory_space=pltpu.SMEM),
            pl.BlockSpec(memory_space=pltpu.VMEM),
            pl.BlockSpec(memory_space=pltpu.SMEM),
        ],
        out_specs=[pl.BlockSpec(memory_space=pltpu.VMEM), pl.BlockSpec(memory_space=pltpu.SMEM)],
        out_shape=[
            jax.ShapeDtypeStruct((devices, 16, 128), F32),
            jax.ShapeDtypeStruct((2,), jnp.int32),
        ],
        scratch_shapes=[
            pltpu.VMEM((devices * slots + 16, 128), F32),
            pltpu.SMEM((devices, 128), F32),
            pltpu.SemaphoreType.DMA,
        ],
        compiler_params=pltpu.CompilerParams(vmem_limit_bytes=VMEM_SMALL),
        name="route",
    )(me, got, token)


def lift(low, high, n, halo, scaled):
    up = SQUARE if scaled else 1.0
    at = 2 if halo else 0
    first, second, third, fourth = ({} for _ in range(4))

    def get(values, i, is_low):
        if halo:
            return values[i]
        return values[min(i, n - 1)] if is_low else values[max(i, 0)]

    lows = {i - at: low[i] for i in range(len(low))}
    highs = {i - at: high[i] for i in range(len(high))}

    def make_first(i):
        first[i] = highs[i] + (ALPHA * up) * (lows[i] + get(lows, i + 1, True))

    def make_second(i):
        second[i] = lows[i] + (BETA / up) * (get(first, i - 1, False) + first[i])

    def make_third(i):
        third[i] = first[i] + (GAMMA * up) * (second[i] + get(second, i + 1, True))

    def make_fourth(i):
        fourth[i] = second[i] + (DELTA / up) * (get(third, i - 1, False) + third[i])

    if halo:
        for i in range(-2, n + 1):
            make_first(i)
            if i >= -1:
                make_second(i)
            if i >= 0:
                make_third(i - 1)
            if i >= 1:
                make_fourth(i - 1)
    else:
        for i in range(n):
            make_first(i)
            make_second(i)
            if i >= 1:
                make_third(i - 1)
                make_fourth(i - 1)
        make_third(n - 1)
        make_fourth(n - 1)
    return [fourth[i] for i in range(n)], [third[i] for i in range(n)]


def fine_kernel(count_ref, _, x_any, w1_ref, w2_ref, *refs, first):
    out_ref, token_ref, x_buf, l_ref, y_ref, c_ref, m_ref, d_ref, sems = refs[-9:]
    step = pl.program_id(0)
    slot = step + first
    edge = x_any.shape[1]
    tiles = x_buf.shape[2]
    pairs = tiles // 2
    half = edge // 2
    corner = 8 * half
    live = slot < count_ref[0]
    lane = lax.broadcasted_iota(jnp.int32, (8, 128), 1)
    front = lane < 64
    inner = (lane & 63) < half
    token_ref[0] = step

    def cross(a, b):
        return pltpu.roll(jnp.where(front, b, a), 64, 1)

    def exchange(a, b):
        crossed = cross(a, b)
        return jnp.where(front, a, crossed), jnp.where(front, crossed, b)

    def with_halo(low, high):
        one, two = cross(low[0], low[-1]), cross(low[1], low[-2])
        low_all = [jnp.where(front, low[2], two), jnp.where(front, low[1], one)] + low
        low_all += [jnp.where(front, one, low[-1]), jnp.where(front, two, low[-2])]
        one, two = cross(high[0], high[-1]), cross(high[1], high[-2])
        high_all = [jnp.where(front, high[1], two), jnp.where(front, high[0], one)] + high
        return low_all, high_all + [jnp.where(front, one, high[-2])]

    def scaled_rows(rows):
        low, high = lift(rows[0::2], rows[1::2], len(rows) // 2, False, False)
        return [v * (1.0 / SCALE) for v in low] + [v * SCALE for v in high]

    def store_terms(ref, row, col, rows):
        for m, (high, low) in enumerate(split_rows(rows)):
            place = pl.ds(pl.multiple_of(row + 16 * m, 16), 16)
            ref[place, pl.ds(col, 128)] = high
            ref[place, pl.ds(256 + col, 128)] = low
            ref[place, pl.ds(512 + col, 128)] = high

    def fetch(which, place):
        for t in range(tiles):
            pltpu.make_async_copy(
                x_any.at[which, :, pl.ds(t * 128, 128)], x_buf.at[place, :, t, :], sems.at[place]
            ).start()

    @pl.when((step == 0) & live)
    def _():
        fetch(slot, 0)

    @pl.when(jnp.logical_not(live))
    def _():
        out_ref[...] = jnp.zeros_like(out_ref)

    @pl.when(live)
    def _():
        x = x_buf.at[step % 2]
        pltpu.make_async_copy(x, x, sems.at[step % 2]).wait()

    @pl.when((step + 1 < pl.num_programs(0)) & (slot + 1 < count_ref[0]))
    def _():
        fetch(slot + 1, (step + 1) % 2)

    @pl.when(live)
    def _():
        x = x_buf.at[step % 2]
        for g in range(4):
            rows = scaled_rows([x[i, pl.ds(8 * g, 8), :] for i in range(edge)])
            store_terms(l_ref, (g % 2) * 8 * edge, (g // 2) * 128, rows)
        lifted = dot(l_ref[...], w1_ref[...])
        y_ref[0] = lifted[:, :128]
        y_ref[1] = lifted[:, 128:]
        for r in range(edge // 8):
            rows = pl.ds(8 * r, 8)

            def tile(part, j):
                return y_ref[part, pl.ds((j // 8) * 8 * edge + 64 * r + j % 8, 8, stride=8), :]

            low = [tile(0, j) for j in range(pairs)]
            high = [tile(1, j) for j in range(pairs)]
            low, high = lift(*with_halo(low, high), pairs, True, True)
            for part, values in enumerate((low, high)):
                for t in range(pairs // 2):
                    a, b = exchange(values[2 * t], values[2 * t + 1])
                    at = part * pairs + t
                    out_ref[0, rows, pl.ds(at * 128, 128)] = a
                    out_ref[0, rows, pl.ds((at + pairs // 2) * 128, 128)] = b
            if r < half // 8:
                low, high = lift(*with_halo(low[0::2], low[1::2]), 8, True, False)
                for i in range(8):
                    c_ref[pl.ds(64 * r + i, 8, stride=8), :] = low[i]
                    c_ref[pl.ds(corner + 64 * r + i, 8, stride=8), :] = high[i]
        for u in range(2):
            rows = scaled_rows([c_ref[pl.ds(u * corner + 8 * i, 8), :] for i in range(half)])
            store_terms(m_ref, 0, u * 128, rows)
        lifted = dot(m_ref[...], w2_ref[...])
        d_ref[0] = lifted[:, :128]
        d_ref[1] = lifted[:, 128:]
        for u in range(2):
            for t in range(4):
                for r in range(half // 8):
                    a = d_ref[u, pl.ds(64 * r + 2 * t, 8, stride=8), :]
                    b = d_ref[u, pl.ds(64 * r + 2 * t + 1, 8, stride=8), :]
                    for at, value in zip((u * 8 + t, u * 8 + 4 + t), exchange(a, b)):
                        rows, cols = pl.ds(8 * r, 8), pl.ds(at * 128, 128)
                        out_ref[0, rows, cols] = jnp.where(inner, value, out_ref[0, rows, cols])


def fine_call(owner_counts, token, density, first, last, before=None):
    slots, edge, plane = density.shape
    tiles = plane // 128
    half = edge // 2
    pairs = tiles // 2
    count = last - first
    one = pass_matrix(edge).T
    zero = np.zeros_like(one)
    w1 = np.block(
        [
            [one / SCALE, zero, zero, zero],
            [zero, zero, one * SCALE, zero],
            [zero, one / SCALE, zero, zero],
            [zero, zero, zero, one * SCALE],
        ]
    )
    two = np.zeros_like(one)
    two[:half, :half] = pass_matrix(half).T
    w2 = np.kron(np.diag([1 / SCALE, 1 / SCALE, SCALE, SCALE]), two)
    anywhere = pl.BlockSpec(memory_space=pl.ANY)
    smem = pl.BlockSpec(memory_space=pltpu.SMEM)
    old = [] if before is None else [before]
    fixed = pl.BlockSpec((768, 256), lambda s: (0, 0))
    return pl.pallas_call(
        functools.partial(fine_kernel, first=first),
        grid=(count,),
        in_specs=[smem, smem, anywhere, fixed, fixed] + [anywhere] * len(old),
        out_specs=[pl.BlockSpec((1, edge, plane), lambda s: (s + first, 0, 0)), smem],
        out_shape=[
            jax.ShapeDtypeStruct(density.shape, F32),
            jax.ShapeDtypeStruct((1,), jnp.int32),
        ],
        scratch_shapes=[
            pltpu.VMEM((2, edge, tiles, 128), F32),
            pltpu.VMEM((pairs * edge, 768), BF16),
            pltpu.VMEM((2, pairs * edge, 128), F32),
            pltpu.VMEM((16 * half, 128), F32),
            pltpu.VMEM((8 * half, 768), BF16),
            pltpu.VMEM((2, 8 * half, 128), F32),
            pltpu.SemaphoreType.DMA((2,)),
        ],
        input_output_aliases={5: 0} if old else {},
        compiler_params=pltpu.CompilerParams(vmem_limit_bytes=VMEM_LIMIT),
        cost_estimate=pl.CostEstimate(
            flops=6 * count * edge * plane * 256, bytes_accessed=2 * count * MIB, transcendentals=0
        ),
        name="fine",
    )(owner_counts, token, density, stacked(w1), stacked(w2), *old)


def coarse_kernel(
    index_ref,
    piece_ref,
    wx_ref,
    wzh_ref,
    wzl_ref,
    wyh_ref,
    wyl_ref,
    w23h_ref,
    w23l_ref,
    wx2_ref,
    wx3_ref,
    fine_ref,
    out_ref,
    block_ref,
    corner_ref,
    corner_sem,
    out_sem,
):
    slots = corner_ref.shape[0]
    lane = lax.broadcasted_iota(jnp.int32, (16, 128), 1)

    def window(s):
        return out_ref.at[s, pl.ds(0, 16), pl.ds(0, 1024)]

    def piece(i):
        return jnp.concatenate([piece_ref[pl.ds(16 * h + i, 16, stride=32), :] for h in range(2)], 1)

    for s in range(slots):
        pltpu.make_async_copy(window(s), corner_ref.at[s], corner_sem.at[s]).start()

    first = [
        [
            times_left(wx_ref[...], jnp.concatenate([piece(o * 8 + 2 * q), piece(o * 8 + 2 * q + 1)], 0))
            for q in range(4)
        ]
        for o in range(2)
    ]
    stacked = []
    for o in range(2):
        for cy in range(2):
            for yh in range(2):
                part = slice(yh * 128, yh * 128 + 128)
                stacked.append(jnp.concatenate([first[o][cy][:, part], first[o][2 + cy][:, part]], 1))
    lifted = times(jnp.concatenate(stacked, 0), wzh_ref[...], wzl_ref[...])
    stacked = []
    for o in range(2):
        for tz in range(2):
            stacked.append(
                jnp.concatenate(
                    [lifted[(o * 4 + u) * 32 : (o * 4 + u + 1) * 32, tz * 128 : tz * 128 + 128] for u in range(4)],
                    1,
                )
            )
    lifted = times(jnp.concatenate(stacked, 0), wyh_ref[...], wyl_ref[...])
    corner = []
    for o in range(2):
        for tz in range(2):
            for ty in range(2):
                for tx in range(2):
                    at = (o * 2 + tz) * 32 + tx * 16
                    value = lifted[at : at + 16, ty * 256 : ty * 256 + 256]
                    if tx + ty + tz == 0:
                        corner.append(value)
                    else:
                        block_ref[o * 8 + tx + 2 * ty + 4 * tz] = value
    both = times(jnp.concatenate(corner, 0), w23h_ref[...], w23l_ref[...])
    depth = lax.broadcasted_iota(jnp.int32, (16, 128), 0)
    small = (depth < 8) & ((lane & 15) < 8)
    for o in range(2):
        mine = both[o * 16 : o * 16 + 16]
        second = times_left(wx2_ref[...], mine[:, :256])
        third = times_left(wx3_ref[...], mine[:, 256:])
        block_ref[o * 8] = jnp.concatenate(
            [jnp.where(small, third, second[:, :128]), second[:, 128:]], 1
        )

    for s in range(slots):
        pltpu.make_async_copy(window(s), corner_ref.at[s], corner_sem.at[s]).wait()
    for s in range(slots):

        @pl.when(s < index_ref[1])
        def _():
            value = block_ref[index_ref[0] + s]
            for t in range(8):
                tile = value[:, (t // 4) * 128 : (t // 4) * 128 + 128]
                near = pltpu.roll(tile, (128 - 32 * (t % 4)) % 128, 1)
                far = pltpu.roll(tile, (64 - 16 - 32 * (t % 4)) % 128, 1)
                old = corner_ref[s, :, pl.ds(t * 128, 128)]
                new = jnp.where(lane < 16, near, jnp.where((lane >= 64) & (lane < 80), far, old))
                corner_ref[s, :, pl.ds(t * 128, 128)] = new
            pltpu.make_async_copy(corner_ref.at[s], window(s), out_sem.at[s]).start()

    for s in range(slots):

        @pl.when(s < index_ref[1])
        def _():
            pltpu.make_async_copy(corner_ref.at[s], window(s), out_sem.at[s]).wait()


def coarse_call(index, pieces, fine):
    slots, edge, plane = fine.shape
    m32, m16, m8 = pass_matrix(32), pass_matrix(16), pass_matrix(8)
    deep = np.zeros((16, 16))
    deep[:8] = m8 @ m16[:8]
    eye8, eye16 = np.eye(8), np.eye(16)
    wz = np.zeros((256, 256))
    for cz in range(2):
        for tz in range(2):
            wz[cz * 128 : cz * 128 + 128, tz * 128 : tz * 128 + 128] = np.kron(
                eye8, m32[tz * 16 : tz * 16 + 16, cz * 16 : cz * 16 + 16].T
            )
    w23 = np.concatenate([np.kron(m16.T, m16.T), np.kron(deep.T, deep.T)[:, :128]], 1)
    weights = [
        left_terms(m32),
        *two_terms(wz),
        *two_terms(np.kron(m32.T, eye16)),
        *two_terms(w23),
        left_terms(m16),
        left_terms(deep),
    ]
    anywhere = pl.BlockSpec(memory_space=pl.ANY)
    vmem = pl.BlockSpec(memory_space=pltpu.VMEM)
    return pl.pallas_call(
        coarse_kernel,
        in_specs=[pl.BlockSpec(memory_space=pltpu.SMEM), vmem] + [vmem] * len(weights) + [anywhere],
        out_specs=anywhere,
        out_shape=jax.ShapeDtypeStruct(fine.shape, F32),
        scratch_shapes=[
            pltpu.VMEM((16, 16, 256), F32),
            pltpu.VMEM((slots, 16, 1024), F32),
            pltpu.SemaphoreType.DMA((slots,)),
            pltpu.SemaphoreType.DMA((slots,)),
        ],
        input_output_aliases={2 + len(weights): 0},
        compiler_params=pltpu.CompilerParams(vmem_limit_bytes=VMEM_SMALL),
        name="coarse",
    )(index, pieces.reshape(-1, 128), *weights, fine)


def exchange(lowpass, slots, token):
    me = lax.axis_index(AXES)
    devices = lax.axis_size(AXES)
    if devices == lowpass.shape[0]:
        got = lax.all_to_all(lowpass, AXES, 0, 0, tiled=True)
        sent, index = route_call(me.reshape(1), got, token, slots)
        return lax.all_to_all(sent, AXES, 0, 0, tiled=True), index
    every = lax.all_gather(lowpass, AXES, axis=0)
    counts = every[:, 0, 7, 0].astype(jnp.int32)
    starts = jnp.cumsum(counts) - counts
    blocks = starts[me] // 8 * 8 + jnp.arange(16, dtype=jnp.int32)
    owners = jnp.sum((starts[None, :] <= blocks[:, None]).astype(jnp.int32), axis=1) - 1
    place = jnp.minimum(blocks - starts[owners], slots - 1)
    pieces = jnp.transpose(every[owners, :, place], (1, 0, 2))
    return pieces, jnp.stack([starts[me] % 8, counts[me]])


def per_device(density, owner_counts):
    slots = density.shape[0]
    early = slots // 3
    lowpass, token = lowpass_call(owner_counts, density)
    fine, token = fine_call(owner_counts, token, density, 0, early)
    pieces, index = exchange(lowpass, slots, token)
    fine, _ = fine_call(owner_counts, index, density, early, slots, fine)
    return coarse_call(index, pieces, fine)


def solution(mesh):
    in_specs = (P(AXES, None, None), P(AXES))
    out_specs = P(AXES, None, None)
    return jax.shard_map(per_device, mesh=mesh, in_specs=in_specs, out_specs=out_specs, check_vma=False)
```

```python
import functools

import jax
import jax.numpy as jnp
import numpy as np
from jax import lax
from jax.experimental import pallas as pl
from jax.experimental.pallas import tpu as pltpu
from jax.sharding import PartitionSpec as P

ALPHA = -1.586134342059924
BETA = -0.052980118572961
GAMMA = 0.882911075530934
DELTA = 0.443506852043971
SCALE = 1.230174104914001
SQUARE = SCALE * SCALE
F32 = jnp.float32
BF16 = jnp.bfloat16
AXES = ("node", "dev")
SWAPPED = ("dev", "node")
MIB = 1 << 20
VMEM_LIMIT = 48 * MIB
VMEM_SMALL = 16 * MIB
VMEM_LARGE = 56 * MIB


def pass_matrix(n):
    low, high = np.eye(n)[0::2], np.eye(n)[1::2]

    def after(v):
        return np.concatenate([v[1:], v[-1:]], 0)

    def before(v):
        return np.concatenate([v[:1], v[:-1]], 0)

    high = high + ALPHA * (low + after(low))
    low = low + BETA * (before(high) + high)
    high = high + GAMMA * (low + after(low))
    low = low + DELTA * (before(high) + high)
    return np.concatenate([low / SCALE, high * SCALE], 0)


def two_terms(matrix):
    matrix = np.asarray(matrix, np.float32)
    first = matrix.astype(BF16)
    return first, (matrix - first.astype(np.float32)).astype(BF16)


def left_terms(matrix):
    first, second = two_terms(matrix)
    return np.concatenate([first, second, first], 1)


def split(value):
    first = value.astype(BF16)
    return first, (value - first.astype(F32)).astype(BF16)


def dot(left, right):
    return jnp.dot(left, right, preferred_element_type=F32)


def times(value, first, second):
    high, low = split(value)
    both = dot(jnp.concatenate([high, low], 0), first)
    count = value.shape[0]
    return both[:count] + both[count:] + dot(high, second)


def times_left(terms, value):
    high, low = split(value)
    return dot(terms, jnp.concatenate([high, high, low], 0))


def split_rows(rows):
    return [split(jnp.concatenate(rows[m : m + 2], 0)) for m in range(0, len(rows), 2)]


def start_tiles(src_ref, dst_ref, sems):
    for t in range(dst_ref.shape[2]):
        pltpu.make_async_copy(
            src_ref.at[:, :, pl.ds(t * 128, 128)], dst_ref.at[:, :, t, :], sems.at[t // 8]
        ).start()


def wait_tiles(dst_ref, sems, group):
    part = dst_ref.at[:, :, pl.ds(8 * group, 8), :]
    pltpu.make_async_copy(part, part, sems.at[group]).wait()


def lowpass_kernel(
    count_ref, x_any, wz_any, wyh_any, wyl_any, out_ref, token_ref, x_ref, wz_ref, wyh_ref, wyl_ref, l_ref, z_ref, sems, w_sems
):
    slots, edge = x_any.shape[:2]
    quarter = edge // 4
    rows_all = slots * 8 * quarter
    token_ref[0] = count_ref[0]
    start_tiles(x_any, x_ref, sems)
    weights = [
        pltpu.make_async_copy(src, dst, w_sems.at[i])
        for i, (src, dst) in enumerate(((wz_any, wz_ref), (wyh_any, wyh_ref), (wyl_any, wyl_ref)))
    ]
    for copy in weights:
        copy.start()
    for g in range(4):
        wait_tiles(x_ref, sems, g)

        @pl.loop(0, slots)
        def _(s):
            rows = [x_ref[s, x, pl.ds(8 * g, 8), :] for x in range(edge)]
            rows, _ = lift(rows[0::2], rows[1::2], edge // 2, False, False)
            rows, _ = lift(rows[0::2], rows[1::2], quarter, False, False)
            for m, (high, low) in enumerate(split_rows(rows)):
                at = pl.multiple_of(s * 8 * quarter + 16 * m, 16)
                cols = pl.ds((g % 2) * 256 + (g // 2) * 128, 128)
                l_ref[pl.ds(at, 16), cols] = high
                l_ref[pl.ds(rows_all + at, 16), cols] = low

    for copy in weights:
        copy.wait()
    made = dot(l_ref[...], wz_ref[...])
    z_ref[...] = (made[:rows_all, :128] + made[rows_all:, :128]) + made[:rows_all, 128:]
    wide = jnp.concatenate([z_ref[pl.ds(i, slots * quarter, stride=8), :] for i in range(8)], 1)
    made = times(wide, wyh_ref[...], wyl_ref[...])
    out_ref[...] = jnp.full(out_ref.shape, count_ref[0].astype(F32))
    for slot in range(slots):
        for h in range(2):
            out_ref[pl.ds(8 * h + slot, quarter, stride=16), :] = made[
                slot * quarter : (slot + 1) * quarter, h * 128 : h * 128 + 128
            ]


def stacked(matrix):
    first, second = two_terms(matrix)
    return np.concatenate([first, first, second], 0)


def lowpass_call(owner_counts, density):
    slots, edge, plane = density.shape
    quarter = edge // 4
    two_levels = pass_matrix(edge // 2)[:quarter] @ pass_matrix(edge)[: edge // 2]
    wz = np.concatenate(two_terms(np.kron(np.eye(8), two_levels.T)), 1)
    i, gp, q, p = np.meshgrid(np.arange(8), np.arange(2), np.arange(2), np.arange(2), indexing="ij")
    entry = (2 * (8 * gp + i) + p + 32 * q).reshape(-1)
    wy = np.kron(two_levels.T[entry] / SQUARE, np.eye(quarter))
    wyh, wyl = two_terms(wy)
    anywhere = pl.BlockSpec(memory_space=pl.ANY)
    vmem = pl.BlockSpec(memory_space=pltpu.VMEM)
    rows_all = slots * 8 * quarter
    pieces, token = pl.pallas_call(
        lowpass_kernel,
        in_specs=[pl.BlockSpec(memory_space=pltpu.SMEM)] + [anywhere] * 4,
        out_specs=[vmem, pl.BlockSpec(memory_space=pltpu.SMEM)],
        out_shape=[
            jax.ShapeDtypeStruct((16 * quarter, 128), F32),
            jax.ShapeDtypeStruct((1,), jnp.int32),
        ],
        scratch_shapes=[
            pltpu.VMEM((slots, edge, plane // 128, 128), F32),
            pltpu.VMEM(wz.shape, BF16),
            pltpu.VMEM(wyh.shape, BF16),
            pltpu.VMEM(wyl.shape, BF16),
            pltpu.VMEM((2 * rows_all, 512), BF16),
            pltpu.VMEM((rows_all, 128), F32),
            pltpu.SemaphoreType.DMA((4,)),
            pltpu.SemaphoreType.DMA((3,)),
        ],
        compiler_params=pltpu.CompilerParams(vmem_limit_bytes=VMEM_LARGE),
        name="lowpass",
    )(owner_counts, density, wz, wyh, wyl)
    return pieces.reshape(2 * quarter, 8, 128), token


def route_kernel(
    me_ref, got_ref, _, send_any, index_ref, send_ref, order_ref, count_ref, sem, send_sem, *, width
):
    devices = got_ref.shape[0]
    place = [d % width * (devices // width) + d // width for d in range(devices)]
    copy = pltpu.make_async_copy(got_ref.at[:, 7, :], count_ref, sem)
    copy.start()
    order_ref[...] = jnp.zeros_like(order_ref)
    copy.wait()
    start, my_start, my_count = 0, 0, 0
    starts = []
    for d in range(devices):
        count = count_ref[place[d], 0].astype(jnp.int32)
        starts.append(start)
        my_start = jnp.where(me_ref[0] == d, start, my_start)
        my_count = jnp.where(me_ref[0] == d, count, my_count)
        order_ref[pl.ds(start, 8), :] = got_ref[place[d]]
        start = start + count
    index_ref[0] = my_start % 8
    index_ref[1] = my_count
    copies = []
    for n, d in enumerate(sorted(range(devices), key=lambda d: place[d])):
        at = pl.multiple_of(starts[d] // 8 * 8, 8) if d else 0
        send_ref[n] = order_ref[pl.ds(at, 16), :]
        if n % 8 == 7:
            part = pl.ds(n - 7, 8)
            copies.append(pltpu.make_async_copy(send_ref.at[part], send_any.at[part], send_sem.at[n // 8]))
            copies[-1].start()
    for copy in copies:
        copy.wait()


def route_call(me, got, token, slots, width):
    devices = got.shape[0]
    return pl.pallas_call(
        functools.partial(route_kernel, width=width),
        in_specs=[
            pl.BlockSpec(memory_space=pltpu.SMEM),
            pl.BlockSpec(memory_space=pltpu.VMEM),
            pl.BlockSpec(memory_space=pltpu.SMEM),
        ],
        out_specs=[pl.BlockSpec(memory_space=pl.ANY), pl.BlockSpec(memory_space=pltpu.SMEM)],
        out_shape=[
            jax.ShapeDtypeStruct((devices, 16, 128), F32),
            jax.ShapeDtypeStruct((2,), jnp.int32),
        ],
        scratch_shapes=[
            pltpu.VMEM((devices, 16, 128), F32),
            pltpu.VMEM((devices * slots + 16, 128), F32),
            pltpu.SMEM((devices, 128), F32),
            pltpu.SemaphoreType.DMA,
            pltpu.SemaphoreType.DMA((devices // 8,)),
        ],
        compiler_params=pltpu.CompilerParams(vmem_limit_bytes=VMEM_SMALL),
        name="route",
    )(me, got, token)


def lift(low, high, n, halo, scaled):
    up = SQUARE if scaled else 1.0
    at = 2 if halo else 0
    first, second, third, fourth = ({} for _ in range(4))

    def get(values, i, is_low):
        if halo:
            return values[i]
        return values[min(i, n - 1)] if is_low else values[max(i, 0)]

    lows = {i - at: low[i] for i in range(len(low))}
    highs = {i - at: high[i] for i in range(len(high))}

    def make_first(i):
        first[i] = highs[i] + (ALPHA * up) * (lows[i] + get(lows, i + 1, True))

    def make_second(i):
        second[i] = lows[i] + (BETA / up) * (get(first, i - 1, False) + first[i])

    def make_third(i):
        third[i] = first[i] + (GAMMA * up) * (second[i] + get(second, i + 1, True))

    def make_fourth(i):
        fourth[i] = second[i] + (DELTA / up) * (get(third, i - 1, False) + third[i])

    if halo:
        for i in range(-2, n + 1):
            make_first(i)
            if i >= -1:
                make_second(i)
            if i >= 0:
                make_third(i - 1)
            if i >= 1:
                make_fourth(i - 1)
    else:
        for i in range(n):
            make_first(i)
            make_second(i)
            if i >= 1:
                make_third(i - 1)
                make_fourth(i - 1)
        make_third(n - 1)
        make_fourth(n - 1)
    return [fourth[i] for i in range(n)], [third[i] for i in range(n)]


def fine_kernel(count_ref, _, x_any, w1_ref, w2_ref, *refs, first):
    out_ref, token_ref, x_buf, l_ref, y_ref, c_ref, m_ref, d_ref, sems = refs[-9:]
    step = pl.program_id(0)
    slot = step + first
    edge = x_any.shape[1]
    tiles = x_buf.shape[2]
    pairs = tiles // 2
    half = edge // 2
    corner = 8 * half
    live = slot < count_ref[0]
    lane = lax.broadcasted_iota(jnp.int32, (8, 128), 1)
    front = lane < 64
    inner = (lane & 63) < half
    token_ref[0] = step

    def cross(a, b):
        return pltpu.roll(jnp.where(front, b, a), 64, 1)

    def exchange(a, b):
        crossed = cross(a, b)
        return jnp.where(front, a, crossed), jnp.where(front, crossed, b)

    def with_halo(low, high):
        one, two = cross(low[0], low[-1]), cross(low[1], low[-2])
        low_all = [jnp.where(front, low[2], two), jnp.where(front, low[1], one)] + low
        low_all += [jnp.where(front, one, low[-1]), jnp.where(front, two, low[-2])]
        one, two = cross(high[0], high[-1]), cross(high[1], high[-2])
        high_all = [jnp.where(front, high[1], two), jnp.where(front, high[0], one)] + high
        return low_all, high_all + [jnp.where(front, one, high[-2])]

    def scaled_rows(rows):
        low, high = lift(rows[0::2], rows[1::2], len(rows) // 2, False, False)
        return [v * (1.0 / SCALE) for v in low] + [v * SCALE for v in high]

    def store_terms(ref, row, col, rows):
        for m, (high, low) in enumerate(split_rows(rows)):
            place = pl.ds(pl.multiple_of(row + 16 * m, 16), 16)
            ref[place, pl.ds(col, 128)] = high
            ref[place, pl.ds(256 + col, 128)] = low
            ref[place, pl.ds(512 + col, 128)] = high

    def fetch(which, place):
        for t in range(tiles):
            pltpu.make_async_copy(
                x_any.at[which, :, pl.ds(t * 128, 128)], x_buf.at[place, :, t, :], sems.at[place]
            ).start()

    @pl.when((step == 0) & live)
    def _():
        fetch(slot, 0)

    @pl.when(jnp.logical_not(live))
    def _():
        out_ref[...] = jnp.zeros_like(out_ref)

    @pl.when(live)
    def _():
        x = x_buf.at[step % 2]
        pltpu.make_async_copy(x, x, sems.at[step % 2]).wait()

    @pl.when((step + 1 < pl.num_programs(0)) & (slot + 1 < count_ref[0]))
    def _():
        fetch(slot + 1, (step + 1) % 2)

    @pl.when(live)
    def _():
        x = x_buf.at[step % 2]
        for g in range(4):
            rows = scaled_rows([x[i, pl.ds(8 * g, 8), :] for i in range(edge)])
            store_terms(l_ref, (g % 2) * 8 * edge, (g // 2) * 128, rows)
        lifted = dot(l_ref[...], w1_ref[...])
        y_ref[0] = lifted[:, :128]
        y_ref[1] = lifted[:, 128:]
        for r in range(edge // 8):
            rows = pl.ds(8 * r, 8)

            def tile(part, j):
                return y_ref[part, pl.ds((j // 8) * 8 * edge + 64 * r + j % 8, 8, stride=8), :]

            low = [tile(0, j) for j in range(pairs)]
            high = [tile(1, j) for j in range(pairs)]
            low, high = lift(*with_halo(low, high), pairs, True, True)
            for part, values in enumerate((low, high)):
                for t in range(pairs // 2):
                    a, b = exchange(values[2 * t], values[2 * t + 1])
                    at = part * pairs + t
                    out_ref[0, rows, pl.ds(at * 128, 128)] = a
                    out_ref[0, rows, pl.ds((at + pairs // 2) * 128, 128)] = b
            if r < half // 8:
                low, high = lift(*with_halo(low[0::2], low[1::2]), 8, True, False)
                for i in range(8):
                    c_ref[pl.ds(64 * r + i, 8, stride=8), :] = low[i]
                    c_ref[pl.ds(corner + 64 * r + i, 8, stride=8), :] = high[i]
        for u in range(2):
            rows = scaled_rows([c_ref[pl.ds(u * corner + 8 * i, 8), :] for i in range(half)])
            store_terms(m_ref, 0, u * 128, rows)
        lifted = dot(m_ref[...], w2_ref[...])
        d_ref[0] = lifted[:, :128]
        d_ref[1] = lifted[:, 128:]
        for u in range(2):
            for t in range(4):
                for r in range(half // 8):
                    a = d_ref[u, pl.ds(64 * r + 2 * t, 8, stride=8), :]
                    b = d_ref[u, pl.ds(64 * r + 2 * t + 1, 8, stride=8), :]
                    for at, value in zip((u * 8 + t, u * 8 + 4 + t), exchange(a, b)):
                        rows, cols = pl.ds(8 * r, 8), pl.ds(at * 128, 128)
                        out_ref[0, rows, cols] = jnp.where(inner, value, out_ref[0, rows, cols])


def fine_call(owner_counts, token, density, first, last, before=None):
    slots, edge, plane = density.shape
    tiles = plane // 128
    half = edge // 2
    pairs = tiles // 2
    count = last - first
    one = pass_matrix(edge).T
    zero = np.zeros_like(one)
    w1 = np.block(
        [
            [one / SCALE, zero, zero, zero],
            [zero, zero, one * SCALE, zero],
            [zero, one / SCALE, zero, zero],
            [zero, zero, zero, one * SCALE],
        ]
    )
    two = np.zeros_like(one)
    two[:half, :half] = pass_matrix(half).T
    w2 = np.kron(np.diag([1 / SCALE, 1 / SCALE, SCALE, SCALE]), two)
    anywhere = pl.BlockSpec(memory_space=pl.ANY)
    smem = pl.BlockSpec(memory_space=pltpu.SMEM)
    old = [] if before is None else [before]
    fixed = pl.BlockSpec((768, 256), lambda s: (0, 0))
    return pl.pallas_call(
        functools.partial(fine_kernel, first=first),
        grid=(count,),
        in_specs=[smem, smem, anywhere, fixed, fixed] + [anywhere] * len(old),
        out_specs=[pl.BlockSpec((1, edge, plane), lambda s: (s + first, 0, 0)), smem],
        out_shape=[
            jax.ShapeDtypeStruct(density.shape, F32),
            jax.ShapeDtypeStruct((1,), jnp.int32),
        ],
        scratch_shapes=[
            pltpu.VMEM((2, edge, tiles, 128), F32),
            pltpu.VMEM((pairs * edge, 768), BF16),
            pltpu.VMEM((2, pairs * edge, 128), F32),
            pltpu.VMEM((16 * half, 128), F32),
            pltpu.VMEM((8 * half, 768), BF16),
            pltpu.VMEM((2, 8 * half, 128), F32),
            pltpu.SemaphoreType.DMA((2,)),
        ],
        input_output_aliases={5: 0} if old else {},
        compiler_params=pltpu.CompilerParams(vmem_limit_bytes=VMEM_LIMIT),
        cost_estimate=pl.CostEstimate(
            flops=6 * count * edge * plane * 256, bytes_accessed=2 * count * MIB, transcendentals=0
        ),
        name="fine",
    )(owner_counts, token, density, stacked(w1), stacked(w2), *old)


def coarse_kernel(
    index_ref,
    piece_ref,
    wx_ref,
    wzh_ref,
    wzl_ref,
    wyh_ref,
    wyl_ref,
    w23h_ref,
    w23l_ref,
    wx2_ref,
    wx3_ref,
    fine_ref,
    out_ref,
    block_ref,
    corner_ref,
    corner_sem,
    out_sem,
):
    slots = corner_ref.shape[0]
    lane = lax.broadcasted_iota(jnp.int32, (16, 128), 1)

    def window(s):
        return out_ref.at[s, pl.ds(0, 16), pl.ds(0, 1024)]

    def piece(i):
        return jnp.concatenate([piece_ref[pl.ds(16 * h + i, 16, stride=32), :] for h in range(2)], 1)

    for s in range(slots):
        pltpu.make_async_copy(window(s), corner_ref.at[s], corner_sem.at[s]).start()

    first = [
        [
            times_left(wx_ref[...], jnp.concatenate([piece(o * 8 + 2 * q), piece(o * 8 + 2 * q + 1)], 0))
            for q in range(4)
        ]
        for o in range(2)
    ]
    stacked = []
    for o in range(2):
        for cy in range(2):
            for yh in range(2):
                part = slice(yh * 128, yh * 128 + 128)
                stacked.append(jnp.concatenate([first[o][cy][:, part], first[o][2 + cy][:, part]], 1))
    lifted = times(jnp.concatenate(stacked, 0), wzh_ref[...], wzl_ref[...])
    stacked = []
    for o in range(2):
        for tz in range(2):
            stacked.append(
                jnp.concatenate(
                    [lifted[(o * 4 + u) * 32 : (o * 4 + u + 1) * 32, tz * 128 : tz * 128 + 128] for u in range(4)],
                    1,
                )
            )
    lifted = times(jnp.concatenate(stacked, 0), wyh_ref[...], wyl_ref[...])
    corner = []
    for o in range(2):
        for tz in range(2):
            for ty in range(2):
                for tx in range(2):
                    at = (o * 2 + tz) * 32 + tx * 16
                    value = lifted[at : at + 16, ty * 256 : ty * 256 + 256]
                    if tx + ty + tz == 0:
                        corner.append(value)
                    else:
                        block_ref[o * 8 + tx + 2 * ty + 4 * tz] = value
    both = times(jnp.concatenate(corner, 0), w23h_ref[...], w23l_ref[...])
    depth = lax.broadcasted_iota(jnp.int32, (16, 128), 0)
    small = (depth < 8) & ((lane & 15) < 8)
    for o in range(2):
        mine = both[o * 16 : o * 16 + 16]
        second = times_left(wx2_ref[...], mine[:, :256])
        third = times_left(wx3_ref[...], mine[:, 256:])
        block_ref[o * 8] = jnp.concatenate(
            [jnp.where(small, third, second[:, :128]), second[:, 128:]], 1
        )

    for s in range(slots):
        pltpu.make_async_copy(window(s), corner_ref.at[s], corner_sem.at[s]).wait()
    for s in range(slots):

        @pl.when(s < index_ref[1])
        def _():
            value = block_ref[index_ref[0] + s]
            for t in range(8):
                tile = value[:, (t // 4) * 128 : (t // 4) * 128 + 128]
                near = pltpu.roll(tile, (128 - 32 * (t % 4)) % 128, 1)
                far = pltpu.roll(tile, (64 - 16 - 32 * (t % 4)) % 128, 1)
                old = corner_ref[s, :, pl.ds(t * 128, 128)]
                new = jnp.where(lane < 16, near, jnp.where((lane >= 64) & (lane < 80), far, old))
                corner_ref[s, :, pl.ds(t * 128, 128)] = new
            pltpu.make_async_copy(corner_ref.at[s], window(s), out_sem.at[s]).start()

    for s in range(slots):

        @pl.when(s < index_ref[1])
        def _():
            pltpu.make_async_copy(corner_ref.at[s], window(s), out_sem.at[s]).wait()


def coarse_call(index, pieces, fine):
    slots, edge, plane = fine.shape
    m32, m16, m8 = pass_matrix(32), pass_matrix(16), pass_matrix(8)
    deep = np.zeros((16, 16))
    deep[:8] = m8 @ m16[:8]
    eye8, eye16 = np.eye(8), np.eye(16)
    wz = np.zeros((256, 256))
    for cz in range(2):
        for tz in range(2):
            wz[cz * 128 : cz * 128 + 128, tz * 128 : tz * 128 + 128] = np.kron(
                eye8, m32[tz * 16 : tz * 16 + 16, cz * 16 : cz * 16 + 16].T
            )
    w23 = np.concatenate([np.kron(m16.T, m16.T), np.kron(deep.T, deep.T)[:, :128]], 1)
    weights = [
        left_terms(m32),
        *two_terms(wz),
        *two_terms(np.kron(m32.T, eye16)),
        *two_terms(w23),
        left_terms(m16),
        left_terms(deep),
    ]
    anywhere = pl.BlockSpec(memory_space=pl.ANY)
    vmem = pl.BlockSpec(memory_space=pltpu.VMEM)
    return pl.pallas_call(
        coarse_kernel,
        in_specs=[pl.BlockSpec(memory_space=pltpu.SMEM), vmem] + [vmem] * len(weights) + [anywhere],
        out_specs=anywhere,
        out_shape=jax.ShapeDtypeStruct(fine.shape, F32),
        scratch_shapes=[
            pltpu.VMEM((16, 16, 256), F32),
            pltpu.VMEM((slots, 16, 1024), F32),
            pltpu.SemaphoreType.DMA((slots,)),
            pltpu.SemaphoreType.DMA((slots,)),
        ],
        input_output_aliases={2 + len(weights): 0},
        compiler_params=pltpu.CompilerParams(vmem_limit_bytes=VMEM_SMALL),
        name="coarse",
    )(index, pieces.reshape(-1, 128), *weights, fine)


def exchange(lowpass, slots, token):
    me = lax.axis_index(AXES)
    devices = lax.axis_size(AXES)
    if devices == lowpass.shape[0]:
        got = lax.all_to_all(lowpass, SWAPPED, 0, 0, tiled=True)
        sent, index = route_call(me.reshape(1), got, token, slots, lax.axis_size("dev"))
        return lax.all_to_all(sent, SWAPPED, 0, 0, tiled=True), index
    every = lax.all_gather(lowpass, AXES, axis=0)
    counts = every[:, 0, 7, 0].astype(jnp.int32)
    starts = jnp.cumsum(counts) - counts
    blocks = starts[me] // 8 * 8 + jnp.arange(16, dtype=jnp.int32)
    owners = jnp.sum((starts[None, :] <= blocks[:, None]).astype(jnp.int32), axis=1) - 1
    place = jnp.minimum(blocks - starts[owners], slots - 1)
    pieces = jnp.transpose(every[owners, :, place], (1, 0, 2))
    return pieces, jnp.stack([starts[me] % 8, counts[me]])


def per_device(density, owner_counts):
    slots = density.shape[0]
    early = slots // 3
    lowpass, token = lowpass_call(owner_counts, density)
    fine, token = fine_call(owner_counts, token, density, 0, early)
    pieces, index = exchange(lowpass, slots, token)
    fine, _ = fine_call(owner_counts, index, density, early, slots, fine)
    return coarse_call(index, pieces, fine)


def solution(mesh):
    in_specs = (P(AXES, None, None), P(AXES))
    out_specs = P(AXES, None, None)
    return jax.shard_map(per_device, mesh=mesh, in_specs=in_specs, out_specs=out_specs, check_vma=False)
```

```python
import functools

import jax
import jax.numpy as jnp
import numpy as np
from jax import lax
from jax.experimental import pallas as pl
from jax.experimental.pallas import tpu as pltpu
from jax.sharding import PartitionSpec as P

ALPHA = -1.586134342059924
BETA = -0.052980118572961
GAMMA = 0.882911075530934
DELTA = 0.443506852043971
SCALE = 1.230174104914001
SQUARE = SCALE * SCALE
F32 = jnp.float32
BF16 = jnp.bfloat16
AXES = ("node", "dev")
SWAPPED = ("dev", "node")
MIB = 1 << 20
VMEM_LIMIT = 48 * MIB
VMEM_SMALL = 16 * MIB
VMEM_LARGE = 56 * MIB


def pass_matrix(n):
    low, high = np.eye(n)[0::2], np.eye(n)[1::2]

    def after(v):
        return np.concatenate([v[1:], v[-1:]], 0)

    def before(v):
        return np.concatenate([v[:1], v[:-1]], 0)

    high = high + ALPHA * (low + after(low))
    low = low + BETA * (before(high) + high)
    high = high + GAMMA * (low + after(low))
    low = low + DELTA * (before(high) + high)
    return np.concatenate([low / SCALE, high * SCALE], 0)


def two_terms(matrix):
    matrix = np.asarray(matrix, np.float32)
    first = matrix.astype(BF16)
    return first, (matrix - first.astype(np.float32)).astype(BF16)


def left_terms(matrix):
    first, second = two_terms(matrix)
    return np.concatenate([first, second, first], 1)


def split(value):
    first = value.astype(BF16)
    return first, (value - first.astype(F32)).astype(BF16)


def dot(left, right):
    return jnp.dot(left, right, preferred_element_type=F32)


def times(value, first, second):
    high, low = split(value)
    both = dot(jnp.concatenate([high, low], 0), first)
    count = value.shape[0]
    return both[:count] + both[count:] + dot(high, second)


def times_left(terms, value):
    high, low = split(value)
    return dot(terms, jnp.concatenate([high, high, low], 0))


def split_rows(rows):
    return [split(jnp.concatenate(rows[m : m + 2], 0)) for m in range(0, len(rows), 2)]


def start_tiles(src_ref, dst_ref, sems):
    for t in range(dst_ref.shape[2]):
        pltpu.make_async_copy(
            src_ref.at[:, :, pl.ds(t * 128, 128)], dst_ref.at[:, :, t, :], sems.at[t // 8]
        ).start(priority=t % 2)


def wait_tiles(dst_ref, sems, group):
    part = dst_ref.at[:, :, pl.ds(8 * group, 8), :]
    pltpu.make_async_copy(part, part, sems.at[group]).wait()


def lowpass_kernel(
    count_ref, x_any, wz_any, wyh_any, wyl_any, out_ref, token_ref, x_ref, wz_ref, wyh_ref, wyl_ref, l_ref, z_ref, sems, w_sems
):
    slots, edge = x_any.shape[:2]
    quarter = edge // 4
    rows_all = slots * 8 * quarter
    token_ref[0] = count_ref[0]
    start_tiles(x_any, x_ref, sems)
    weights = [
        pltpu.make_async_copy(src, dst, w_sems.at[i])
        for i, (src, dst) in enumerate(((wz_any, wz_ref), (wyh_any, wyh_ref), (wyl_any, wyl_ref)))
    ]
    for i, copy in enumerate(weights):
        copy.start(priority=i % 2)
    for g in range(4):
        wait_tiles(x_ref, sems, g)

        @pl.loop(0, slots)
        def _(s):
            rows = [x_ref[s, x, pl.ds(8 * g, 8), :] for x in range(edge)]
            rows, _ = lift(rows[0::2], rows[1::2], edge // 2, False, False)
            rows, _ = lift(rows[0::2], rows[1::2], quarter, False, False)
            for m, (high, low) in enumerate(split_rows(rows)):
                at = pl.multiple_of(s * 8 * quarter + 16 * m, 16)
                cols = pl.ds((g % 2) * 256 + (g // 2) * 128, 128)
                l_ref[pl.ds(at, 16), cols] = high
                l_ref[pl.ds(rows_all + at, 16), cols] = low

    for copy in weights:
        copy.wait()
    made = dot(l_ref[...], wz_ref[...])
    z_ref[...] = (made[:rows_all, :128] + made[rows_all:, :128]) + made[:rows_all, 128:]
    wide = jnp.concatenate([z_ref[pl.ds(i, slots * quarter, stride=8), :] for i in range(8)], 1)
    made = times(wide, wyh_ref[...], wyl_ref[...])
    out_ref[...] = jnp.full(out_ref.shape, count_ref[0].astype(F32))
    for slot in range(slots):
        for h in range(2):
            out_ref[pl.ds(8 * h + slot, quarter, stride=16), :] = made[
                slot * quarter : (slot + 1) * quarter, h * 128 : h * 128 + 128
            ]


def stacked(matrix):
    first, second = two_terms(matrix)
    return np.concatenate([first, first, second], 0)


def lowpass_call(owner_counts, density):
    slots, edge, plane = density.shape
    quarter = edge // 4
    two_levels = pass_matrix(edge // 2)[:quarter] @ pass_matrix(edge)[: edge // 2]
    wz = np.concatenate(two_terms(np.kron(np.eye(8), two_levels.T)), 1)
    i, gp, q, p = np.meshgrid(np.arange(8), np.arange(2), np.arange(2), np.arange(2), indexing="ij")
    entry = (2 * (8 * gp + i) + p + 32 * q).reshape(-1)
    wy = np.kron(two_levels.T[entry] / SQUARE, np.eye(quarter))
    wyh, wyl = two_terms(wy)
    anywhere = pl.BlockSpec(memory_space=pl.ANY)
    vmem = pl.BlockSpec(memory_space=pltpu.VMEM)
    rows_all = slots * 8 * quarter
    pieces, token = pl.pallas_call(
        lowpass_kernel,
        in_specs=[pl.BlockSpec(memory_space=pltpu.SMEM)] + [anywhere] * 4,
        out_specs=[vmem, pl.BlockSpec(memory_space=pltpu.SMEM)],
        out_shape=[
            jax.ShapeDtypeStruct((16 * quarter, 128), F32),
            jax.ShapeDtypeStruct((1,), jnp.int32),
        ],
        scratch_shapes=[
            pltpu.VMEM((slots, edge, plane // 128, 128), F32),
            pltpu.VMEM(wz.shape, BF16),
            pltpu.VMEM(wyh.shape, BF16),
            pltpu.VMEM(wyl.shape, BF16),
            pltpu.VMEM((2 * rows_all, 512), BF16),
            pltpu.VMEM((rows_all, 128), F32),
            pltpu.SemaphoreType.DMA((4,)),
            pltpu.SemaphoreType.DMA((3,)),
        ],
        compiler_params=pltpu.CompilerParams(vmem_limit_bytes=VMEM_LARGE),
        name="lowpass",
    )(owner_counts, density, wz, wyh, wyl)
    return pieces.reshape(2 * quarter, 8, 128), token


def route_kernel(me_ref, got_ref, _, send_ref, index_ref, order_ref, count_ref, sem, *, width):
    devices = got_ref.shape[0]
    place = [d % width * (devices // width) + d // width for d in range(devices)]
    copy = pltpu.make_async_copy(got_ref.at[:, 7, :], count_ref, sem)
    copy.start()
    order_ref[...] = jnp.zeros_like(order_ref)
    copy.wait()
    start, my_start, my_count = 0, 0, 0
    starts = []
    for d in range(devices):
        count = count_ref[place[d], 0].astype(jnp.int32)
        starts.append(start)
        my_start = jnp.where(me_ref[0] == d, start, my_start)
        my_count = jnp.where(me_ref[0] == d, count, my_count)
        order_ref[pl.ds(start, 8), :] = got_ref[place[d]]
        start = start + count
    index_ref[0] = my_start % 8
    index_ref[1] = my_count
    for d in range(devices):
        at = pl.multiple_of(starts[d] // 8 * 8, 8) if d else 0
        send_ref[place[d]] = order_ref[pl.ds(at, 16), :]


def route_call(me, got, token, slots, width):
    devices = got.shape[0]
    return pl.pallas_call(
        functools.partial(route_kernel, width=width),
        in_specs=[
            pl.BlockSpec(memory_space=pltpu.SMEM),
            pl.BlockSpec(memory_space=pltpu.VMEM),
            pl.BlockSpec(memory_space=pltpu.SMEM),
        ],
        out_specs=[pl.BlockSpec(memory_space=pltpu.VMEM), pl.BlockSpec(memory_space=pltpu.SMEM)],
        out_shape=[
            jax.ShapeDtypeStruct((devices, 16, 128), F32),
            jax.ShapeDtypeStruct((2,), jnp.int32),
        ],
        scratch_shapes=[
            pltpu.VMEM((devices * slots + 16, 128), F32),
            pltpu.SMEM((devices, 128), F32),
            pltpu.SemaphoreType.DMA,
        ],
        compiler_params=pltpu.CompilerParams(vmem_limit_bytes=VMEM_SMALL),
        name="route",
    )(me, got, token)


def lift(low, high, n, halo, scaled):
    up = SQUARE if scaled else 1.0
    at = 2 if halo else 0
    first, second, third, fourth = ({} for _ in range(4))

    def get(values, i, is_low):
        if halo:
            return values[i]
        return values[min(i, n - 1)] if is_low else values[max(i, 0)]

    lows = {i - at: low[i] for i in range(len(low))}
    highs = {i - at: high[i] for i in range(len(high))}

    def make_first(i):
        first[i] = highs[i] + (ALPHA * up) * (lows[i] + get(lows, i + 1, True))

    def make_second(i):
        second[i] = lows[i] + (BETA / up) * (get(first, i - 1, False) + first[i])

    def make_third(i):
        third[i] = first[i] + (GAMMA * up) * (second[i] + get(second, i + 1, True))

    def make_fourth(i):
        fourth[i] = second[i] + (DELTA / up) * (get(third, i - 1, False) + third[i])

    if halo:
        for i in range(-2, n + 1):
            make_first(i)
            if i >= -1:
                make_second(i)
            if i >= 0:
                make_third(i - 1)
            if i >= 1:
                make_fourth(i - 1)
    else:
        for i in range(n):
            make_first(i)
            make_second(i)
            if i >= 1:
                make_third(i - 1)
                make_fourth(i - 1)
        make_third(n - 1)
        make_fourth(n - 1)
    return [fourth[i] for i in range(n)], [third[i] for i in range(n)]


def fine_kernel(count_ref, _, x_any, w1_ref, w2_ref, *refs, first):
    out_ref, token_ref, x_buf, l_ref, y_ref, c_ref, m_ref, d_ref, sems = refs[-9:]
    step = pl.program_id(0)
    slot = step + first
    edge = x_any.shape[1]
    tiles = x_buf.shape[2]
    pairs = tiles // 2
    half = edge // 2
    corner = 8 * half
    live = slot < count_ref[0]
    lane = lax.broadcasted_iota(jnp.int32, (8, 128), 1)
    front = lane < 64
    inner = (lane & 63) < half
    token_ref[0] = step

    def cross(a, b):
        return pltpu.roll(jnp.where(front, b, a), 64, 1)

    def exchange(a, b):
        crossed = cross(a, b)
        return jnp.where(front, a, crossed), jnp.where(front, crossed, b)

    def with_halo(low, high):
        one, two = cross(low[0], low[-1]), cross(low[1], low[-2])
        low_all = [jnp.where(front, low[2], two), jnp.where(front, low[1], one)] + low
        low_all += [jnp.where(front, one, low[-1]), jnp.where(front, two, low[-2])]
        one, two = cross(high[0], high[-1]), cross(high[1], high[-2])
        high_all = [jnp.where(front, high[1], two), jnp.where(front, high[0], one)] + high
        return low_all, high_all + [jnp.where(front, one, high[-2])]

    def scaled_rows(rows):
        low, high = lift(rows[0::2], rows[1::2], len(rows) // 2, False, False)
        return [v * (1.0 / SCALE) for v in low] + [v * SCALE for v in high]

    def store_terms(ref, row, col, rows):
        for m, (high, low) in enumerate(split_rows(rows)):
            place = pl.ds(pl.multiple_of(row + 16 * m, 16), 16)
            ref[place, pl.ds(col, 128)] = high
            ref[place, pl.ds(256 + col, 128)] = low
            ref[place, pl.ds(512 + col, 128)] = high

    def fetch(which, place):
        for t in range(tiles):
            pltpu.make_async_copy(
                x_any.at[which, :, pl.ds(t * 128, 128)], x_buf.at[place, :, t, :], sems.at[place]
            ).start(priority=t % 2)

    @pl.when((step == 0) & live)
    def _():
        fetch(slot, 0)

    @pl.when(jnp.logical_not(live))
    def _():
        out_ref[...] = jnp.zeros_like(out_ref)

    @pl.when(live)
    def _():
        x = x_buf.at[step % 2]
        pltpu.make_async_copy(x, x, sems.at[step % 2]).wait()

    @pl.when((step + 1 < pl.num_programs(0)) & (slot + 1 < count_ref[0]))
    def _():
        fetch(slot + 1, (step + 1) % 2)

    @pl.when(live)
    def _():
        x = x_buf.at[step % 2]
        @pl.loop(0, 4)
        def _(g):
            rows = scaled_rows([x[i, pl.ds(pl.multiple_of(8 * g, 8), 8), :] for i in range(edge)])
            store_terms(l_ref, (g % 2) * 8 * edge, pl.multiple_of((g // 2) * 128, 128), rows)

        lifted = dot(l_ref[...], w1_ref[...])
        y_ref[0] = lifted[:, :128]
        y_ref[1] = lifted[:, 128:]
        def second(r, deeper):
            rows = pl.ds(pl.multiple_of(8 * r, 8), 8)

            def tile(part, j):
                return y_ref[part, pl.ds((j // 8) * 8 * edge + 64 * r + j % 8, 8, stride=8), :]

            low = [tile(0, j) for j in range(pairs)]
            high = [tile(1, j) for j in range(pairs)]
            low, high = lift(*with_halo(low, high), pairs, True, True)
            for part, values in enumerate((low, high)):
                for t in range(pairs // 2):
                    a, b = exchange(values[2 * t], values[2 * t + 1])
                    at = part * pairs + t
                    out_ref[0, rows, pl.ds(at * 128, 128)] = a
                    out_ref[0, rows, pl.ds((at + pairs // 2) * 128, 128)] = b
            if deeper:
                low, high = lift(*with_halo(low[0::2], low[1::2]), 8, True, False)
                for i in range(8):
                    c_ref[pl.ds(64 * r + i, 8, stride=8), :] = low[i]
                    c_ref[pl.ds(corner + 64 * r + i, 8, stride=8), :] = high[i]

        for deeper in (True, False):

            @pl.loop(0, half // 16)
            def _(q):
                for u in range(2):
                    second(2 * q + u + (0 if deeper else half // 8), deeper)

        for u in range(2):
            rows = scaled_rows([c_ref[pl.ds(u * corner + 8 * i, 8), :] for i in range(half)])
            store_terms(m_ref, 0, u * 128, rows)
        lifted = dot(m_ref[...], w2_ref[...])
        d_ref[0] = lifted[:, :128]
        d_ref[1] = lifted[:, 128:]
        for u in range(2):
            for t in range(4):
                for r in range(half // 8):
                    a = d_ref[u, pl.ds(64 * r + 2 * t, 8, stride=8), :]
                    b = d_ref[u, pl.ds(64 * r + 2 * t + 1, 8, stride=8), :]
                    for at, value in zip((u * 8 + t, u * 8 + 4 + t), exchange(a, b)):
                        rows, cols = pl.ds(8 * r, 8), pl.ds(at * 128, 128)
                        out_ref[0, rows, cols] = jnp.where(inner, value, out_ref[0, rows, cols])


def fine_call(owner_counts, token, density, first, last, before=None):
    slots, edge, plane = density.shape
    tiles = plane // 128
    half = edge // 2
    pairs = tiles // 2
    count = last - first
    one = pass_matrix(edge).T
    zero = np.zeros_like(one)
    w1 = np.block(
        [
            [one / SCALE, zero, zero, zero],
            [zero, zero, one * SCALE, zero],
            [zero, one / SCALE, zero, zero],
            [zero, zero, zero, one * SCALE],
        ]
    )
    two = np.zeros_like(one)
    two[:half, :half] = pass_matrix(half).T
    w2 = np.kron(np.diag([1 / SCALE, 1 / SCALE, SCALE, SCALE]), two)
    anywhere = pl.BlockSpec(memory_space=pl.ANY)
    smem = pl.BlockSpec(memory_space=pltpu.SMEM)
    old = [] if before is None else [before]
    fixed = pl.BlockSpec((768, 256), lambda s: (0, 0))
    return pl.pallas_call(
        functools.partial(fine_kernel, first=first),
        grid=(count,),
        in_specs=[smem, smem, anywhere, fixed, fixed] + [anywhere] * len(old),
        out_specs=[pl.BlockSpec((1, edge, plane), lambda s: (s + first, 0, 0)), smem],
        out_shape=[
            jax.ShapeDtypeStruct(density.shape, F32),
            jax.ShapeDtypeStruct((1,), jnp.int32),
        ],
        scratch_shapes=[
            pltpu.VMEM((2, edge, tiles, 128), F32),
            pltpu.VMEM((pairs * edge, 768), BF16),
            pltpu.VMEM((2, pairs * edge, 128), F32),
            pltpu.VMEM((16 * half, 128), F32),
            pltpu.VMEM((8 * half, 768), BF16),
            pltpu.VMEM((2, 8 * half, 128), F32),
            pltpu.SemaphoreType.DMA((2,)),
        ],
        input_output_aliases={5: 0} if old else {},
        compiler_params=pltpu.CompilerParams(vmem_limit_bytes=VMEM_LIMIT),
        cost_estimate=pl.CostEstimate(
            flops=6 * count * edge * plane * 256, bytes_accessed=2 * count * MIB, transcendentals=0
        ),
        name="fine",
    )(owner_counts, token, density, stacked(w1), stacked(w2), *old)


def coarse_kernel(
    index_ref,
    piece_ref,
    wx_ref,
    wzh_ref,
    wzl_ref,
    wyh_ref,
    wyl_ref,
    w23h_ref,
    w23l_ref,
    wx2_ref,
    wx3_ref,
    fine_ref,
    out_ref,
    block_ref,
    corner_ref,
    corner_sem,
    out_sem,
):
    slots = corner_ref.shape[0]
    lane = lax.broadcasted_iota(jnp.int32, (16, 128), 1)

    def window(s):
        return out_ref.at[s, pl.ds(0, 16), pl.ds(0, 1024)]

    def piece(i):
        return jnp.concatenate([piece_ref[pl.ds(16 * h + i, 16, stride=32), :] for h in range(2)], 1)

    for s in range(slots):
        pltpu.make_async_copy(window(s), corner_ref.at[s], corner_sem.at[s]).start(priority=s % 2)

    first = [
        [
            times_left(wx_ref[...], jnp.concatenate([piece(o * 8 + 2 * q), piece(o * 8 + 2 * q + 1)], 0))
            for q in range(4)
        ]
        for o in range(2)
    ]
    stacked = []
    for o in range(2):
        for cy in range(2):
            for yh in range(2):
                part = slice(yh * 128, yh * 128 + 128)
                stacked.append(jnp.concatenate([first[o][cy][:, part], first[o][2 + cy][:, part]], 1))
    lifted = times(jnp.concatenate(stacked, 0), wzh_ref[...], wzl_ref[...])
    stacked = []
    for o in range(2):
        for tz in range(2):
            stacked.append(
                jnp.concatenate(
                    [lifted[(o * 4 + u) * 32 : (o * 4 + u + 1) * 32, tz * 128 : tz * 128 + 128] for u in range(4)],
                    1,
                )
            )
    lifted = times(jnp.concatenate(stacked, 0), wyh_ref[...], wyl_ref[...])
    corner = []
    for o in range(2):
        for tz in range(2):
            for ty in range(2):
                for tx in range(2):
                    at = (o * 2 + tz) * 32 + tx * 16
                    value = lifted[at : at + 16, ty * 256 : ty * 256 + 256]
                    if tx + ty + tz == 0:
                        corner.append(value)
                    else:
                        block_ref[o * 8 + tx + 2 * ty + 4 * tz] = value
    both = times(jnp.concatenate(corner, 0), w23h_ref[...], w23l_ref[...])
    depth = lax.broadcasted_iota(jnp.int32, (16, 128), 0)
    small = (depth < 8) & ((lane & 15) < 8)
    for o in range(2):
        mine = both[o * 16 : o * 16 + 16]
        second = times_left(wx2_ref[...], mine[:, :256])
        third = times_left(wx3_ref[...], mine[:, 256:])
        block_ref[o * 8] = jnp.concatenate(
            [jnp.where(small, third, second[:, :128]), second[:, 128:]], 1
        )

    for s in range(slots):
        pltpu.make_async_copy(window(s), corner_ref.at[s], corner_sem.at[s]).wait()
    for s in range(slots):

        @pl.when(s < index_ref[1])
        def _():
            value = block_ref[index_ref[0] + s]
            for t in range(8):
                tile = value[:, (t // 4) * 128 : (t // 4) * 128 + 128]
                near = pltpu.roll(tile, (128 - 32 * (t % 4)) % 128, 1)
                far = pltpu.roll(tile, (64 - 16 - 32 * (t % 4)) % 128, 1)
                old = corner_ref[s, :, pl.ds(t * 128, 128)]
                new = jnp.where(lane < 16, near, jnp.where((lane >= 64) & (lane < 80), far, old))
                corner_ref[s, :, pl.ds(t * 128, 128)] = new
            pltpu.make_async_copy(corner_ref.at[s], window(s), out_sem.at[s]).start(priority=s % 2)

    for s in range(slots):

        @pl.when(s < index_ref[1])
        def _():
            pltpu.make_async_copy(corner_ref.at[s], window(s), out_sem.at[s]).wait()


def coarse_call(index, pieces, fine):
    slots, edge, plane = fine.shape
    m32, m16, m8 = pass_matrix(32), pass_matrix(16), pass_matrix(8)
    deep = np.zeros((16, 16))
    deep[:8] = m8 @ m16[:8]
    eye8, eye16 = np.eye(8), np.eye(16)
    wz = np.zeros((256, 256))
    for cz in range(2):
        for tz in range(2):
            wz[cz * 128 : cz * 128 + 128, tz * 128 : tz * 128 + 128] = np.kron(
                eye8, m32[tz * 16 : tz * 16 + 16, cz * 16 : cz * 16 + 16].T
            )
    w23 = np.concatenate([np.kron(m16.T, m16.T), np.kron(deep.T, deep.T)[:, :128]], 1)
    weights = [
        left_terms(m32),
        *two_terms(wz),
        *two_terms(np.kron(m32.T, eye16)),
        *two_terms(w23),
        left_terms(m16),
        left_terms(deep),
    ]
    anywhere = pl.BlockSpec(memory_space=pl.ANY)
    vmem = pl.BlockSpec(memory_space=pltpu.VMEM)
    return pl.pallas_call(
        coarse_kernel,
        in_specs=[pl.BlockSpec(memory_space=pltpu.SMEM), vmem] + [vmem] * len(weights) + [anywhere],
        out_specs=anywhere,
        out_shape=jax.ShapeDtypeStruct(fine.shape, F32),
        scratch_shapes=[
            pltpu.VMEM((16, 16, 256), F32),
            pltpu.VMEM((slots, 16, 1024), F32),
            pltpu.SemaphoreType.DMA((slots,)),
            pltpu.SemaphoreType.DMA((slots,)),
        ],
        input_output_aliases={2 + len(weights): 0},
        compiler_params=pltpu.CompilerParams(vmem_limit_bytes=VMEM_SMALL),
        name="coarse",
    )(index, pieces.reshape(-1, 128), *weights, fine)


def exchange(lowpass, slots, token):
    me = lax.axis_index(AXES)
    devices = lax.axis_size(AXES)
    if devices == lowpass.shape[0]:
        got = lax.all_to_all(lowpass, SWAPPED, 0, 0, tiled=True)
        sent, index = route_call(me.reshape(1), got, token, slots, lax.axis_size("dev"))
        return lax.all_to_all(sent, SWAPPED, 0, 0, tiled=True), index
    every = lax.all_gather(lowpass, AXES, axis=0)
    counts = every[:, 0, 7, 0].astype(jnp.int32)
    starts = jnp.cumsum(counts) - counts
    blocks = starts[me] // 8 * 8 + jnp.arange(16, dtype=jnp.int32)
    owners = jnp.sum((starts[None, :] <= blocks[:, None]).astype(jnp.int32), axis=1) - 1
    place = jnp.minimum(blocks - starts[owners], slots - 1)
    pieces = jnp.transpose(every[owners, :, place], (1, 0, 2))
    return pieces, jnp.stack([starts[me] % 8, counts[me]])


def per_device(density, owner_counts):
    slots = density.shape[0]
    early = slots // 3
    lowpass, token = lowpass_call(owner_counts, density)
    fine, token = fine_call(owner_counts, token, density, 0, early)
    pieces, index = exchange(lowpass, slots, token)
    fine, _ = fine_call(owner_counts, index, density, early, slots, fine)
    return coarse_call(index, pieces, fine)


def solution(mesh):
    in_specs = (P(AXES, None, None), P(AXES))
    out_specs = P(AXES, None, None)
    return jax.shard_map(per_device, mesh=mesh, in_specs=in_specs, out_specs=out_specs, check_vma=False)
```

```python
import functools

import jax
import jax.numpy as jnp
import numpy as np
from jax import lax
from jax.experimental import pallas as pl
from jax.experimental.pallas import tpu as pltpu
from jax.sharding import PartitionSpec as P

ALPHA = -1.586134342059924
BETA = -0.052980118572961
GAMMA = 0.882911075530934
DELTA = 0.443506852043971
SCALE = 1.230174104914001
SQUARE = SCALE * SCALE
F32 = jnp.float32
BF16 = jnp.bfloat16
AXES = ("node", "dev")
SWAPPED = ("dev", "node")
MIB = 1 << 20
VMEM_LIMIT = 48 * MIB
VMEM_SMALL = 16 * MIB
VMEM_LARGE = 56 * MIB


def pass_matrix(n):
    low, high = np.eye(n)[0::2], np.eye(n)[1::2]

    def after(v):
        return np.concatenate([v[1:], v[-1:]], 0)

    def before(v):
        return np.concatenate([v[:1], v[:-1]], 0)

    high = high + ALPHA * (low + after(low))
    low = low + BETA * (before(high) + high)
    high = high + GAMMA * (low + after(low))
    low = low + DELTA * (before(high) + high)
    return np.concatenate([low / SCALE, high * SCALE], 0)


def two_terms(matrix):
    matrix = np.asarray(matrix, np.float32)
    first = matrix.astype(BF16)
    return first, (matrix - first.astype(np.float32)).astype(BF16)


def left_terms(matrix):
    first, second = two_terms(matrix)
    return np.concatenate([first, second, first], 1)


def split(value):
    first = value.astype(BF16)
    return first, (value - first.astype(F32)).astype(BF16)


def dot(left, right):
    return jnp.dot(left, right, preferred_element_type=F32)


def times(value, first, second):
    high, low = split(value)
    both = dot(jnp.concatenate([high, low], 0), first)
    count = value.shape[0]
    return both[:count] + both[count:] + dot(high, second)


def times_left(terms, value):
    high, low = split(value)
    return dot(terms, jnp.concatenate([high, high, low], 0))


def split_rows(rows):
    return [split(jnp.concatenate(rows[m : m + 2], 0)) for m in range(0, len(rows), 2)]


def start_tiles(src_ref, dst_ref, sems):
    for t in range(dst_ref.shape[2]):
        pltpu.make_async_copy(
            src_ref.at[:, :, pl.ds(t * 128, 128)], dst_ref.at[:, :, t, :], sems.at[t // 8]
        ).start()


def wait_tiles(dst_ref, sems, group):
    part = dst_ref.at[:, :, pl.ds(8 * group, 8), :]
    pltpu.make_async_copy(part, part, sems.at[group]).wait()


def lowpass_kernel(
    count_ref, x_any, wz_any, wyh_any, wyl_any, out_ref, token_ref, x_ref, wz_ref, wyh_ref, wyl_ref, l_ref, z_ref, sems, w_sems
):
    slots, edge = x_any.shape[:2]
    quarter = edge // 4
    rows_all = slots * 8 * quarter
    token_ref[0] = count_ref[0]
    start_tiles(x_any, x_ref, sems)
    weights = [
        pltpu.make_async_copy(src, dst, w_sems.at[i])
        for i, (src, dst) in enumerate(((wz_any, wz_ref), (wyh_any, wyh_ref), (wyl_any, wyl_ref)))
    ]
    for copy in weights:
        copy.start()
    for g in range(4):
        wait_tiles(x_ref, sems, g)

        def first_dimension(s):
            rows = [x_ref[s, x, pl.ds(8 * g, 8), :] for x in range(edge)]
            rows, _ = lift(rows[0::2], rows[1::2], edge // 2, False, False)
            rows, _ = lift(rows[0::2], rows[1::2], quarter, False, False)
            for m, (high, low) in enumerate(split_rows(rows)):
                at = pl.multiple_of(s * 8 * quarter + 16 * m, 16)
                cols = pl.ds((g % 2) * 256 + (g // 2) * 128, 128)
                l_ref[pl.ds(at, 16), cols] = high
                l_ref[pl.ds(rows_all + at, 16), cols] = low

        together = 3 if slots % 3 == 0 else 1

        @pl.loop(0, slots // together)
        def _(n):
            for u in range(together):
                first_dimension(n * together + u)

    for copy in weights:
        copy.wait()
    made = dot(l_ref[...], wz_ref[...])
    z_ref[...] = (made[:rows_all, :128] + made[rows_all:, :128]) + made[:rows_all, 128:]
    wide = jnp.concatenate([z_ref[pl.ds(i, slots * quarter, stride=8), :] for i in range(8)], 1)
    made = times(wide, wyh_ref[...], wyl_ref[...])
    out_ref[...] = jnp.full(out_ref.shape, count_ref[0].astype(F32))
    for slot in range(slots):
        for h in range(2):
            out_ref[pl.ds(8 * h + slot, quarter, stride=16), :] = made[
                slot * quarter : (slot + 1) * quarter, h * 128 : h * 128 + 128
            ]


def stacked(matrix):
    first, second = two_terms(matrix)
    return np.concatenate([first, first, second], 0)


def lowpass_call(owner_counts, density):
    slots, edge, plane = density.shape
    quarter = edge // 4
    two_levels = pass_matrix(edge // 2)[:quarter] @ pass_matrix(edge)[: edge // 2]
    wz = np.concatenate(two_terms(np.kron(np.eye(8), two_levels.T)), 1)
    i, gp, q, p = np.meshgrid(np.arange(8), np.arange(2), np.arange(2), np.arange(2), indexing="ij")
    entry = (2 * (8 * gp + i) + p + 32 * q).reshape(-1)
    wy = np.kron(two_levels.T[entry] / SQUARE, np.eye(quarter))
    wyh, wyl = two_terms(wy)
    anywhere = pl.BlockSpec(memory_space=pl.ANY)
    vmem = pl.BlockSpec(memory_space=pltpu.VMEM)
    rows_all = slots * 8 * quarter
    pieces, token = pl.pallas_call(
        lowpass_kernel,
        in_specs=[pl.BlockSpec(memory_space=pltpu.SMEM)] + [anywhere] * 4,
        out_specs=[vmem, pl.BlockSpec(memory_space=pltpu.SMEM)],
        out_shape=[
            jax.ShapeDtypeStruct((16 * quarter, 128), F32),
            jax.ShapeDtypeStruct((1,), jnp.int32),
        ],
        scratch_shapes=[
            pltpu.VMEM((slots, edge, plane // 128, 128), F32),
            pltpu.VMEM(wz.shape, BF16),
            pltpu.VMEM(wyh.shape, BF16),
            pltpu.VMEM(wyl.shape, BF16),
            pltpu.VMEM((2 * rows_all, 512), BF16),
            pltpu.VMEM((rows_all, 128), F32),
            pltpu.SemaphoreType.DMA((4,)),
            pltpu.SemaphoreType.DMA((3,)),
        ],
        compiler_params=pltpu.CompilerParams(vmem_limit_bytes=VMEM_LARGE),
        name="lowpass",
    )(owner_counts, density, wz, wyh, wyl)
    return pieces.reshape(2 * quarter, 8, 128), token


def route_kernel(me_ref, got_ref, _, send_ref, index_ref, order_ref, count_ref, sem, *, width):
    devices = got_ref.shape[0]
    place = [d % width * (devices // width) + d // width for d in range(devices)]
    copy = pltpu.make_async_copy(got_ref.at[:, 7, :], count_ref, sem)
    copy.start()
    order_ref[...] = jnp.zeros_like(order_ref)
    copy.wait()
    start, my_start, my_count = 0, 0, 0
    starts = []
    for d in range(devices):
        count = count_ref[place[d], 0].astype(jnp.int32)
        starts.append(start)
        my_start = jnp.where(me_ref[0] == d, start, my_start)
        my_count = jnp.where(me_ref[0] == d, count, my_count)
        order_ref[pl.ds(start, 8), :] = got_ref[place[d]]
        start = start + count
    index_ref[0] = my_start % 8
    index_ref[1] = my_count
    for d in range(devices):
        at = pl.multiple_of(starts[d] // 8 * 8, 8) if d else 0
        send_ref[place[d]] = order_ref[pl.ds(at, 16), :]


def route_call(me, got, token, slots, width):
    devices = got.shape[0]
    return pl.pallas_call(
        functools.partial(route_kernel, width=width),
        in_specs=[
            pl.BlockSpec(memory_space=pltpu.SMEM),
            pl.BlockSpec(memory_space=pltpu.VMEM),
            pl.BlockSpec(memory_space=pltpu.SMEM),
        ],
        out_specs=[pl.BlockSpec(memory_space=pltpu.VMEM), pl.BlockSpec(memory_space=pltpu.SMEM)],
        out_shape=[
            jax.ShapeDtypeStruct((devices, 16, 128), F32),
            jax.ShapeDtypeStruct((2,), jnp.int32),
        ],
        scratch_shapes=[
            pltpu.VMEM((devices * slots + 16, 128), F32),
            pltpu.SMEM((devices, 128), F32),
            pltpu.SemaphoreType.DMA,
        ],
        compiler_params=pltpu.CompilerParams(vmem_limit_bytes=VMEM_SMALL),
        name="route",
    )(me, got, token)


def lift(low, high, n, halo, scaled):
    up = SQUARE if scaled else 1.0
    at = 2 if halo else 0
    first, second, third, fourth = ({} for _ in range(4))

    def get(values, i, is_low):
        if halo:
            return values[i]
        return values[min(i, n - 1)] if is_low else values[max(i, 0)]

    lows = {i - at: low[i] for i in range(len(low))}
    highs = {i - at: high[i] for i in range(len(high))}

    def make_first(i):
        first[i] = highs[i] + (ALPHA * up) * (lows[i] + get(lows, i + 1, True))

    def make_second(i):
        second[i] = lows[i] + (BETA / up) * (get(first, i - 1, False) + first[i])

    def make_third(i):
        third[i] = first[i] + (GAMMA * up) * (second[i] + get(second, i + 1, True))

    def make_fourth(i):
        fourth[i] = second[i] + (DELTA / up) * (get(third, i - 1, False) + third[i])

    if halo:
        for i in range(-2, n + 1):
            make_first(i)
            if i >= -1:
                make_second(i)
            if i >= 0:
                make_third(i - 1)
            if i >= 1:
                make_fourth(i - 1)
    else:
        for i in range(n):
            make_first(i)
            make_second(i)
            if i >= 1:
                make_third(i - 1)
                make_fourth(i - 1)
        make_third(n - 1)
        make_fourth(n - 1)
    return [fourth[i] for i in range(n)], [third[i] for i in range(n)]


def fine_kernel(count_ref, _, x_any, w1_ref, w2_ref, *refs, first):
    out_ref, token_ref, x_buf, l_ref, y_ref, c_ref, m_ref, d_ref, sems = refs[-9:]
    step = pl.program_id(0)
    slot = step + first
    edge = x_any.shape[1]
    tiles = x_buf.shape[2]
    pairs = tiles // 2
    half = edge // 2
    corner = 8 * half
    live = slot < count_ref[0]
    lane = lax.broadcasted_iota(jnp.int32, (8, 128), 1)
    front = lane < 64
    inner = (lane & 63) < half
    token_ref[0] = step

    def cross(a, b):
        return pltpu.roll(jnp.where(front, b, a), 64, 1)

    def exchange(a, b):
        crossed = cross(a, b)
        return jnp.where(front, a, crossed), jnp.where(front, crossed, b)

    def with_halo(low, high):
        one, two = cross(low[0], low[-1]), cross(low[1], low[-2])
        low_all = [jnp.where(front, low[2], two), jnp.where(front, low[1], one)] + low
        low_all += [jnp.where(front, one, low[-1]), jnp.where(front, two, low[-2])]
        one, two = cross(high[0], high[-1]), cross(high[1], high[-2])
        high_all = [jnp.where(front, high[1], two), jnp.where(front, high[0], one)] + high
        return low_all, high_all + [jnp.where(front, one, high[-2])]

    def scaled_rows(rows):
        low, high = lift(rows[0::2], rows[1::2], len(rows) // 2, False, False)
        return [v * (1.0 / SCALE) for v in low] + [v * SCALE for v in high]

    def store_terms(ref, row, col, rows):
        for m, (high, low) in enumerate(split_rows(rows)):
            place = pl.ds(pl.multiple_of(row + 16 * m, 16), 16)
            ref[place, pl.ds(col, 128)] = high
            ref[place, pl.ds(256 + col, 128)] = low
            ref[place, pl.ds(512 + col, 128)] = high

    def fetch(which, place):
        for t in range(tiles):
            pltpu.make_async_copy(
                x_any.at[which, :, pl.ds(t * 128, 128)], x_buf.at[place, :, t, :], sems.at[place]
            ).start()

    @pl.when((step == 0) & live)
    def _():
        fetch(slot, 0)

    @pl.when(jnp.logical_not(live))
    def _():
        out_ref[...] = jnp.zeros_like(out_ref)

    @pl.when(live)
    def _():
        x = x_buf.at[step % 2]
        pltpu.make_async_copy(x, x, sems.at[step % 2]).wait()

    @pl.when((step + 1 < pl.num_programs(0)) & (slot + 1 < count_ref[0]))
    def _():
        fetch(slot + 1, (step + 1) % 2)

    @pl.when(live)
    def _():
        x = x_buf.at[step % 2]
        for g in range(4):
            rows = scaled_rows([x[i, pl.ds(8 * g, 8), :] for i in range(edge)])
            store_terms(l_ref, (g % 2) * 8 * edge, (g // 2) * 128, rows)
        lifted = dot(l_ref[...], w1_ref[...])
        y_ref[0] = lifted[:, :128]
        y_ref[1] = lifted[:, 128:]
        for r in range(edge // 8):
            rows = pl.ds(8 * r, 8)

            def tile(part, j):
                return y_ref[part, pl.ds((j // 8) * 8 * edge + 64 * r + j % 8, 8, stride=8), :]

            low = [tile(0, j) for j in range(pairs)]
            high = [tile(1, j) for j in range(pairs)]
            low, high = lift(*with_halo(low, high), pairs, True, True)
            for part, values in enumerate((low, high)):
                for t in range(pairs // 2):
                    a, b = exchange(values[2 * t], values[2 * t + 1])
                    at = part * pairs + t
                    out_ref[0, rows, pl.ds(at * 128, 128)] = a
                    out_ref[0, rows, pl.ds((at + pairs // 2) * 128, 128)] = b
            if r < half // 8:
                low, high = lift(*with_halo(low[0::2], low[1::2]), 8, True, False)
                for i in range(8):
                    c_ref[pl.ds(64 * r + i, 8, stride=8), :] = low[i]
                    c_ref[pl.ds(corner + 64 * r + i, 8, stride=8), :] = high[i]
        for u in range(2):
            rows = scaled_rows([c_ref[pl.ds(u * corner + 8 * i, 8), :] for i in range(half)])
            store_terms(m_ref, 0, u * 128, rows)
        lifted = dot(m_ref[...], w2_ref[...])
        d_ref[0] = lifted[:, :128]
        d_ref[1] = lifted[:, 128:]
        for u in range(2):
            for t in range(4):
                for r in range(half // 8):
                    a = d_ref[u, pl.ds(64 * r + 2 * t, 8, stride=8), :]
                    b = d_ref[u, pl.ds(64 * r + 2 * t + 1, 8, stride=8), :]
                    for at, value in zip((u * 8 + t, u * 8 + 4 + t), exchange(a, b)):
                        rows, cols = pl.ds(8 * r, 8), pl.ds(at * 128, 128)
                        out_ref[0, rows, cols] = jnp.where(inner, value, out_ref[0, rows, cols])


def fine_call(owner_counts, token, density, first, last, before=None):
    slots, edge, plane = density.shape
    tiles = plane // 128
    half = edge // 2
    pairs = tiles // 2
    count = last - first
    one = pass_matrix(edge).T
    zero = np.zeros_like(one)
    w1 = np.block(
        [
            [one / SCALE, zero, zero, zero],
            [zero, zero, one * SCALE, zero],
            [zero, one / SCALE, zero, zero],
            [zero, zero, zero, one * SCALE],
        ]
    )
    two = np.zeros_like(one)
    two[:half, :half] = pass_matrix(half).T
    w2 = np.kron(np.diag([1 / SCALE, 1 / SCALE, SCALE, SCALE]), two)
    anywhere = pl.BlockSpec(memory_space=pl.ANY)
    smem = pl.BlockSpec(memory_space=pltpu.SMEM)
    old = [] if before is None else [before]
    fixed = pl.BlockSpec((768, 256), lambda s: (0, 0))
    return pl.pallas_call(
        functools.partial(fine_kernel, first=first),
        grid=(count,),
        in_specs=[smem, smem, anywhere, fixed, fixed] + [anywhere] * len(old),
        out_specs=[pl.BlockSpec((1, edge, plane), lambda s: (s + first, 0, 0)), smem],
        out_shape=[
            jax.ShapeDtypeStruct(density.shape, F32),
            jax.ShapeDtypeStruct((1,), jnp.int32),
        ],
        scratch_shapes=[
            pltpu.VMEM((2, edge, tiles, 128), F32),
            pltpu.VMEM((pairs * edge, 768), BF16),
            pltpu.VMEM((2, pairs * edge, 128), F32),
            pltpu.VMEM((16 * half, 128), F32),
            pltpu.VMEM((8 * half, 768), BF16),
            pltpu.VMEM((2, 8 * half, 128), F32),
            pltpu.SemaphoreType.DMA((2,)),
        ],
        input_output_aliases={5: 0} if old else {},
        compiler_params=pltpu.CompilerParams(vmem_limit_bytes=VMEM_LIMIT),
        cost_estimate=pl.CostEstimate(
            flops=6 * count * edge * plane * 256, bytes_accessed=2 * count * MIB, transcendentals=0
        ),
        name="fine",
    )(owner_counts, token, density, stacked(w1), stacked(w2), *old)


def coarse_kernel(
    index_ref,
    piece_ref,
    wx_ref,
    wzh_ref,
    wzl_ref,
    wyh_ref,
    wyl_ref,
    w23h_ref,
    w23l_ref,
    wx2_ref,
    wx3_ref,
    fine_ref,
    out_ref,
    block_ref,
    corner_ref,
    corner_sem,
    out_sem,
):
    slots = corner_ref.shape[0]
    lane = lax.broadcasted_iota(jnp.int32, (16, 128), 1)

    def window(s):
        return out_ref.at[s, pl.ds(0, 16), pl.ds(0, 1024)]

    def piece(i):
        return jnp.concatenate([piece_ref[pl.ds(16 * h + i, 16, stride=32), :] for h in range(2)], 1)

    for s in range(slots):
        pltpu.make_async_copy(window(s), corner_ref.at[s], corner_sem.at[s]).start()

    first = [
        [
            times_left(wx_ref[...], jnp.concatenate([piece(o * 8 + 2 * q), piece(o * 8 + 2 * q + 1)], 0))
            for q in range(4)
        ]
        for o in range(2)
    ]
    stacked = []
    for o in range(2):
        for cy in range(2):
            for yh in range(2):
                part = slice(yh * 128, yh * 128 + 128)
                stacked.append(jnp.concatenate([first[o][cy][:, part], first[o][2 + cy][:, part]], 1))
    lifted = times(jnp.concatenate(stacked, 0), wzh_ref[...], wzl_ref[...])
    stacked = []
    for o in range(2):
        for tz in range(2):
            stacked.append(
                jnp.concatenate(
                    [lifted[(o * 4 + u) * 32 : (o * 4 + u + 1) * 32, tz * 128 : tz * 128 + 128] for u in range(4)],
                    1,
                )
            )
    lifted = times(jnp.concatenate(stacked, 0), wyh_ref[...], wyl_ref[...])
    corner = []
    for o in range(2):
        for tz in range(2):
            for ty in range(2):
                for tx in range(2):
                    at = (o * 2 + tz) * 32 + tx * 16
                    value = lifted[at : at + 16, ty * 256 : ty * 256 + 256]
                    if tx + ty + tz == 0:
                        corner.append(value)
                    else:
                        block_ref[o * 8 + tx + 2 * ty + 4 * tz] = value
    both = times(jnp.concatenate(corner, 0), w23h_ref[...], w23l_ref[...])
    depth = lax.broadcasted_iota(jnp.int32, (16, 128), 0)
    small = (depth < 8) & ((lane & 15) < 8)
    for o in range(2):
        mine = both[o * 16 : o * 16 + 16]
        second = times_left(wx2_ref[...], mine[:, :256])
        third = times_left(wx3_ref[...], mine[:, 256:])
        block_ref[o * 8] = jnp.concatenate(
            [jnp.where(small, third, second[:, :128]), second[:, 128:]], 1
        )

    for s in range(slots):
        pltpu.make_async_copy(window(s), corner_ref.at[s], corner_sem.at[s]).wait()
    placed = (lane & 63) < 16
    for s in range(slots):
        value = block_ref[index_ref[0] + s]
        for t in range(8):
            tile = value[:, (t // 4) * 128 : (t // 4) * 128 + 128]
            if t % 4:
                tile = pltpu.roll(tile, 128 - 16 * (t % 4), 1)
            cols = pl.ds(t * 128, 128)
            corner_ref[s, :, cols] = jnp.where(placed, tile, corner_ref[s, :, cols])
    for s in range(slots):

        @pl.when(s < index_ref[1])
        def _():
            pltpu.make_async_copy(corner_ref.at[s], window(s), out_sem.at[s]).start()

    for s in range(slots):

        @pl.when(s < index_ref[1])
        def _():
            pltpu.make_async_copy(corner_ref.at[s], window(s), out_sem.at[s]).wait()


def coarse_call(index, pieces, fine):
    slots, edge, plane = fine.shape
    m32, m16, m8 = pass_matrix(32), pass_matrix(16), pass_matrix(8)
    deep = np.zeros((16, 16))
    deep[:8] = m8 @ m16[:8]
    eye8, eye16 = np.eye(8), np.eye(16)
    wz = np.zeros((256, 256))
    for cz in range(2):
        for tz in range(2):
            wz[cz * 128 : cz * 128 + 128, tz * 128 : tz * 128 + 128] = np.kron(
                eye8, m32[tz * 16 : tz * 16 + 16, cz * 16 : cz * 16 + 16].T
            )
    lanes = np.arange(256).reshape(2, 4, 2, 16).transpose(0, 2, 1, 3).reshape(-1)
    wy = np.kron(m32.T, eye16)[:, np.concatenate([lanes, 256 + lanes])]
    w23 = np.concatenate([np.kron(m16.T, m16.T)[:, lanes], np.kron(deep.T, deep.T)[:, lanes[:128]]], 1)[lanes]
    weights = [
        left_terms(m32),
        *two_terms(wz),
        *two_terms(wy),
        *two_terms(w23),
        left_terms(m16),
        left_terms(deep),
    ]
    anywhere = pl.BlockSpec(memory_space=pl.ANY)
    vmem = pl.BlockSpec(memory_space=pltpu.VMEM)
    return pl.pallas_call(
        coarse_kernel,
        in_specs=[pl.BlockSpec(memory_space=pltpu.SMEM), vmem] + [vmem] * len(weights) + [anywhere],
        out_specs=anywhere,
        out_shape=jax.ShapeDtypeStruct(fine.shape, F32),
        scratch_shapes=[
            pltpu.VMEM((16, 16, 256), F32),
            pltpu.VMEM((slots, 16, 1024), F32),
            pltpu.SemaphoreType.DMA((slots,)),
            pltpu.SemaphoreType.DMA((slots,)),
        ],
        input_output_aliases={2 + len(weights): 0},
        compiler_params=pltpu.CompilerParams(vmem_limit_bytes=VMEM_SMALL),
        name="coarse",
    )(index, pieces.reshape(-1, 128), *weights, fine)


def exchange(lowpass, slots, token):
    me = lax.axis_index(AXES)
    devices = lax.axis_size(AXES)
    if devices == lowpass.shape[0]:
        got = lax.all_to_all(lowpass, SWAPPED, 0, 0, tiled=True)
        sent, index = route_call(me.reshape(1), got, token, slots, lax.axis_size("dev"))
        return lax.all_to_all(sent, SWAPPED, 0, 0, tiled=True), index
    every = lax.all_gather(lowpass, AXES, axis=0)
    counts = every[:, 0, 7, 0].astype(jnp.int32)
    starts = jnp.cumsum(counts) - counts
    blocks = starts[me] // 8 * 8 + jnp.arange(16, dtype=jnp.int32)
    owners = jnp.sum((starts[None, :] <= blocks[:, None]).astype(jnp.int32), axis=1) - 1
    place = jnp.minimum(blocks - starts[owners], slots - 1)
    pieces = jnp.transpose(every[owners, :, place], (1, 0, 2))
    return pieces, jnp.stack([starts[me] % 8, counts[me]])


def per_device(density, owner_counts):
    slots = density.shape[0]
    early = slots // 3
    lowpass, token = lowpass_call(owner_counts, density)
    fine, token = fine_call(owner_counts, token, density, 0, early)
    pieces, index = exchange(lowpass, slots, token)
    fine, _ = fine_call(owner_counts, index, density, early, slots, fine)
    return coarse_call(index, pieces, fine)


def solution(mesh):
    in_specs = (P(AXES, None, None), P(AXES))
    out_specs = P(AXES, None, None)
    return jax.shard_map(per_device, mesh=mesh, in_specs=in_specs, out_specs=out_specs, check_vma=False)
```

```python
import functools

import jax
import jax.numpy as jnp
import numpy as np
from jax import lax
from jax.experimental import pallas as pl
from jax.experimental.pallas import tpu as pltpu
from jax.sharding import PartitionSpec as P

ALPHA = -1.586134342059924
BETA = -0.052980118572961
GAMMA = 0.882911075530934
DELTA = 0.443506852043971
SCALE = 1.230174104914001
SQUARE = SCALE * SCALE
F32 = jnp.float32
BF16 = jnp.bfloat16
AXES = ("node", "dev")
SWAPPED = ("dev", "node")
MIB = 1 << 20
VMEM_LIMIT = 48 * MIB
VMEM_SMALL = 16 * MIB
VMEM_LARGE = 56 * MIB


def pass_matrix(n):
    low, high = np.eye(n)[0::2], np.eye(n)[1::2]

    def after(v):
        return np.concatenate([v[1:], v[-1:]], 0)

    def before(v):
        return np.concatenate([v[:1], v[:-1]], 0)

    high = high + ALPHA * (low + after(low))
    low = low + BETA * (before(high) + high)
    high = high + GAMMA * (low + after(low))
    low = low + DELTA * (before(high) + high)
    return np.concatenate([low / SCALE, high * SCALE], 0)


def two_terms(matrix):
    matrix = np.asarray(matrix, np.float32)
    first = matrix.astype(BF16)
    return first, (matrix - first.astype(np.float32)).astype(BF16)


def left_terms(matrix):
    first, second = two_terms(matrix)
    return np.concatenate([first, second, first], 1)


def split(value):
    first = value.astype(BF16)
    return first, (value - first.astype(F32)).astype(BF16)


def dot(left, right):
    return jnp.dot(left, right, preferred_element_type=F32)


def times(value, first, second):
    high, low = split(value)
    both = dot(jnp.concatenate([high, low], 0), first)
    count = value.shape[0]
    return both[:count] + both[count:] + dot(high, second)


def times_left(terms, value):
    high, low = split(value)
    return dot(terms, jnp.concatenate([high, high, low], 0))


def split_rows(rows):
    return [split(jnp.concatenate(rows[m : m + 2], 0)) for m in range(0, len(rows), 2)]


def tiled_view(density):
    slots, edge, plane = density.shape
    view = density.reshape(slots, edge // 8, 8, plane // 128, 128)
    return jnp.transpose(view, (0, 1, 3, 2, 4))


def tile_rows(ref, block, group, edge, tiles):
    base = block * edge * tiles + 64 * group
    return [ref[pl.ds(base + (x // 8) * 8 * tiles + x % 8, 8, stride=8), :] for x in range(edge)]


def lowpass_kernel(
    count_ref, x_any, wz_any, wyh_any, wyl_any, out_ref, token_ref, x_ref, wz_ref, wyh_ref, wyl_ref, l_ref, z_ref, sems, w_sems
):
    slots, edge, tiles = x_any.shape[0], 8 * x_any.shape[1], x_any.shape[2]
    quarter = edge // 4
    rows_all = slots * 8 * quarter
    token_ref[0] = count_ref[0]
    blocks = [
        pltpu.make_async_copy(x_any.at[n], x_ref.at[n], sems.at[n]) for n in range(slots)
    ]
    for copy in blocks:
        copy.start()
    flat = x_ref.reshape(slots * edge * tiles, 128)
    weights = [
        pltpu.make_async_copy(src, dst, w_sems.at[i])
        for i, (src, dst) in enumerate(((wz_any, wz_ref), (wyh_any, wyh_ref), (wyl_any, wyl_ref)))
    ]
    for copy in weights:
        copy.start()
    for s in range(slots):
        blocks[s].wait()

        @pl.loop(0, 2)
        def _(q):
            for u in range(2):
                rows = tile_rows(flat, s, 2 * q + u, edge, tiles)
                rows, _ = lift(rows[0::2], rows[1::2], edge // 2, False, False)
                rows, _ = lift(rows[0::2], rows[1::2], quarter, False, False)
                for m, (high, low) in enumerate(split_rows(rows)):
                    at = s * 8 * quarter + 16 * m
                    cols = pl.ds(pl.multiple_of(u * 256 + q * 128, 128), 128)
                    l_ref[pl.ds(at, 16), cols] = high
                    l_ref[pl.ds(rows_all + at, 16), cols] = low

    for copy in weights:
        copy.wait()
    made = dot(l_ref[...], wz_ref[...])
    z_ref[...] = (made[:rows_all, :128] + made[rows_all:, :128]) + made[:rows_all, 128:]
    wide = jnp.concatenate([z_ref[pl.ds(i, slots * quarter, stride=8), :] for i in range(8)], 1)
    made = times(wide, wyh_ref[...], wyl_ref[...])
    out_ref[...] = jnp.full(out_ref.shape, count_ref[0].astype(F32))
    for slot in range(slots):
        for h in range(2):
            out_ref[pl.ds(8 * h + slot, quarter, stride=16), :] = made[
                slot * quarter : (slot + 1) * quarter, h * 128 : h * 128 + 128
            ]


def stacked(matrix):
    first, second = two_terms(matrix)
    return np.concatenate([first, first, second], 0)


def lowpass_call(owner_counts, density):
    slots, edge, plane = density.shape
    quarter = edge // 4
    two_levels = pass_matrix(edge // 2)[:quarter] @ pass_matrix(edge)[: edge // 2]
    wz = np.concatenate(two_terms(np.kron(np.eye(8), two_levels.T)), 1)
    i, gp, q, p = np.meshgrid(np.arange(8), np.arange(2), np.arange(2), np.arange(2), indexing="ij")
    entry = (2 * (8 * gp + i) + p + 32 * q).reshape(-1)
    wy = np.kron(two_levels.T[entry] / SQUARE, np.eye(quarter))
    wyh, wyl = two_terms(wy)
    anywhere = pl.BlockSpec(memory_space=pl.ANY)
    vmem = pl.BlockSpec(memory_space=pltpu.VMEM)
    rows_all = slots * 8 * quarter
    pieces, token = pl.pallas_call(
        lowpass_kernel,
        in_specs=[pl.BlockSpec(memory_space=pltpu.SMEM)] + [anywhere] * 4,
        out_specs=[vmem, pl.BlockSpec(memory_space=pltpu.SMEM)],
        out_shape=[
            jax.ShapeDtypeStruct((16 * quarter, 128), F32),
            jax.ShapeDtypeStruct((1,), jnp.int32),
        ],
        scratch_shapes=[
            pltpu.VMEM((slots, edge // 8, plane // 128, 8, 128), F32),
            pltpu.VMEM(wz.shape, BF16),
            pltpu.VMEM(wyh.shape, BF16),
            pltpu.VMEM(wyl.shape, BF16),
            pltpu.VMEM((2 * rows_all, 512), BF16),
            pltpu.VMEM((rows_all, 128), F32),
            pltpu.SemaphoreType.DMA((slots,)),
            pltpu.SemaphoreType.DMA((3,)),
        ],
        compiler_params=pltpu.CompilerParams(vmem_limit_bytes=VMEM_LARGE),
        name="lowpass",
    )(owner_counts, tiled_view(density), wz, wyh, wyl)
    return pieces.reshape(2 * quarter, 8, 128), token


def route_kernel(me_ref, got_ref, _, send_ref, index_ref, order_ref, count_ref, sem, *, width):
    devices = got_ref.shape[0]
    place = [d % width * (devices // width) + d // width for d in range(devices)]
    copy = pltpu.make_async_copy(got_ref.at[:, 7, :], count_ref, sem)
    copy.start()
    order_ref[...] = jnp.zeros_like(order_ref)
    copy.wait()
    start, my_start, my_count = 0, 0, 0
    starts = []
    for d in range(devices):
        count = count_ref[place[d], 0].astype(jnp.int32)
        starts.append(start)
        my_start = jnp.where(me_ref[0] == d, start, my_start)
        my_count = jnp.where(me_ref[0] == d, count, my_count)
        order_ref[pl.ds(start, 8), :] = got_ref[place[d]]
        start = start + count
    index_ref[0] = my_start % 8
    index_ref[1] = my_count
    for d in range(devices):
        at = pl.multiple_of(starts[d] // 8 * 8, 8) if d else 0
        send_ref[place[d]] = order_ref[pl.ds(at, 16), :]


def route_call(me, got, token, slots, width):
    devices = got.shape[0]
    return pl.pallas_call(
        functools.partial(route_kernel, width=width),
        in_specs=[
            pl.BlockSpec(memory_space=pltpu.SMEM),
            pl.BlockSpec(memory_space=pltpu.VMEM),
            pl.BlockSpec(memory_space=pltpu.SMEM),
        ],
        out_specs=[pl.BlockSpec(memory_space=pltpu.VMEM), pl.BlockSpec(memory_space=pltpu.SMEM)],
        out_shape=[
            jax.ShapeDtypeStruct((devices, 16, 128), F32),
            jax.ShapeDtypeStruct((2,), jnp.int32),
        ],
        scratch_shapes=[
            pltpu.VMEM((devices * slots + 16, 128), F32),
            pltpu.SMEM((devices, 128), F32),
            pltpu.SemaphoreType.DMA,
        ],
        compiler_params=pltpu.CompilerParams(vmem_limit_bytes=VMEM_SMALL),
        name="route",
    )(me, got, token)


def lift(low, high, n, halo, scaled):
    up = SQUARE if scaled else 1.0
    at = 2 if halo else 0
    first, second, third, fourth = ({} for _ in range(4))

    def get(values, i, is_low):
        if halo:
            return values[i]
        return values[min(i, n - 1)] if is_low else values[max(i, 0)]

    lows = {i - at: low[i] for i in range(len(low))}
    highs = {i - at: high[i] for i in range(len(high))}

    def make_first(i):
        first[i] = highs[i] + (ALPHA * up) * (lows[i] + get(lows, i + 1, True))

    def make_second(i):
        second[i] = lows[i] + (BETA / up) * (get(first, i - 1, False) + first[i])

    def make_third(i):
        third[i] = first[i] + (GAMMA * up) * (second[i] + get(second, i + 1, True))

    def make_fourth(i):
        fourth[i] = second[i] + (DELTA / up) * (get(third, i - 1, False) + third[i])

    if halo:
        for i in range(-2, n + 1):
            make_first(i)
            if i >= -1:
                make_second(i)
            if i >= 0:
                make_third(i - 1)
            if i >= 1:
                make_fourth(i - 1)
    else:
        for i in range(n):
            make_first(i)
            make_second(i)
            if i >= 1:
                make_third(i - 1)
                make_fourth(i - 1)
        make_third(n - 1)
        make_fourth(n - 1)
    return [fourth[i] for i in range(n)], [third[i] for i in range(n)]


def fine_kernel(count_ref, _, x_any, w1_ref, w2_ref, *refs, first):
    out_ref, token_ref, x_buf, l_ref, y_ref, c_ref, m_ref, d_ref, sems = refs[-9:]
    step = pl.program_id(0)
    slot = step + first
    edge, tiles = 8 * x_any.shape[1], x_any.shape[2]
    pairs = tiles // 2
    half = edge // 2
    corner = 8 * half
    live = slot < count_ref[0]
    lane = lax.broadcasted_iota(jnp.int32, (8, 128), 1)
    front = lane < 64
    inner = (lane & 63) < half
    token_ref[0] = step

    def cross(a, b):
        return pltpu.roll(jnp.where(front, b, a), 64, 1)

    def exchange(a, b):
        crossed = cross(a, b)
        return jnp.where(front, a, crossed), jnp.where(front, crossed, b)

    def with_halo(low, high):
        one, two = cross(low[0], low[-1]), cross(low[1], low[-2])
        low_all = [jnp.where(front, low[2], two), jnp.where(front, low[1], one)] + low
        low_all += [jnp.where(front, one, low[-1]), jnp.where(front, two, low[-2])]
        one, two = cross(high[0], high[-1]), cross(high[1], high[-2])
        high_all = [jnp.where(front, high[1], two), jnp.where(front, high[0], one)] + high
        return low_all, high_all + [jnp.where(front, one, high[-2])]

    def scaled_rows(rows):
        low, high = lift(rows[0::2], rows[1::2], len(rows) // 2, False, False)
        return [v * (1.0 / SCALE) for v in low] + [v * SCALE for v in high]

    def store_terms(ref, row, col, rows):
        for m, (high, low) in enumerate(split_rows(rows)):
            place = pl.ds(pl.multiple_of(row + 16 * m, 16), 16)
            ref[place, pl.ds(col, 128)] = high
            ref[place, pl.ds(256 + col, 128)] = low
            ref[place, pl.ds(512 + col, 128)] = high

    def fetch(which, place):
        return pltpu.make_async_copy(x_any.at[which], x_buf.at[place], sems.at[place])

    @pl.when((step == 0) & live)
    def _():
        fetch(slot, 0).start()

    @pl.when(jnp.logical_not(live))
    def _():
        out_ref[...] = jnp.zeros_like(out_ref)

    @pl.when(live)
    def _():
        fetch(slot, step % 2).wait()

    @pl.when((step + 1 < pl.num_programs(0)) & (slot + 1 < count_ref[0]))
    def _():
        fetch(slot + 1, (step + 1) % 2).start()

    @pl.when(live)
    def _():
        flat = x_buf.reshape(2 * edge * tiles, 128)
        for g in range(4):
            rows = scaled_rows(tile_rows(flat, step % 2, g, edge, tiles))
            store_terms(l_ref, (g % 2) * 8 * edge, (g // 2) * 128, rows)
        lifted = dot(l_ref[...], w1_ref[...])
        y_ref[0] = lifted[:, :128]
        y_ref[1] = lifted[:, 128:]
        for r in range(edge // 8):
            rows = pl.ds(8 * r, 8)

            def tile(part, j):
                return y_ref[part, pl.ds((j // 8) * 8 * edge + 64 * r + j % 8, 8, stride=8), :]

            low = [tile(0, j) for j in range(pairs)]
            high = [tile(1, j) for j in range(pairs)]
            low, high = lift(*with_halo(low, high), pairs, True, True)
            for part, values in enumerate((low, high)):
                for t in range(pairs // 2):
                    a, b = exchange(values[2 * t], values[2 * t + 1])
                    at = part * pairs + t
                    out_ref[0, rows, pl.ds(at * 128, 128)] = a
                    out_ref[0, rows, pl.ds((at + pairs // 2) * 128, 128)] = b
            if r < half // 8:
                low, high = lift(*with_halo(low[0::2], low[1::2]), 8, True, False)
                for i in range(8):
                    c_ref[pl.ds(64 * r + i, 8, stride=8), :] = low[i]
                    c_ref[pl.ds(corner + 64 * r + i, 8, stride=8), :] = high[i]
        for u in range(2):
            rows = scaled_rows([c_ref[pl.ds(u * corner + 8 * i, 8), :] for i in range(half)])
            store_terms(m_ref, 0, u * 128, rows)
        lifted = dot(m_ref[...], w2_ref[...])
        d_ref[0] = lifted[:, :128]
        d_ref[1] = lifted[:, 128:]
        for u in range(2):
            for t in range(4):
                for r in range(half // 8):
                    a = d_ref[u, pl.ds(64 * r + 2 * t, 8, stride=8), :]
                    b = d_ref[u, pl.ds(64 * r + 2 * t + 1, 8, stride=8), :]
                    for at, value in zip((u * 8 + t, u * 8 + 4 + t), exchange(a, b)):
                        rows, cols = pl.ds(8 * r, 8), pl.ds(at * 128, 128)
                        out_ref[0, rows, cols] = jnp.where(inner, value, out_ref[0, rows, cols])


def fine_call(owner_counts, token, density, first, last, before=None):
    slots, edge, plane = density.shape
    tiles = plane // 128
    half = edge // 2
    pairs = tiles // 2
    count = last - first
    one = pass_matrix(edge).T
    zero = np.zeros_like(one)
    w1 = np.block(
        [
            [one / SCALE, zero, zero, zero],
            [zero, zero, one * SCALE, zero],
            [zero, one / SCALE, zero, zero],
            [zero, zero, zero, one * SCALE],
        ]
    )
    two = np.zeros_like(one)
    two[:half, :half] = pass_matrix(half).T
    w2 = np.kron(np.diag([1 / SCALE, 1 / SCALE, SCALE, SCALE]), two)
    anywhere = pl.BlockSpec(memory_space=pl.ANY)
    smem = pl.BlockSpec(memory_space=pltpu.SMEM)
    old = [] if before is None else [before]
    fixed = pl.BlockSpec((768, 256), lambda s: (0, 0))
    return pl.pallas_call(
        functools.partial(fine_kernel, first=first),
        grid=(count,),
        in_specs=[smem, smem, anywhere, fixed, fixed] + [anywhere] * len(old),
        out_specs=[pl.BlockSpec((1, edge, plane), lambda s: (s + first, 0, 0)), smem],
        out_shape=[
            jax.ShapeDtypeStruct(density.shape, F32),
            jax.ShapeDtypeStruct((1,), jnp.int32),
        ],
        scratch_shapes=[
            pltpu.VMEM((2, edge // 8, tiles, 8, 128), F32),
            pltpu.VMEM((pairs * edge, 768), BF16),
            pltpu.VMEM((2, pairs * edge, 128), F32),
            pltpu.VMEM((16 * half, 128), F32),
            pltpu.VMEM((8 * half, 768), BF16),
            pltpu.VMEM((2, 8 * half, 128), F32),
            pltpu.SemaphoreType.DMA((2,)),
        ],
        input_output_aliases={5: 0} if old else {},
        compiler_params=pltpu.CompilerParams(vmem_limit_bytes=VMEM_LIMIT),
        cost_estimate=pl.CostEstimate(
            flops=6 * count * edge * plane * 256, bytes_accessed=2 * count * MIB, transcendentals=0
        ),
        name="fine",
    )(owner_counts, token, tiled_view(density), stacked(w1), stacked(w2), *old)


def coarse_kernel(
    index_ref,
    piece_ref,
    wx_ref,
    wzh_ref,
    wzl_ref,
    wyh_ref,
    wyl_ref,
    w23h_ref,
    w23l_ref,
    wx2_ref,
    wx3_ref,
    fine_ref,
    out_ref,
    block_ref,
    corner_ref,
    corner_sem,
    out_sem,
):
    slots = corner_ref.shape[0]
    lane = lax.broadcasted_iota(jnp.int32, (16, 128), 1)

    def window(s):
        return out_ref.at[s, pl.ds(0, 16), pl.ds(0, 1024)]

    def piece(i):
        return jnp.concatenate([piece_ref[pl.ds(16 * h + i, 16, stride=32), :] for h in range(2)], 1)

    for s in range(slots):
        pltpu.make_async_copy(window(s), corner_ref.at[s], corner_sem.at[s]).start()

    first = [
        [
            times_left(wx_ref[...], jnp.concatenate([piece(o * 8 + 2 * q), piece(o * 8 + 2 * q + 1)], 0))
            for q in range(4)
        ]
        for o in range(2)
    ]
    stacked = []
    for o in range(2):
        for cy in range(2):
            for yh in range(2):
                part = slice(yh * 128, yh * 128 + 128)
                stacked.append(jnp.concatenate([first[o][cy][:, part], first[o][2 + cy][:, part]], 1))
    lifted = times(jnp.concatenate(stacked, 0), wzh_ref[...], wzl_ref[...])
    stacked = []
    for o in range(2):
        for tz in range(2):
            stacked.append(
                jnp.concatenate(
                    [lifted[(o * 4 + u) * 32 : (o * 4 + u + 1) * 32, tz * 128 : tz * 128 + 128] for u in range(4)],
                    1,
                )
            )
    lifted = times(jnp.concatenate(stacked, 0), wyh_ref[...], wyl_ref[...])
    corner = []
    for o in range(2):
        for tz in range(2):
            for ty in range(2):
                for tx in range(2):
                    at = (o * 2 + tz) * 32 + tx * 16
                    value = lifted[at : at + 16, ty * 256 : ty * 256 + 256]
                    if tx + ty + tz == 0:
                        corner.append(value)
                    else:
                        block_ref[o * 8 + tx + 2 * ty + 4 * tz] = value
    both = times(jnp.concatenate(corner, 0), w23h_ref[...], w23l_ref[...])
    depth = lax.broadcasted_iota(jnp.int32, (16, 128), 0)
    small = (depth < 8) & ((lane & 15) < 8)
    for o in range(2):
        mine = both[o * 16 : o * 16 + 16]
        second = times_left(wx2_ref[...], mine[:, :256])
        third = times_left(wx3_ref[...], mine[:, 256:])
        block_ref[o * 8] = jnp.concatenate(
            [jnp.where(small, third, second[:, :128]), second[:, 128:]], 1
        )

    for s in range(slots):
        pltpu.make_async_copy(window(s), corner_ref.at[s], corner_sem.at[s]).wait()
    placed = (lane & 63) < 16
    for s in range(slots):
        value = block_ref[index_ref[0] + s]
        for t in range(8):
            tile = value[:, (t // 4) * 128 : (t // 4) * 128 + 128]
            if t % 4:
                tile = pltpu.roll(tile, 128 - 16 * (t % 4), 1)
            cols = pl.ds(t * 128, 128)
            corner_ref[s, :, cols] = jnp.where(placed, tile, corner_ref[s, :, cols])
    for s in range(slots):

        @pl.when(s < index_ref[1])
        def _():
            pltpu.make_async_copy(corner_ref.at[s], window(s), out_sem.at[s]).start()

    for s in range(slots):

        @pl.when(s < index_ref[1])
        def _():
            pltpu.make_async_copy(corner_ref.at[s], window(s), out_sem.at[s]).wait()


def coarse_call(index, pieces, fine):
    slots, edge, plane = fine.shape
    m32, m16, m8 = pass_matrix(32), pass_matrix(16), pass_matrix(8)
    deep = np.zeros((16, 16))
    deep[:8] = m8 @ m16[:8]
    eye8, eye16 = np.eye(8), np.eye(16)
    wz = np.zeros((256, 256))
    for cz in range(2):
        for tz in range(2):
            wz[cz * 128 : cz * 128 + 128, tz * 128 : tz * 128 + 128] = np.kron(
                eye8, m32[tz * 16 : tz * 16 + 16, cz * 16 : cz * 16 + 16].T
            )
    lanes = np.arange(256).reshape(2, 4, 2, 16).transpose(0, 2, 1, 3).reshape(-1)
    wy = np.kron(m32.T, eye16)[:, np.concatenate([lanes, 256 + lanes])]
    w23 = np.concatenate([np.kron(m16.T, m16.T)[:, lanes], np.kron(deep.T, deep.T)[:, lanes[:128]]], 1)[lanes]
    weights = [
        left_terms(m32),
        *two_terms(wz),
        *two_terms(wy),
        *two_terms(w23),
        left_terms(m16),
        left_terms(deep),
    ]
    anywhere = pl.BlockSpec(memory_space=pl.ANY)
    vmem = pl.BlockSpec(memory_space=pltpu.VMEM)
    return pl.pallas_call(
        coarse_kernel,
        in_specs=[pl.BlockSpec(memory_space=pltpu.SMEM), vmem] + [vmem] * len(weights) + [anywhere],
        out_specs=anywhere,
        out_shape=jax.ShapeDtypeStruct(fine.shape, F32),
        scratch_shapes=[
            pltpu.VMEM((16, 16, 256), F32),
            pltpu.VMEM((slots, 16, 1024), F32),
            pltpu.SemaphoreType.DMA((slots,)),
            pltpu.SemaphoreType.DMA((slots,)),
        ],
        input_output_aliases={2 + len(weights): 0},
        compiler_params=pltpu.CompilerParams(vmem_limit_bytes=VMEM_SMALL),
        name="coarse",
    )(index, pieces.reshape(-1, 128), *weights, fine)


def exchange(lowpass, slots, token):
    me = lax.axis_index(AXES)
    devices = lax.axis_size(AXES)
    if devices == lowpass.shape[0]:
        got = lax.all_to_all(lowpass, SWAPPED, 0, 0, tiled=True)
        sent, index = route_call(me.reshape(1), got, token, slots, lax.axis_size("dev"))
        return lax.all_to_all(sent, SWAPPED, 0, 0, tiled=True), index
    every = lax.all_gather(lowpass, AXES, axis=0)
    counts = every[:, 0, 7, 0].astype(jnp.int32)
    starts = jnp.cumsum(counts) - counts
    blocks = starts[me] // 8 * 8 + jnp.arange(16, dtype=jnp.int32)
    owners = jnp.sum((starts[None, :] <= blocks[:, None]).astype(jnp.int32), axis=1) - 1
    place = jnp.minimum(blocks - starts[owners], slots - 1)
    pieces = jnp.transpose(every[owners, :, place], (1, 0, 2))
    return pieces, jnp.stack([starts[me] % 8, counts[me]])


def per_device(density, owner_counts):
    slots = density.shape[0]
    early = slots // 3
    lowpass, token = lowpass_call(owner_counts, density)
    fine, token = fine_call(owner_counts, token, density, 0, early)
    pieces, index = exchange(lowpass, slots, token)
    fine, _ = fine_call(owner_counts, index, density, early, slots, fine)
    return coarse_call(index, pieces, fine)


def solution(mesh):
    in_specs = (P(AXES, None, None), P(AXES))
    out_specs = P(AXES, None, None)
    return jax.shard_map(per_device, mesh=mesh, in_specs=in_specs, out_specs=out_specs, check_vma=False)
```

```python
import functools

import jax
import jax.numpy as jnp
import numpy as np
from jax import lax
from jax.experimental import pallas as pl
from jax.experimental.pallas import tpu as pltpu
from jax.sharding import PartitionSpec as P

ALPHA = -1.586134342059924
BETA = -0.052980118572961
GAMMA = 0.882911075530934
DELTA = 0.443506852043971
SCALE = 1.230174104914001
SQUARE = SCALE * SCALE
F32 = jnp.float32
BF16 = jnp.bfloat16
AXES = ("node", "dev")
SWAPPED = ("dev", "node")
MIB = 1 << 20
VMEM_LIMIT = 48 * MIB
VMEM_SMALL = 16 * MIB
VMEM_LARGE = 56 * MIB


def pass_matrix(n):
    low, high = np.eye(n)[0::2], np.eye(n)[1::2]

    def after(v):
        return np.concatenate([v[1:], v[-1:]], 0)

    def before(v):
        return np.concatenate([v[:1], v[:-1]], 0)

    high = high + ALPHA * (low + after(low))
    low = low + BETA * (before(high) + high)
    high = high + GAMMA * (low + after(low))
    low = low + DELTA * (before(high) + high)
    return np.concatenate([low / SCALE, high * SCALE], 0)


def three_terms(matrix):
    rest = np.asarray(matrix, np.float32)
    terms = []
    for _ in range(3):
        terms.append(rest.astype(BF16))
        rest = rest - terms[-1].astype(np.float32)
    return terms


def left_terms(matrix):
    first, second, third = three_terms(matrix)
    return np.concatenate([first, first, first, second, second, third], 1)


def split(value):
    terms = []
    for _ in range(3):
        terms.append(value.astype(BF16))
        value = value - terms[-1].astype(F32)
    return terms


def dot(left, right):
    return jnp.dot(left, right, preferred_element_type=F32)


def times(value, first, second, third):
    high, middle, low = split(value)
    count = value.shape[0]
    one = dot(jnp.concatenate([high, middle, low], 0), first)
    two = dot(jnp.concatenate([high, middle], 0), second)
    small = (one[2 * count :] + two[count:]) + dot(high, third)
    return one[:count] + ((one[count : 2 * count] + two[:count]) + small)


def times_left(terms, value):
    high, middle, low = split(value)
    return dot(terms, jnp.concatenate([high, middle, low, high, middle, high], 0))


def split_rows(rows):
    return [split(jnp.concatenate(rows[m : m + 2], 0)) for m in range(0, len(rows), 2)]


def tiled_view(density):
    slots, edge, plane = density.shape
    view = density.reshape(slots, edge // 8, 8, plane // 128, 128)
    return jnp.transpose(view, (0, 1, 3, 2, 4))


def tile_rows(ref, block, group, edge, tiles):
    base = block * edge * tiles + 64 * group
    return [ref[pl.ds(base + (x // 8) * 8 * tiles + x % 8, 8, stride=8), :] for x in range(edge)]


def lowpass_kernel(
    count_ref, x_any, wz_any, wy_any, out_ref, token_ref, x_ref, wz_ref, wy_ref, l_ref, z_ref, sems, w_sems
):
    slots, edge, tiles = x_any.shape[0], 8 * x_any.shape[1], x_any.shape[2]
    quarter = edge // 4
    rows_all = slots * 8 * quarter
    token_ref[0] = count_ref[0]
    blocks = [
        pltpu.make_async_copy(x_any.at[n], x_ref.at[n], sems.at[n]) for n in range(slots)
    ]
    for copy in blocks:
        copy.start()
    flat = x_ref.reshape(slots * edge * tiles, 128)
    weights = [
        pltpu.make_async_copy(src, dst, w_sems.at[i])
        for i, (src, dst) in enumerate(((wz_any, wz_ref), (wy_any, wy_ref)))
    ]
    for copy in weights:
        copy.start()
    for s in range(slots):
        blocks[s].wait()

        @pl.loop(0, 2)
        def _(q):
            for u in range(2):
                rows = tile_rows(flat, s, 2 * q + u, edge, tiles)
                rows, _ = lift(rows[0::2], rows[1::2], edge // 2, False, False)
                rows, _ = lift(rows[0::2], rows[1::2], quarter, False, False)
                for m, terms in enumerate(split_rows(rows)):
                    cols = pl.ds(pl.multiple_of(u * 256 + q * 128, 128), 128)
                    for n, term in enumerate(terms):
                        l_ref[pl.ds(n * rows_all + s * 8 * quarter + 16 * m, 16), cols] = term

    for copy in weights:
        copy.wait()
    made = dot(l_ref[...], wz_ref[:, :256])
    small = (made[2 * rows_all :, :128] + made[rows_all : 2 * rows_all, 128:]) + dot(
        l_ref[pl.ds(0, rows_all), :], wz_ref[:, 256:]
    )
    z_ref[...] = made[:rows_all, :128] + (
        (made[rows_all : 2 * rows_all, :128] + made[:rows_all, 128:]) + small
    )
    wide = jnp.concatenate([z_ref[pl.ds(i, slots * quarter, stride=8), :] for i in range(8)], 1)
    made = times(wide, wy_ref[0], wy_ref[1], wy_ref[2])
    out_ref[...] = jnp.full(out_ref.shape, count_ref[0].astype(F32))
    for slot in range(slots):
        for h in range(2):
            out_ref[pl.ds(8 * h + slot, quarter, stride=16), :] = made[
                slot * quarter : (slot + 1) * quarter, h * 128 : h * 128 + 128
            ]


def triple(matrix):
    return np.stack([np.concatenate([term] * 3, 0) for term in three_terms(matrix)])


def lowpass_call(owner_counts, density):
    slots, edge, plane = density.shape
    quarter = edge // 4
    two_levels = pass_matrix(edge // 2)[:quarter] @ pass_matrix(edge)[: edge // 2]
    wz = np.concatenate(three_terms(np.kron(np.eye(8), two_levels.T)), 1)
    i, gp, q, p = np.meshgrid(np.arange(8), np.arange(2), np.arange(2), np.arange(2), indexing="ij")
    entry = (2 * (8 * gp + i) + p + 32 * q).reshape(-1)
    wy = np.kron(two_levels.T[entry] / SQUARE, np.eye(quarter))
    wy = np.stack(three_terms(wy))
    anywhere = pl.BlockSpec(memory_space=pl.ANY)
    vmem = pl.BlockSpec(memory_space=pltpu.VMEM)
    rows_all = slots * 8 * quarter
    pieces, token = pl.pallas_call(
        lowpass_kernel,
        in_specs=[pl.BlockSpec(memory_space=pltpu.SMEM)] + [anywhere] * 3,
        out_specs=[vmem, pl.BlockSpec(memory_space=pltpu.SMEM)],
        out_shape=[
            jax.ShapeDtypeStruct((16 * quarter, 128), F32),
            jax.ShapeDtypeStruct((1,), jnp.int32),
        ],
        scratch_shapes=[
            pltpu.VMEM((slots, edge // 8, plane // 128, 8, 128), F32),
            pltpu.VMEM(wz.shape, BF16),
            pltpu.VMEM(wy.shape, BF16),
            pltpu.VMEM((3 * rows_all, 512), BF16),
            pltpu.VMEM((rows_all, 128), F32),
            pltpu.SemaphoreType.DMA((slots,)),
            pltpu.SemaphoreType.DMA((2,)),
        ],
        compiler_params=pltpu.CompilerParams(vmem_limit_bytes=VMEM_LARGE),
        name="lowpass",
    )(owner_counts, tiled_view(density), wz, wy)
    return pieces.reshape(2 * quarter, 8, 128), token


def route_kernel(me_ref, got_ref, _, send_ref, index_ref, order_ref, count_ref, sem, *, width):
    devices = got_ref.shape[0]
    place = [d % width * (devices // width) + d // width for d in range(devices)]
    copy = pltpu.make_async_copy(got_ref.at[:, 7, :], count_ref, sem)
    copy.start()
    order_ref[...] = jnp.zeros_like(order_ref)
    copy.wait()
    start, my_start, my_count = 0, 0, 0
    starts = []
    for d in range(devices):
        count = count_ref[place[d], 0].astype(jnp.int32)
        starts.append(start)
        my_start = jnp.where(me_ref[0] == d, start, my_start)
        my_count = jnp.where(me_ref[0] == d, count, my_count)
        order_ref[pl.ds(start, 8), :] = got_ref[place[d]]
        start = start + count
    index_ref[0] = my_start % 8
    index_ref[1] = my_count
    for d in range(devices):
        at = pl.multiple_of(starts[d] // 8 * 8, 8) if d else 0
        send_ref[place[d]] = order_ref[pl.ds(at, 16), :]


def route_call(me, got, token, slots, width):
    devices = got.shape[0]
    return pl.pallas_call(
        functools.partial(route_kernel, width=width),
        in_specs=[
            pl.BlockSpec(memory_space=pltpu.SMEM),
            pl.BlockSpec(memory_space=pltpu.VMEM),
            pl.BlockSpec(memory_space=pltpu.SMEM),
        ],
        out_specs=[pl.BlockSpec(memory_space=pltpu.VMEM), pl.BlockSpec(memory_space=pltpu.SMEM)],
        out_shape=[
            jax.ShapeDtypeStruct((devices, 16, 128), F32),
            jax.ShapeDtypeStruct((2,), jnp.int32),
        ],
        scratch_shapes=[
            pltpu.VMEM((devices * slots + 16, 128), F32),
            pltpu.SMEM((devices, 128), F32),
            pltpu.SemaphoreType.DMA,
        ],
        compiler_params=pltpu.CompilerParams(vmem_limit_bytes=VMEM_SMALL),
        name="route",
    )(me, got, token)


def lift(low, high, n, halo, scaled):
    up = SQUARE if scaled else 1.0
    at = 2 if halo else 0
    first, second, third, fourth = ({} for _ in range(4))

    def get(values, i, is_low):
        if halo:
            return values[i]
        return values[min(i, n - 1)] if is_low else values[max(i, 0)]

    lows = {i - at: low[i] for i in range(len(low))}
    highs = {i - at: high[i] for i in range(len(high))}

    def make_first(i):
        first[i] = highs[i] + (ALPHA * up) * (lows[i] + get(lows, i + 1, True))

    def make_second(i):
        second[i] = lows[i] + (BETA / up) * (get(first, i - 1, False) + first[i])

    def make_third(i):
        third[i] = first[i] + (GAMMA * up) * (second[i] + get(second, i + 1, True))

    def make_fourth(i):
        fourth[i] = second[i] + (DELTA / up) * (get(third, i - 1, False) + third[i])

    if halo:
        for i in range(-2, n + 1):
            make_first(i)
            if i >= -1:
                make_second(i)
            if i >= 0:
                make_third(i - 1)
            if i >= 1:
                make_fourth(i - 1)
    else:
        for i in range(n):
            make_first(i)
            make_second(i)
            if i >= 1:
                make_third(i - 1)
                make_fourth(i - 1)
        make_third(n - 1)
        make_fourth(n - 1)
    return [fourth[i] for i in range(n)], [third[i] for i in range(n)]


def fine_kernel(count_ref, _, x_any, w1_ref, w2_ref, *refs, first):
    out_ref, token_ref, x_buf, l_ref, y_ref, c_ref, m_ref, d_ref, sems = refs[-9:]
    step = pl.program_id(0)
    slot = step + first
    edge, tiles = 8 * x_any.shape[1], x_any.shape[2]
    pairs = tiles // 2
    half = edge // 2
    corner = 8 * half
    live = slot < count_ref[0]
    lane = lax.broadcasted_iota(jnp.int32, (8, 128), 1)
    front = lane < 64
    inner = (lane & 63) < half
    token_ref[0] = step

    def cross(a, b):
        return pltpu.roll(jnp.where(front, b, a), 64, 1)

    def exchange(a, b):
        crossed = cross(a, b)
        return jnp.where(front, a, crossed), jnp.where(front, crossed, b)

    def with_halo(low, high):
        one, two = cross(low[0], low[-1]), cross(low[1], low[-2])
        low_all = [jnp.where(front, low[2], two), jnp.where(front, low[1], one)] + low
        low_all += [jnp.where(front, one, low[-1]), jnp.where(front, two, low[-2])]
        one, two = cross(high[0], high[-1]), cross(high[1], high[-2])
        high_all = [jnp.where(front, high[1], two), jnp.where(front, high[0], one)] + high
        return low_all, high_all + [jnp.where(front, one, high[-2])]

    def scaled_rows(rows):
        low, high = lift(rows[0::2], rows[1::2], len(rows) // 2, False, False)
        return [v * (1.0 / SCALE) for v in low] + [v * SCALE for v in high]

    def store_terms(ref, row, col, rows):
        for m, terms in enumerate(split_rows(rows)):
            place = pl.ds(pl.multiple_of(row + 16 * m, 16), 16)
            for n, term in enumerate(terms):
                ref[place, pl.ds(256 * n + col, 128)] = term

    def fetch(which, place):
        return pltpu.make_async_copy(x_any.at[which], x_buf.at[place], sems.at[place])

    @pl.when((step == 0) & live)
    def _():
        fetch(slot, 0).start()

    @pl.when(jnp.logical_not(live))
    def _():
        out_ref[...] = jnp.zeros_like(out_ref)

    @pl.when(live)
    def _():
        fetch(slot, step % 2).wait()

    @pl.when((step + 1 < pl.num_programs(0)) & (slot + 1 < count_ref[0]))
    def _():
        fetch(slot + 1, (step + 1) % 2).start()

    @pl.when(live)
    def _():
        flat = x_buf.reshape(2 * edge * tiles, 128)
        for g in range(4):
            rows = scaled_rows(tile_rows(flat, step % 2, g, edge, tiles))
            store_terms(l_ref, (g % 2) * 8 * edge, (g // 2) * 128, rows)
        lifted = dot(l_ref[...], w1_ref[0]) + dot(l_ref[:, :512], w1_ref[1, :512])
        lifted += dot(l_ref[:, :256], w1_ref[2, :256])
        y_ref[0] = lifted[:, :128]
        y_ref[1] = lifted[:, 128:]
        for r in range(edge // 8):
            rows = pl.ds(8 * r, 8)

            def tile(part, j):
                return y_ref[part, pl.ds((j // 8) * 8 * edge + 64 * r + j % 8, 8, stride=8), :]

            low = [tile(0, j) for j in range(pairs)]
            high = [tile(1, j) for j in range(pairs)]
            low, high = lift(*with_halo(low, high), pairs, True, True)
            for part, values in enumerate((low, high)):
                for t in range(pairs // 2):
                    a, b = exchange(values[2 * t], values[2 * t + 1])
                    at = part * pairs + t
                    out_ref[0, rows, pl.ds(at * 128, 128)] = a
                    out_ref[0, rows, pl.ds((at + pairs // 2) * 128, 128)] = b
            if r < half // 8:
                low, high = lift(*with_halo(low[0::2], low[1::2]), 8, True, False)
                for i in range(8):
                    c_ref[pl.ds(64 * r + i, 8, stride=8), :] = low[i]
                    c_ref[pl.ds(corner + 64 * r + i, 8, stride=8), :] = high[i]
        for u in range(2):
            rows = scaled_rows([c_ref[pl.ds(u * corner + 8 * i, 8), :] for i in range(half)])
            store_terms(m_ref, 0, u * 128, rows)
        lifted = dot(m_ref[...], w2_ref[0]) + dot(m_ref[:, :512], w2_ref[1, :512])
        lifted += dot(m_ref[:, :256], w2_ref[2, :256])
        d_ref[0] = lifted[:, :128]
        d_ref[1] = lifted[:, 128:]
        for u in range(2):
            for t in range(4):
                for r in range(half // 8):
                    a = d_ref[u, pl.ds(64 * r + 2 * t, 8, stride=8), :]
                    b = d_ref[u, pl.ds(64 * r + 2 * t + 1, 8, stride=8), :]
                    for at, value in zip((u * 8 + t, u * 8 + 4 + t), exchange(a, b)):
                        rows, cols = pl.ds(8 * r, 8), pl.ds(at * 128, 128)
                        out_ref[0, rows, cols] = jnp.where(inner, value, out_ref[0, rows, cols])


def fine_call(owner_counts, token, density, first, last, before=None):
    slots, edge, plane = density.shape
    tiles = plane // 128
    half = edge // 2
    pairs = tiles // 2
    count = last - first
    one = pass_matrix(edge).T
    zero = np.zeros_like(one)
    w1 = np.block(
        [
            [one / SCALE, zero, zero, zero],
            [zero, zero, one * SCALE, zero],
            [zero, one / SCALE, zero, zero],
            [zero, zero, zero, one * SCALE],
        ]
    )
    two = np.zeros_like(one)
    two[:half, :half] = pass_matrix(half).T
    w2 = np.kron(np.diag([1 / SCALE, 1 / SCALE, SCALE, SCALE]), two)
    anywhere = pl.BlockSpec(memory_space=pl.ANY)
    smem = pl.BlockSpec(memory_space=pltpu.SMEM)
    old = [] if before is None else [before]
    fixed = pl.BlockSpec((3, 768, 256), lambda s: (0, 0, 0))
    return pl.pallas_call(
        functools.partial(fine_kernel, first=first),
        grid=(count,),
        in_specs=[smem, smem, anywhere, fixed, fixed] + [anywhere] * len(old),
        out_specs=[pl.BlockSpec((1, edge, plane), lambda s: (s + first, 0, 0)), smem],
        out_shape=[
            jax.ShapeDtypeStruct(density.shape, F32),
            jax.ShapeDtypeStruct((1,), jnp.int32),
        ],
        scratch_shapes=[
            pltpu.VMEM((2, edge // 8, tiles, 8, 128), F32),
            pltpu.VMEM((pairs * edge, 768), BF16),
            pltpu.VMEM((2, pairs * edge, 128), F32),
            pltpu.VMEM((16 * half, 128), F32),
            pltpu.VMEM((8 * half, 768), BF16),
            pltpu.VMEM((2, 8 * half, 128), F32),
            pltpu.SemaphoreType.DMA((2,)),
        ],
        input_output_aliases={5: 0} if old else {},
        compiler_params=pltpu.CompilerParams(vmem_limit_bytes=VMEM_LIMIT),
        cost_estimate=pl.CostEstimate(
            flops=6 * count * edge * plane * 256, bytes_accessed=2 * count * MIB, transcendentals=0
        ),
        name="fine",
    )(owner_counts, token, tiled_view(density), triple(w1), triple(w2), *old)


def coarse_kernel(
    index_ref,
    piece_ref,
    wx_ref,
    wz_ref,
    wy_ref,
    w23_ref,
    wx2_ref,
    wx3_ref,
    fine_ref,
    out_ref,
    block_ref,
    corner_ref,
    corner_sem,
    out_sem,
):
    slots = corner_ref.shape[0]
    lane = lax.broadcasted_iota(jnp.int32, (16, 128), 1)

    def window(s):
        return out_ref.at[s, pl.ds(0, 16), pl.ds(0, 1024)]

    def piece(i):
        return jnp.concatenate([piece_ref[pl.ds(16 * h + i, 16, stride=32), :] for h in range(2)], 1)

    for s in range(slots):
        pltpu.make_async_copy(window(s), corner_ref.at[s], corner_sem.at[s]).start()

    first = [
        [
            times_left(wx_ref[...], jnp.concatenate([piece(o * 8 + 2 * q), piece(o * 8 + 2 * q + 1)], 0))
            for q in range(4)
        ]
        for o in range(2)
    ]
    stacked = []
    for o in range(2):
        for cy in range(2):
            for yh in range(2):
                part = slice(yh * 128, yh * 128 + 128)
                stacked.append(jnp.concatenate([first[o][cy][:, part], first[o][2 + cy][:, part]], 1))
    lifted = times(jnp.concatenate(stacked, 0), wz_ref[0], wz_ref[1], wz_ref[2])
    stacked = []
    for o in range(2):
        for tz in range(2):
            stacked.append(
                jnp.concatenate(
                    [lifted[(o * 4 + u) * 32 : (o * 4 + u + 1) * 32, tz * 128 : tz * 128 + 128] for u in range(4)],
                    1,
                )
            )
    lifted = times(jnp.concatenate(stacked, 0), wy_ref[0], wy_ref[1], wy_ref[2])
    corner = []
    for o in range(2):
        for tz in range(2):
            for ty in range(2):
                for tx in range(2):
                    at = (o * 2 + tz) * 32 + tx * 16
                    value = lifted[at : at + 16, ty * 256 : ty * 256 + 256]
                    if tx + ty + tz == 0:
                        corner.append(value)
                    else:
                        block_ref[o * 8 + tx + 2 * ty + 4 * tz] = value
    both = times(jnp.concatenate(corner, 0), w23_ref[0], w23_ref[1], w23_ref[2])
    depth = lax.broadcasted_iota(jnp.int32, (16, 128), 0)
    small = (depth < 8) & ((lane & 15) < 8)
    for o in range(2):
        mine = both[o * 16 : o * 16 + 16]
        second = times_left(wx2_ref[...], mine[:, :256])
        third = times_left(wx3_ref[...], mine[:, 256:])
        block_ref[o * 8] = jnp.concatenate(
            [jnp.where(small, third, second[:, :128]), second[:, 128:]], 1
        )

    for s in range(slots):
        pltpu.make_async_copy(window(s), corner_ref.at[s], corner_sem.at[s]).wait()
    placed = (lane & 63) < 16
    for s in range(slots):
        value = block_ref[index_ref[0] + s]
        for t in range(8):
            tile = value[:, (t // 4) * 128 : (t // 4) * 128 + 128]
            if t % 4:
                tile = pltpu.roll(tile, 128 - 16 * (t % 4), 1)
            cols = pl.ds(t * 128, 128)
            corner_ref[s, :, cols] = jnp.where(placed, tile, corner_ref[s, :, cols])
    for s in range(slots):

        @pl.when(s < index_ref[1])
        def _():
            pltpu.make_async_copy(corner_ref.at[s], window(s), out_sem.at[s]).start()

    for s in range(slots):

        @pl.when(s < index_ref[1])
        def _():
            pltpu.make_async_copy(corner_ref.at[s], window(s), out_sem.at[s]).wait()


def coarse_call(index, pieces, fine):
    slots, edge, plane = fine.shape
    m32, m16, m8 = pass_matrix(32), pass_matrix(16), pass_matrix(8)
    deep = np.zeros((16, 16))
    deep[:8] = m8 @ m16[:8]
    eye8, eye16 = np.eye(8), np.eye(16)
    wz = np.zeros((256, 256))
    for cz in range(2):
        for tz in range(2):
            wz[cz * 128 : cz * 128 + 128, tz * 128 : tz * 128 + 128] = np.kron(
                eye8, m32[tz * 16 : tz * 16 + 16, cz * 16 : cz * 16 + 16].T
            )
    lanes = np.arange(256).reshape(2, 4, 2, 16).transpose(0, 2, 1, 3).reshape(-1)
    wy = np.kron(m32.T, eye16)[:, np.concatenate([lanes, 256 + lanes])]
    w23 = np.concatenate([np.kron(m16.T, m16.T)[:, lanes], np.kron(deep.T, deep.T)[:, lanes[:128]]], 1)[lanes]
    weights = [
        left_terms(m32),
        np.stack(three_terms(wz)),
        np.stack(three_terms(wy)),
        np.stack(three_terms(w23)),
        left_terms(m16),
        left_terms(deep),
    ]
    anywhere = pl.BlockSpec(memory_space=pl.ANY)
    vmem = pl.BlockSpec(memory_space=pltpu.VMEM)
    return pl.pallas_call(
        coarse_kernel,
        in_specs=[pl.BlockSpec(memory_space=pltpu.SMEM), vmem] + [vmem] * len(weights) + [anywhere],
        out_specs=anywhere,
        out_shape=jax.ShapeDtypeStruct(fine.shape, F32),
        scratch_shapes=[
            pltpu.VMEM((16, 16, 256), F32),
            pltpu.VMEM((slots, 16, 1024), F32),
            pltpu.SemaphoreType.DMA((slots,)),
            pltpu.SemaphoreType.DMA((slots,)),
        ],
        input_output_aliases={2 + len(weights): 0},
        compiler_params=pltpu.CompilerParams(vmem_limit_bytes=VMEM_SMALL),
        name="coarse",
    )(index, pieces.reshape(-1, 128), *weights, fine)


def exchange(lowpass, slots, token):
    me = lax.axis_index(AXES)
    devices = lax.axis_size(AXES)
    if devices == lowpass.shape[0]:
        got = lax.all_to_all(lowpass, SWAPPED, 0, 0, tiled=True)
        sent, index = route_call(me.reshape(1), got, token, slots, lax.axis_size("dev"))
        return lax.all_to_all(sent, SWAPPED, 0, 0, tiled=True), index
    every = lax.all_gather(lowpass, AXES, axis=0)
    counts = every[:, 0, 7, 0].astype(jnp.int32)
    starts = jnp.cumsum(counts) - counts
    blocks = starts[me] // 8 * 8 + jnp.arange(16, dtype=jnp.int32)
    owners = jnp.sum((starts[None, :] <= blocks[:, None]).astype(jnp.int32), axis=1) - 1
    place = jnp.minimum(blocks - starts[owners], slots - 1)
    pieces = jnp.transpose(every[owners, :, place], (1, 0, 2))
    return pieces, jnp.stack([starts[me] % 8, counts[me]])


def per_device(density, owner_counts):
    slots = density.shape[0]
    early = slots // 3
    lowpass, token = lowpass_call(owner_counts, density)
    fine, token = fine_call(owner_counts, token, density, 0, early)
    pieces, index = exchange(lowpass, slots, token)
    fine, _ = fine_call(owner_counts, index, density, early, slots, fine)
    return coarse_call(index, pieces, fine)


def solution(mesh):
    in_specs = (P(AXES, None, None), P(AXES))
    out_specs = P(AXES, None, None)
    return jax.shard_map(per_device, mesh=mesh, in_specs=in_specs, out_specs=out_specs, check_vma=False)
```

```python
import functools

import jax
import jax.numpy as jnp
import numpy as np
from jax import lax
from jax.experimental import pallas as pl
from jax.experimental.pallas import tpu as pltpu
from jax.sharding import PartitionSpec as P

ALPHA = -1.586134342059924
BETA = -0.052980118572961
GAMMA = 0.882911075530934
DELTA = 0.443506852043971
SCALE = 1.230174104914001
SQUARE = SCALE * SCALE
F32 = jnp.float32
BF16 = jnp.bfloat16
AXES = ("node", "dev")
SWAPPED = ("dev", "node")
MIB = 1 << 20
VMEM_LIMIT = 48 * MIB
VMEM_SMALL = 16 * MIB
VMEM_LARGE = 56 * MIB


def pass_matrix(n):
    low, high = np.eye(n)[0::2], np.eye(n)[1::2]

    def after(v):
        return np.concatenate([v[1:], v[-1:]], 0)

    def before(v):
        return np.concatenate([v[:1], v[:-1]], 0)

    high = high + ALPHA * (low + after(low))
    low = low + BETA * (before(high) + high)
    high = high + GAMMA * (low + after(low))
    low = low + DELTA * (before(high) + high)
    return np.concatenate([low / SCALE, high * SCALE], 0)


def two_terms(matrix):
    matrix = np.asarray(matrix, np.float32)
    first = matrix.astype(BF16)
    return first, (matrix - first.astype(np.float32)).astype(BF16)


def left_terms(matrix):
    first, second = two_terms(matrix)
    return np.concatenate([first, second, first], 1)


def split(value):
    first = value.astype(BF16)
    return first, (value - first.astype(F32)).astype(BF16)


def dot(left, right):
    return jnp.dot(left, right, preferred_element_type=F32)


def times(value, first, second):
    high, low = split(value)
    both = dot(jnp.concatenate([high, low], 0), first)
    count = value.shape[0]
    return both[:count] + both[count:] + dot(high, second)


def times_left(terms, value):
    high, low = split(value)
    return dot(terms, jnp.concatenate([high, high, low], 0))


def split_rows(rows):
    return [split(jnp.concatenate(rows[m : m + 2], 0)) for m in range(0, len(rows), 2)]


def tiled_view(density):
    slots, edge, plane = density.shape
    view = density.reshape(slots, edge // 8, 8, plane // 128, 128)
    return jnp.transpose(view, (0, 1, 3, 2, 4))


def tile_rows(ref, block, group, edge, tiles):
    base = block * edge * tiles + 64 * group
    return [ref[pl.ds(base + (x // 8) * 8 * tiles + x % 8, 8, stride=8), :] for x in range(edge)]


def lowpass_kernel(
    count_ref, x_any, wz_any, wy_ref, out_ref, token_ref, x_ref, wz_ref, wyh_ref, wyl_ref, l_ref, z_ref, sems, w_sem
):
    slots, edge, tiles = x_any.shape[0], 8 * x_any.shape[1], x_any.shape[2]
    quarter = edge // 4
    rows_all = slots * 8 * quarter
    token_ref[0] = count_ref[0]
    blocks = [
        pltpu.make_async_copy(x_any.at[n], x_ref.at[n], sems.at[n]) for n in range(slots)
    ]
    for copy in blocks:
        copy.start()
    flat = x_ref.reshape(slots * edge * tiles, 128)
    weights = pltpu.make_async_copy(wz_any, wz_ref, w_sem)
    weights.start()
    same = lax.broadcasted_iota(jnp.int32, (16, 256), 0) == (
        lax.broadcasted_iota(jnp.int32, (16, 256), 1) & 15
    )
    for k in range(edge):
        for term, ref in enumerate((wyh_ref, wyl_ref)):
            row = jnp.broadcast_to(wy_ref[term, pl.ds(k, 1), :], (16, 256))
            ref[pl.ds(16 * k, 16), :] = jnp.where(same, row, 0.0).astype(BF16)
    for s in range(slots):
        blocks[s].wait()

        @pl.loop(0, 2)
        def _(q):
            for u in range(2):
                rows = tile_rows(flat, s, 2 * q + u, edge, tiles)
                rows, _ = lift(rows[0::2], rows[1::2], edge // 2, False, False)
                rows, _ = lift(rows[0::2], rows[1::2], quarter, False, False)
                for m, (high, low) in enumerate(split_rows(rows)):
                    at = s * 8 * quarter + 16 * m
                    cols = pl.ds(pl.multiple_of(u * 256 + q * 128, 128), 128)
                    l_ref[pl.ds(at, 16), cols] = high
                    l_ref[pl.ds(rows_all + at, 16), cols] = low

    weights.wait()
    made = dot(l_ref[...], wz_ref[...])
    z_ref[...] = (made[:rows_all, :128] + made[rows_all:, :128]) + made[:rows_all, 128:]
    wide = jnp.concatenate([z_ref[pl.ds(i, slots * quarter, stride=8), :] for i in range(8)], 1)
    made = times(wide, wyh_ref[...], wyl_ref[...])
    out_ref[...] = jnp.full(out_ref.shape, count_ref[0].astype(F32))
    for slot in range(slots):
        for h in range(2):
            out_ref[pl.ds(8 * h + slot, quarter, stride=16), :] = made[
                slot * quarter : (slot + 1) * quarter, h * 128 : h * 128 + 128
            ]


def stacked(matrix):
    first, second = two_terms(matrix)
    return np.concatenate([first, first, second], 0)


def lowpass_call(owner_counts, density):
    slots, edge, plane = density.shape
    quarter = edge // 4
    two_levels = pass_matrix(edge // 2)[:quarter] @ pass_matrix(edge)[: edge // 2]
    wz = np.concatenate(two_terms(np.kron(np.eye(8), two_levels.T)), 1)
    i, gp, q, p = np.meshgrid(np.arange(8), np.arange(2), np.arange(2), np.arange(2), indexing="ij")
    entry = (2 * (8 * gp + i) + p + 32 * q).reshape(-1)
    wy = np.repeat(two_levels.T[entry] / SQUARE, quarter, 1)
    wy = np.stack([term.astype(np.float32) for term in two_terms(wy)])
    anywhere = pl.BlockSpec(memory_space=pl.ANY)
    vmem = pl.BlockSpec(memory_space=pltpu.VMEM)
    rows_all = slots * 8 * quarter
    pieces, token = pl.pallas_call(
        lowpass_kernel,
        in_specs=[pl.BlockSpec(memory_space=pltpu.SMEM)] + [anywhere] * 2 + [vmem],
        out_specs=[vmem, pl.BlockSpec(memory_space=pltpu.SMEM)],
        out_shape=[
            jax.ShapeDtypeStruct((16 * quarter, 128), F32),
            jax.ShapeDtypeStruct((1,), jnp.int32),
        ],
        scratch_shapes=[
            pltpu.VMEM((slots, edge // 8, plane // 128, 8, 128), F32),
            pltpu.VMEM(wz.shape, BF16),
            pltpu.VMEM((quarter * edge, quarter * quarter), BF16),
            pltpu.VMEM((quarter * edge, quarter * quarter), BF16),
            pltpu.VMEM((2 * rows_all, 512), BF16),
            pltpu.VMEM((rows_all, 128), F32),
            pltpu.SemaphoreType.DMA((slots,)),
            pltpu.SemaphoreType.DMA,
        ],
        compiler_params=pltpu.CompilerParams(vmem_limit_bytes=VMEM_LARGE),
        name="lowpass",
    )(owner_counts, tiled_view(density), wz, wy)
    return pieces.reshape(2 * quarter, 8, 128), token


def route_kernel(me_ref, got_ref, _, send_ref, index_ref, order_ref, count_ref, sem, *, width):
    devices = got_ref.shape[0]
    place = [d % width * (devices // width) + d // width for d in range(devices)]
    copy = pltpu.make_async_copy(got_ref.at[:, 7, :], count_ref, sem)
    copy.start()
    order_ref[...] = jnp.zeros_like(order_ref)
    copy.wait()
    start, my_start, my_count = 0, 0, 0
    starts = []
    for d in range(devices):
        count = count_ref[place[d], 0].astype(jnp.int32)
        starts.append(start)
        my_start = jnp.where(me_ref[0] == d, start, my_start)
        my_count = jnp.where(me_ref[0] == d, count, my_count)
        order_ref[pl.ds(start, 8), :] = got_ref[place[d]]
        start = start + count
    index_ref[0] = my_start % 8
    index_ref[1] = my_count
    for d in range(devices):
        at = pl.multiple_of(starts[d] // 8 * 8, 8) if d else 0
        send_ref[place[d]] = order_ref[pl.ds(at, 16), :]


def route_call(me, got, token, slots, width):
    devices = got.shape[0]
    return pl.pallas_call(
        functools.partial(route_kernel, width=width),
        in_specs=[
            pl.BlockSpec(memory_space=pltpu.SMEM),
            pl.BlockSpec(memory_space=pltpu.VMEM),
            pl.BlockSpec(memory_space=pltpu.SMEM),
        ],
        out_specs=[pl.BlockSpec(memory_space=pltpu.VMEM), pl.BlockSpec(memory_space=pltpu.SMEM)],
        out_shape=[
            jax.ShapeDtypeStruct((devices, 16, 128), F32),
            jax.ShapeDtypeStruct((2,), jnp.int32),
        ],
        scratch_shapes=[
            pltpu.VMEM((devices * slots + 16, 128), F32),
            pltpu.SMEM((devices, 128), F32),
            pltpu.SemaphoreType.DMA,
        ],
        compiler_params=pltpu.CompilerParams(vmem_limit_bytes=VMEM_SMALL),
        name="route",
    )(me, got, token)


def lift(low, high, n, halo, scaled):
    up = SQUARE if scaled else 1.0
    at = 2 if halo else 0
    first, second, third, fourth = ({} for _ in range(4))

    def get(values, i, is_low):
        if halo:
            return values[i]
        return values[min(i, n - 1)] if is_low else values[max(i, 0)]

    lows = {i - at: low[i] for i in range(len(low))}
    highs = {i - at: high[i] for i in range(len(high))}

    def make_first(i):
        first[i] = highs[i] + (ALPHA * up) * (lows[i] + get(lows, i + 1, True))

    def make_second(i):
        second[i] = lows[i] + (BETA / up) * (get(first, i - 1, False) + first[i])

    def make_third(i):
        third[i] = first[i] + (GAMMA * up) * (second[i] + get(second, i + 1, True))

    def make_fourth(i):
        fourth[i] = second[i] + (DELTA / up) * (get(third, i - 1, False) + third[i])

    if halo:
        for i in range(-2, n + 1):
            make_first(i)
            if i >= -1:
                make_second(i)
            if i >= 0:
                make_third(i - 1)
            if i >= 1:
                make_fourth(i - 1)
    else:
        for i in range(n):
            make_first(i)
            make_second(i)
            if i >= 1:
                make_third(i - 1)
                make_fourth(i - 1)
        make_third(n - 1)
        make_fourth(n - 1)
    return [fourth[i] for i in range(n)], [third[i] for i in range(n)]


def fine_kernel(count_ref, _, x_any, w1_ref, w2_ref, *refs, first):
    out_ref, token_ref, x_buf, l_ref, y_ref, c_ref, m_ref, d_ref, sems = refs[-9:]
    step = pl.program_id(0)
    slot = step + first
    edge, tiles = 8 * x_any.shape[1], x_any.shape[2]
    pairs = tiles // 2
    half = edge // 2
    corner = 8 * half
    live = slot < count_ref[0]
    lane = lax.broadcasted_iota(jnp.int32, (8, 128), 1)
    front = lane < 64
    inner = (lane & 63) < half
    token_ref[0] = step

    def cross(a, b):
        return pltpu.roll(jnp.where(front, b, a), 64, 1)

    def exchange(a, b):
        crossed = cross(a, b)
        return jnp.where(front, a, crossed), jnp.where(front, crossed, b)

    def with_halo(low, high):
        one, two = cross(low[0], low[-1]), cross(low[1], low[-2])
        low_all = [jnp.where(front, low[2], two), jnp.where(front, low[1], one)] + low
        low_all += [jnp.where(front, one, low[-1]), jnp.where(front, two, low[-2])]
        one, two = cross(high[0], high[-1]), cross(high[1], high[-2])
        high_all = [jnp.where(front, high[1], two), jnp.where(front, high[0], one)] + high
        return low_all, high_all + [jnp.where(front, one, high[-2])]

    def scaled_rows(rows):
        low, high = lift(rows[0::2], rows[1::2], len(rows) // 2, False, False)
        return [v * (1.0 / SCALE) for v in low] + [v * SCALE for v in high]

    def store_terms(ref, row, col, rows):
        for m, (high, low) in enumerate(split_rows(rows)):
            place = pl.ds(pl.multiple_of(row + 16 * m, 16), 16)
            ref[place, pl.ds(col, 128)] = high
            ref[place, pl.ds(256 + col, 128)] = low
            ref[place, pl.ds(512 + col, 128)] = high

    def fetch(which, place):
        return pltpu.make_async_copy(x_any.at[which], x_buf.at[place], sems.at[place])

    @pl.when((step == 0) & live)
    def _():
        fetch(slot, 0).start()

    @pl.when(jnp.logical_not(live))
    def _():
        out_ref[...] = jnp.zeros_like(out_ref)

    @pl.when(live)
    def _():
        fetch(slot, step % 2).wait()

    @pl.when((step + 1 < pl.num_programs(0)) & (slot + 1 < count_ref[0]))
    def _():
        fetch(slot + 1, (step + 1) % 2).start()

    @pl.when(live)
    def _():
        flat = x_buf.reshape(2 * edge * tiles, 128)
        for g in range(4):
            rows = scaled_rows(tile_rows(flat, step % 2, g, edge, tiles))
            store_terms(l_ref, (g % 2) * 8 * edge, (g // 2) * 128, rows)
        lifted = dot(l_ref[...], w1_ref[...])
        y_ref[0] = lifted[:, :128]
        y_ref[1] = lifted[:, 128:]
        for r in range(edge // 8):
            rows = pl.ds(8 * r, 8)

            def tile(part, j):
                return y_ref[part, pl.ds((j // 8) * 8 * edge + 64 * r + j % 8, 8, stride=8), :]

            low = [tile(0, j) for j in range(pairs)]
            high = [tile(1, j) for j in range(pairs)]
            low, high = lift(*with_halo(low, high), pairs, True, True)
            for part, values in enumerate((low, high)):
                for t in range(pairs // 2):
                    a, b = exchange(values[2 * t], values[2 * t + 1])
                    at = part * pairs + t
                    out_ref[0, rows, pl.ds(at * 128, 128)] = a
                    out_ref[0, rows, pl.ds((at + pairs // 2) * 128, 128)] = b
            if r < half // 8:
                low, high = lift(*with_halo(low[0::2], low[1::2]), 8, True, False)
                for i in range(8):
                    c_ref[pl.ds(64 * r + i, 8, stride=8), :] = low[i]
                    c_ref[pl.ds(corner + 64 * r + i, 8, stride=8), :] = high[i]
        for u in range(2):
            rows = scaled_rows([c_ref[pl.ds(u * corner + 8 * i, 8), :] for i in range(half)])
            store_terms(m_ref, 0, u * 128, rows)
        lifted = dot(m_ref[...], w2_ref[...])
        d_ref[0] = lifted[:, :128]
        d_ref[1] = lifted[:, 128:]
        for u in range(2):
            for t in range(4):
                for r in range(half // 8):
                    a = d_ref[u, pl.ds(64 * r + 2 * t, 8, stride=8), :]
                    b = d_ref[u, pl.ds(64 * r + 2 * t + 1, 8, stride=8), :]
                    for at, value in zip((u * 8 + t, u * 8 + 4 + t), exchange(a, b)):
                        rows, cols = pl.ds(8 * r, 8), pl.ds(at * 128, 128)
                        out_ref[0, rows, cols] = jnp.where(inner, value, out_ref[0, rows, cols])


def fine_call(owner_counts, token, density, first, last, before=None):
    slots, edge, plane = density.shape
    tiles = plane // 128
    half = edge // 2
    pairs = tiles // 2
    count = last - first
    one = pass_matrix(edge).T
    zero = np.zeros_like(one)
    w1 = np.block(
        [
            [one / SCALE, zero, zero, zero],
            [zero, zero, one * SCALE, zero],
            [zero, one / SCALE, zero, zero],
            [zero, zero, zero, one * SCALE],
        ]
    )
    two = np.zeros_like(one)
    two[:half, :half] = pass_matrix(half).T
    w2 = np.kron(np.diag([1 / SCALE, 1 / SCALE, SCALE, SCALE]), two)
    anywhere = pl.BlockSpec(memory_space=pl.ANY)
    smem = pl.BlockSpec(memory_space=pltpu.SMEM)
    old = [] if before is None else [before]
    fixed = pl.BlockSpec((768, 256), lambda s: (0, 0))
    return pl.pallas_call(
        functools.partial(fine_kernel, first=first),
        grid=(count,),
        in_specs=[smem, smem, anywhere, fixed, fixed] + [anywhere] * len(old),
        out_specs=[pl.BlockSpec((1, edge, plane), lambda s: (s + first, 0, 0)), smem],
        out_shape=[
            jax.ShapeDtypeStruct(density.shape, F32),
            jax.ShapeDtypeStruct((1,), jnp.int32),
        ],
        scratch_shapes=[
            pltpu.VMEM((2, edge // 8, tiles, 8, 128), F32),
            pltpu.VMEM((pairs * edge, 768), BF16),
            pltpu.VMEM((2, pairs * edge, 128), F32),
            pltpu.VMEM((16 * half, 128), F32),
            pltpu.VMEM((8 * half, 768), BF16),
            pltpu.VMEM((2, 8 * half, 128), F32),
            pltpu.SemaphoreType.DMA((2,)),
        ],
        input_output_aliases={5: 0} if old else {},
        compiler_params=pltpu.CompilerParams(vmem_limit_bytes=VMEM_LIMIT),
        cost_estimate=pl.CostEstimate(
            flops=6 * count * edge * plane * 256, bytes_accessed=2 * count * MIB, transcendentals=0
        ),
        name="fine",
    )(owner_counts, token, tiled_view(density), stacked(w1), stacked(w2), *old)


def coarse_kernel(
    index_ref,
    piece_ref,
    wx_ref,
    wzh_ref,
    wzl_ref,
    wyh_ref,
    wyl_ref,
    w23h_ref,
    w23l_ref,
    wx2_ref,
    wx3_ref,
    fine_ref,
    out_ref,
    block_ref,
    corner_ref,
    corner_sem,
    out_sem,
):
    slots = corner_ref.shape[0]
    lane = lax.broadcasted_iota(jnp.int32, (16, 128), 1)

    def window(s):
        return out_ref.at[s, pl.ds(0, 16), pl.ds(0, 1024)]

    def piece(i):
        return jnp.concatenate([piece_ref[pl.ds(16 * h + i, 16, stride=32), :] for h in range(2)], 1)

    for s in range(slots):
        pltpu.make_async_copy(window(s), corner_ref.at[s], corner_sem.at[s]).start()

    first = [
        [
            times_left(wx_ref[...], jnp.concatenate([piece(o * 8 + 2 * q), piece(o * 8 + 2 * q + 1)], 0))
            for q in range(4)
        ]
        for o in range(2)
    ]
    stacked = []
    for o in range(2):
        for cy in range(2):
            for yh in range(2):
                part = slice(yh * 128, yh * 128 + 128)
                stacked.append(jnp.concatenate([first[o][cy][:, part], first[o][2 + cy][:, part]], 1))
    lifted = times(jnp.concatenate(stacked, 0), wzh_ref[...], wzl_ref[...])
    stacked = []
    for o in range(2):
        for tz in range(2):
            stacked.append(
                jnp.concatenate(
                    [lifted[(o * 4 + u) * 32 : (o * 4 + u + 1) * 32, tz * 128 : tz * 128 + 128] for u in range(4)],
                    1,
                )
            )
    lifted = times(jnp.concatenate(stacked, 0), wyh_ref[...], wyl_ref[...])
    corner = []
    for o in range(2):
        for tz in range(2):
            for ty in range(2):
                for tx in range(2):
                    at = (o * 2 + tz) * 32 + tx * 16
                    value = lifted[at : at + 16, ty * 256 : ty * 256 + 256]
                    if tx + ty + tz == 0:
                        corner.append(value)
                    else:
                        block_ref[o * 8 + tx + 2 * ty + 4 * tz] = value
    both = times(jnp.concatenate(corner, 0), w23h_ref[...], w23l_ref[...])
    depth = lax.broadcasted_iota(jnp.int32, (16, 128), 0)
    small = (depth < 8) & ((lane & 15) < 8)
    for o in range(2):
        mine = both[o * 16 : o * 16 + 16]
        second = times_left(wx2_ref[...], mine[:, :256])
        third = times_left(wx3_ref[...], mine[:, 256:])
        block_ref[o * 8] = jnp.concatenate(
            [jnp.where(small, third, second[:, :128]), second[:, 128:]], 1
        )

    for s in range(slots):
        pltpu.make_async_copy(window(s), corner_ref.at[s], corner_sem.at[s]).wait()
    placed = (lane & 63) < 16
    for s in range(slots):
        value = block_ref[index_ref[0] + s]
        for t in range(8):
            tile = value[:, (t // 4) * 128 : (t // 4) * 128 + 128]
            if t % 4:
                tile = pltpu.roll(tile, 128 - 16 * (t % 4), 1)
            cols = pl.ds(t * 128, 128)
            corner_ref[s, :, cols] = jnp.where(placed, tile, corner_ref[s, :, cols])
    for s in range(slots):

        @pl.when(s < index_ref[1])
        def _():
            pltpu.make_async_copy(corner_ref.at[s], window(s), out_sem.at[s]).start()

    for s in range(slots):

        @pl.when(s < index_ref[1])
        def _():
            pltpu.make_async_copy(corner_ref.at[s], window(s), out_sem.at[s]).wait()


def coarse_call(index, pieces, fine):
    slots, edge, plane = fine.shape
    m32, m16, m8 = pass_matrix(32), pass_matrix(16), pass_matrix(8)
    deep = np.zeros((16, 16))
    deep[:8] = m8 @ m16[:8]
    eye8, eye16 = np.eye(8), np.eye(16)
    wz = np.zeros((256, 256))
    for cz in range(2):
        for tz in range(2):
            wz[cz * 128 : cz * 128 + 128, tz * 128 : tz * 128 + 128] = np.kron(
                eye8, m32[tz * 16 : tz * 16 + 16, cz * 16 : cz * 16 + 16].T
            )
    lanes = np.arange(256).reshape(2, 4, 2, 16).transpose(0, 2, 1, 3).reshape(-1)
    wy = np.kron(m32.T, eye16)[:, np.concatenate([lanes, 256 + lanes])]
    w23 = np.concatenate([np.kron(m16.T, m16.T)[:, lanes], np.kron(deep.T, deep.T)[:, lanes[:128]]], 1)[lanes]
    weights = [
        left_terms(m32),
        *two_terms(wz),
        *two_terms(wy),
        *two_terms(w23),
        left_terms(m16),
        left_terms(deep),
    ]
    anywhere = pl.BlockSpec(memory_space=pl.ANY)
    vmem = pl.BlockSpec(memory_space=pltpu.VMEM)
    return pl.pallas_call(
        coarse_kernel,
        in_specs=[pl.BlockSpec(memory_space=pltpu.SMEM), vmem] + [vmem] * len(weights) + [anywhere],
        out_specs=anywhere,
        out_shape=jax.ShapeDtypeStruct(fine.shape, F32),
        scratch_shapes=[
            pltpu.VMEM((16, 16, 256), F32),
            pltpu.VMEM((slots, 16, 1024), F32),
            pltpu.SemaphoreType.DMA((slots,)),
            pltpu.SemaphoreType.DMA((slots,)),
        ],
        input_output_aliases={2 + len(weights): 0},
        compiler_params=pltpu.CompilerParams(vmem_limit_bytes=VMEM_SMALL),
        name="coarse",
    )(index, pieces.reshape(-1, 128), *weights, fine)


def exchange(lowpass, slots, token):
    me = lax.axis_index(AXES)
    devices = lax.axis_size(AXES)
    if devices == lowpass.shape[0]:
        got = lax.all_to_all(lowpass, SWAPPED, 0, 0, tiled=True)
        sent, index = route_call(me.reshape(1), got, token, slots, lax.axis_size("dev"))
        return lax.all_to_all(sent, SWAPPED, 0, 0, tiled=True), index
    every = lax.all_gather(lowpass, AXES, axis=0)
    counts = every[:, 0, 7, 0].astype(jnp.int32)
    starts = jnp.cumsum(counts) - counts
    blocks = starts[me] // 8 * 8 + jnp.arange(16, dtype=jnp.int32)
    owners = jnp.sum((starts[None, :] <= blocks[:, None]).astype(jnp.int32), axis=1) - 1
    place = jnp.minimum(blocks - starts[owners], slots - 1)
    pieces = jnp.transpose(every[owners, :, place], (1, 0, 2))
    return pieces, jnp.stack([starts[me] % 8, counts[me]])


def per_device(density, owner_counts):
    slots = density.shape[0]
    early = slots // 3
    lowpass, token = lowpass_call(owner_counts, density)
    fine, token = fine_call(owner_counts, token, density, 0, early)
    pieces, index = exchange(lowpass, slots, token)
    fine, _ = fine_call(owner_counts, index, density, early, slots, fine)
    return coarse_call(index, pieces, fine)


def solution(mesh):
    in_specs = (P(AXES, None, None), P(AXES))
    out_specs = P(AXES, None, None)
    return jax.shard_map(per_device, mesh=mesh, in_specs=in_specs, out_specs=out_specs, check_vma=False)
```

```python
import functools

import jax
import jax.numpy as jnp
import numpy as np
from jax import lax
from jax.experimental import pallas as pl
from jax.experimental.pallas import tpu as pltpu
from jax.sharding import PartitionSpec as P

ALPHA = -1.586134342059924
BETA = -0.052980118572961
GAMMA = 0.882911075530934
DELTA = 0.443506852043971
SCALE = 1.230174104914001
SQUARE = SCALE * SCALE
F32 = jnp.float32
BF16 = jnp.bfloat16
AXES = ("node", "dev")
SWAPPED = ("dev", "node")
MIB = 1 << 20
VMEM_LIMIT = 48 * MIB
VMEM_SMALL = 16 * MIB
VMEM_LARGE = 56 * MIB


def pass_matrix(n):
    low, high = np.eye(n)[0::2], np.eye(n)[1::2]

    def after(v):
        return np.concatenate([v[1:], v[-1:]], 0)

    def before(v):
        return np.concatenate([v[:1], v[:-1]], 0)

    high = high + ALPHA * (low + after(low))
    low = low + BETA * (before(high) + high)
    high = high + GAMMA * (low + after(low))
    low = low + DELTA * (before(high) + high)
    return np.concatenate([low / SCALE, high * SCALE], 0)


def two_terms(matrix):
    matrix = np.asarray(matrix, np.float32)
    first = matrix.astype(BF16)
    return first, (matrix - first.astype(np.float32)).astype(BF16)


def left_terms(matrix):
    first, second = two_terms(matrix)
    return np.concatenate([first, second, first], 1)


def split(value):
    first = value.astype(BF16)
    return first, (value - first.astype(F32)).astype(BF16)


def dot(left, right):
    return jnp.dot(left, right, preferred_element_type=F32)


def times(value, first, second):
    high, low = split(value)
    both = dot(jnp.concatenate([high, low], 0), first)
    count = value.shape[0]
    return both[:count] + both[count:] + dot(high, second)


def times_left(terms, value):
    high, low = split(value)
    return dot(terms, jnp.concatenate([high, high, low], 0))


def split_rows(rows):
    return [split(jnp.concatenate(rows[m : m + 2], 0)) for m in range(0, len(rows), 2)]


def tiled_view(density):
    slots, edge, plane = density.shape
    view = density.reshape(slots, edge // 8, 8, plane // 128, 128)
    return jnp.transpose(view, (0, 1, 3, 2, 4))


def tile_rows(ref, block, group, edge, tiles):
    base = block * edge * tiles + 64 * group
    return [ref[pl.ds(base + (x // 8) * 8 * tiles + x % 8, 8, stride=8), :] for x in range(edge)]


def lowpass_kernel(
    count_ref, x_any, wz_any, wyh_any, wyl_any, out_ref, token_ref, x_ref, wz_ref, wyh_ref, wyl_ref, l_ref, k_ref, z_ref, sems, w_sems
):
    slots, edge, tiles = x_any.shape[0], 8 * x_any.shape[1], x_any.shape[2]
    quarter = edge // 4
    token_ref[0] = count_ref[0]
    blocks = [
        pltpu.make_async_copy(x_any.at[n], x_ref.at[n], sems.at[n]) for n in range(slots)
    ]
    for copy in blocks:
        copy.start()
    flat = x_ref.reshape(slots * edge * tiles, 128)
    weights = [
        pltpu.make_async_copy(src, dst, w_sems.at[i])
        for i, (src, dst) in enumerate(((wz_any, wz_ref), (wyh_any, wyh_ref), (wyl_any, wyl_ref)))
    ]
    for copy in weights:
        copy.start()
    part = slots // 2
    rows_part = part * 8 * quarter

    def first_dimension(s, g):
        rows = tile_rows(flat, s, g, edge, tiles)
        rows, _ = lift(rows[0::2], rows[1::2], edge // 2, False, False)
        rows, _ = lift(rows[0::2], rows[1::2], quarter, False, False)
        ref = (l_ref, k_ref)[s // part]
        for m, (high, low) in enumerate(split_rows(rows)):
            at = (s % part) * 8 * quarter + 16 * m
            cols = pl.ds((g % 2) * 256 + (g // 2) * 128, 128)
            ref[pl.ds(at, 16), cols] = high
            ref[pl.ds(rows_part + at, 16), cols] = low

    def third_dimension(ref, half):
        made = dot(ref[...], wz_ref[...])
        z_ref[pl.ds(half * rows_part, rows_part), :] = (
            made[:rows_part, :128] + made[rows_part:, :128]
        ) + made[:rows_part, 128:]

    for s in range(part):
        blocks[s].wait()
        for g in range(4):
            first_dimension(s, g)
    for copy in weights:
        copy.wait()
    for s in range(part, slots):
        blocks[s].wait()
    third_dimension(l_ref, 0)
    for s in range(part, slots):
        for g in range(4):
            first_dimension(s, g)
    third_dimension(k_ref, 1)
    wide = jnp.concatenate([z_ref[pl.ds(i, slots * quarter, stride=8), :] for i in range(8)], 1)
    made = times(wide, wyh_ref[...], wyl_ref[...])
    out_ref[...] = jnp.full(out_ref.shape, count_ref[0].astype(F32))
    for slot in range(slots):
        for h in range(2):
            out_ref[pl.ds(8 * h + slot, quarter, stride=16), :] = made[
                slot * quarter : (slot + 1) * quarter, h * 128 : h * 128 + 128
            ]


def stacked(matrix):
    first, second = two_terms(matrix)
    return np.concatenate([first, first, second], 0)


def lowpass_call(owner_counts, density):
    slots, edge, plane = density.shape
    quarter = edge // 4
    two_levels = pass_matrix(edge // 2)[:quarter] @ pass_matrix(edge)[: edge // 2]
    wz = np.concatenate(two_terms(np.kron(np.eye(8), two_levels.T)), 1)
    i, gp, q, p = np.meshgrid(np.arange(8), np.arange(2), np.arange(2), np.arange(2), indexing="ij")
    entry = (2 * (8 * gp + i) + p + 32 * q).reshape(-1)
    wy = np.kron(two_levels.T[entry] / SQUARE, np.eye(quarter))
    wyh, wyl = two_terms(wy)
    anywhere = pl.BlockSpec(memory_space=pl.ANY)
    vmem = pl.BlockSpec(memory_space=pltpu.VMEM)
    rows_all = slots * 8 * quarter
    pieces, token = pl.pallas_call(
        lowpass_kernel,
        in_specs=[pl.BlockSpec(memory_space=pltpu.SMEM)] + [anywhere] * 4,
        out_specs=[vmem, pl.BlockSpec(memory_space=pltpu.SMEM)],
        out_shape=[
            jax.ShapeDtypeStruct((16 * quarter, 128), F32),
            jax.ShapeDtypeStruct((1,), jnp.int32),
        ],
        scratch_shapes=[
            pltpu.VMEM((slots, edge // 8, plane // 128, 8, 128), F32),
            pltpu.VMEM(wz.shape, BF16),
            pltpu.VMEM(wyh.shape, BF16),
            pltpu.VMEM(wyl.shape, BF16),
            pltpu.VMEM((rows_all, 512), BF16),
            pltpu.VMEM((rows_all, 512), BF16),
            pltpu.VMEM((rows_all, 128), F32),
            pltpu.SemaphoreType.DMA((slots,)),
            pltpu.SemaphoreType.DMA((3,)),
        ],
        compiler_params=pltpu.CompilerParams(vmem_limit_bytes=VMEM_LARGE),
        name="lowpass",
    )(owner_counts, tiled_view(density), wz, wyh, wyl)
    return pieces.reshape(2 * quarter, 8, 128), token


def route_kernel(me_ref, got_ref, _, send_ref, index_ref, order_ref, count_ref, sem, *, width):
    devices = got_ref.shape[0]
    place = [d % width * (devices // width) + d // width for d in range(devices)]
    copy = pltpu.make_async_copy(got_ref.at[:, 7, :], count_ref, sem)
    copy.start()
    order_ref[...] = jnp.zeros_like(order_ref)
    copy.wait()
    start, my_start, my_count = 0, 0, 0
    starts = []
    for d in range(devices):
        count = count_ref[place[d], 0].astype(jnp.int32)
        starts.append(start)
        my_start = jnp.where(me_ref[0] == d, start, my_start)
        my_count = jnp.where(me_ref[0] == d, count, my_count)
        order_ref[pl.ds(start, 8), :] = got_ref[place[d]]
        start = start + count
    index_ref[0] = my_start % 8
    index_ref[1] = my_count
    for d in range(devices):
        at = pl.multiple_of(starts[d] // 8 * 8, 8) if d else 0
        send_ref[place[d]] = order_ref[pl.ds(at, 16), :]


def route_call(me, got, token, slots, width):
    devices = got.shape[0]
    return pl.pallas_call(
        functools.partial(route_kernel, width=width),
        in_specs=[
            pl.BlockSpec(memory_space=pltpu.SMEM),
            pl.BlockSpec(memory_space=pltpu.VMEM),
            pl.BlockSpec(memory_space=pltpu.SMEM),
        ],
        out_specs=[pl.BlockSpec(memory_space=pltpu.VMEM), pl.BlockSpec(memory_space=pltpu.SMEM)],
        out_shape=[
            jax.ShapeDtypeStruct((devices, 16, 128), F32),
            jax.ShapeDtypeStruct((2,), jnp.int32),
        ],
        scratch_shapes=[
            pltpu.VMEM((devices * slots + 16, 128), F32),
            pltpu.SMEM((devices, 128), F32),
            pltpu.SemaphoreType.DMA,
        ],
        compiler_params=pltpu.CompilerParams(vmem_limit_bytes=VMEM_SMALL),
        name="route",
    )(me, got, token)


def lift(low, high, n, halo, scaled):
    up = SQUARE if scaled else 1.0
    at = 2 if halo else 0
    first, second, third, fourth = ({} for _ in range(4))

    def get(values, i, is_low):
        if halo:
            return values[i]
        return values[min(i, n - 1)] if is_low else values[max(i, 0)]

    lows = {i - at: low[i] for i in range(len(low))}
    highs = {i - at: high[i] for i in range(len(high))}

    def make_first(i):
        first[i] = highs[i] + (ALPHA * up) * (lows[i] + get(lows, i + 1, True))

    def make_second(i):
        second[i] = lows[i] + (BETA / up) * (get(first, i - 1, False) + first[i])

    def make_third(i):
        third[i] = first[i] + (GAMMA * up) * (second[i] + get(second, i + 1, True))

    def make_fourth(i):
        fourth[i] = second[i] + (DELTA / up) * (get(third, i - 1, False) + third[i])

    if halo:
        for i in range(-2, n + 1):
            make_first(i)
            if i >= -1:
                make_second(i)
            if i >= 0:
                make_third(i - 1)
            if i >= 1:
                make_fourth(i - 1)
    else:
        for i in range(n):
            make_first(i)
            make_second(i)
            if i >= 1:
                make_third(i - 1)
                make_fourth(i - 1)
        make_third(n - 1)
        make_fourth(n - 1)
    return [fourth[i] for i in range(n)], [third[i] for i in range(n)]


def fine_kernel(count_ref, _, x_any, w1_ref, w2_ref, *refs, first):
    out_ref, token_ref, x_buf, l_ref, y_ref, c_ref, m_ref, d_ref, sems = refs[-9:]
    step = pl.program_id(0)
    slot = step + first
    edge, tiles = 8 * x_any.shape[1], x_any.shape[2]
    pairs = tiles // 2
    half = edge // 2
    corner = 8 * half
    live = slot < count_ref[0]
    lane = lax.broadcasted_iota(jnp.int32, (8, 128), 1)
    front = lane < 64
    inner = (lane & 63) < half
    token_ref[0] = step

    def cross(a, b):
        return pltpu.roll(jnp.where(front, b, a), 64, 1)

    def exchange(a, b):
        crossed = cross(a, b)
        return jnp.where(front, a, crossed), jnp.where(front, crossed, b)

    def with_halo(low, high):
        one, two = cross(low[0], low[-1]), cross(low[1], low[-2])
        low_all = [jnp.where(front, low[2], two), jnp.where(front, low[1], one)] + low
        low_all += [jnp.where(front, one, low[-1]), jnp.where(front, two, low[-2])]
        one, two = cross(high[0], high[-1]), cross(high[1], high[-2])
        high_all = [jnp.where(front, high[1], two), jnp.where(front, high[0], one)] + high
        return low_all, high_all + [jnp.where(front, one, high[-2])]

    def scaled_rows(rows):
        low, high = lift(rows[0::2], rows[1::2], len(rows) // 2, False, False)
        return [v * (1.0 / SCALE) for v in low] + [v * SCALE for v in high]

    def store_terms(ref, row, col, rows):
        for m, (high, low) in enumerate(split_rows(rows)):
            place = pl.ds(pl.multiple_of(row + 16 * m, 16), 16)
            ref[place, pl.ds(col, 128)] = high
            ref[place, pl.ds(256 + col, 128)] = low
            ref[place, pl.ds(512 + col, 128)] = high

    def fetch(which, place):
        return pltpu.make_async_copy(x_any.at[which], x_buf.at[place], sems.at[place])

    @pl.when((step == 0) & live)
    def _():
        fetch(slot, 0).start()

    @pl.when(jnp.logical_not(live))
    def _():
        out_ref[...] = jnp.zeros_like(out_ref)

    @pl.when(live)
    def _():
        fetch(slot, step % 2).wait()

    @pl.when((step + 1 < pl.num_programs(0)) & (slot + 1 < count_ref[0]))
    def _():
        fetch(slot + 1, (step + 1) % 2).start()

    @pl.when(live)
    def _():
        flat = x_buf.reshape(2 * edge * tiles, 128)
        for g in range(4):
            rows = scaled_rows(tile_rows(flat, step % 2, g, edge, tiles))
            store_terms(l_ref, (g % 2) * 8 * edge, (g // 2) * 128, rows)
        lifted = dot(l_ref[...], w1_ref[...])
        y_ref[0] = lifted[:, :128]
        y_ref[1] = lifted[:, 128:]
        for r in range(edge // 8):
            rows = pl.ds(8 * r, 8)

            def tile(part, j):
                return y_ref[part, pl.ds((j // 8) * 8 * edge + 64 * r + j % 8, 8, stride=8), :]

            low = [tile(0, j) for j in range(pairs)]
            high = [tile(1, j) for j in range(pairs)]
            low, high = lift(*with_halo(low, high), pairs, True, True)
            for part, values in enumerate((low, high)):
                for t in range(pairs // 2):
                    a, b = exchange(values[2 * t], values[2 * t + 1])
                    at = part * pairs + t
                    out_ref[0, rows, pl.ds(at * 128, 128)] = a
                    out_ref[0, rows, pl.ds((at + pairs // 2) * 128, 128)] = b
            if r < half // 8:
                low, high = lift(*with_halo(low[0::2], low[1::2]), 8, True, False)
                for i in range(8):
                    c_ref[pl.ds(64 * r + i, 8, stride=8), :] = low[i]
                    c_ref[pl.ds(corner + 64 * r + i, 8, stride=8), :] = high[i]
        for u in range(2):
            rows = scaled_rows([c_ref[pl.ds(u * corner + 8 * i, 8), :] for i in range(half)])
            store_terms(m_ref, 0, u * 128, rows)
        lifted = dot(m_ref[...], w2_ref[...])
        d_ref[0] = lifted[:, :128]
        d_ref[1] = lifted[:, 128:]
        for u in range(2):
            for t in range(4):
                for r in range(half // 8):
                    a = d_ref[u, pl.ds(64 * r + 2 * t, 8, stride=8), :]
                    b = d_ref[u, pl.ds(64 * r + 2 * t + 1, 8, stride=8), :]
                    for at, value in zip((u * 8 + t, u * 8 + 4 + t), exchange(a, b)):
                        rows, cols = pl.ds(8 * r, 8), pl.ds(at * 128, 128)
                        out_ref[0, rows, cols] = jnp.where(inner, value, out_ref[0, rows, cols])


def fine_call(owner_counts, token, density, first, last, before=None):
    slots, edge, plane = density.shape
    tiles = plane // 128
    half = edge // 2
    pairs = tiles // 2
    count = last - first
    one = pass_matrix(edge).T
    zero = np.zeros_like(one)
    w1 = np.block(
        [
            [one / SCALE, zero, zero, zero],
            [zero, zero, one * SCALE, zero],
            [zero, one / SCALE, zero, zero],
            [zero, zero, zero, one * SCALE],
        ]
    )
    two = np.zeros_like(one)
    two[:half, :half] = pass_matrix(half).T
    w2 = np.kron(np.diag([1 / SCALE, 1 / SCALE, SCALE, SCALE]), two)
    anywhere = pl.BlockSpec(memory_space=pl.ANY)
    smem = pl.BlockSpec(memory_space=pltpu.SMEM)
    old = [] if before is None else [before]
    fixed = pl.BlockSpec((768, 256), lambda s: (0, 0))
    return pl.pallas_call(
        functools.partial(fine_kernel, first=first),
        grid=(count,),
        in_specs=[smem, smem, anywhere, fixed, fixed] + [anywhere] * len(old),
        out_specs=[pl.BlockSpec((1, edge, plane), lambda s: (s + first, 0, 0)), smem],
        out_shape=[
            jax.ShapeDtypeStruct(density.shape, F32),
            jax.ShapeDtypeStruct((1,), jnp.int32),
        ],
        scratch_shapes=[
            pltpu.VMEM((2, edge // 8, tiles, 8, 128), F32),
            pltpu.VMEM((pairs * edge, 768), BF16),
            pltpu.VMEM((2, pairs * edge, 128), F32),
            pltpu.VMEM((16 * half, 128), F32),
            pltpu.VMEM((8 * half, 768), BF16),
            pltpu.VMEM((2, 8 * half, 128), F32),
            pltpu.SemaphoreType.DMA((2,)),
        ],
        input_output_aliases={5: 0} if old else {},
        compiler_params=pltpu.CompilerParams(vmem_limit_bytes=VMEM_LIMIT),
        cost_estimate=pl.CostEstimate(
            flops=6 * count * edge * plane * 256, bytes_accessed=2 * count * MIB, transcendentals=0
        ),
        name="fine",
    )(owner_counts, token, tiled_view(density), stacked(w1), stacked(w2), *old)


def coarse_kernel(
    index_ref,
    piece_ref,
    wx_ref,
    wzh_ref,
    wzl_ref,
    wyh_ref,
    wyl_ref,
    w23h_ref,
    w23l_ref,
    wx2_ref,
    wx3_ref,
    fine_ref,
    out_ref,
    block_ref,
    corner_ref,
    corner_sem,
    out_sem,
):
    slots = corner_ref.shape[0]
    lane = lax.broadcasted_iota(jnp.int32, (16, 128), 1)

    def window(s):
        return out_ref.at[s, pl.ds(0, 16), pl.ds(0, 1024)]

    def piece(i):
        return jnp.concatenate([piece_ref[pl.ds(16 * h + i, 16, stride=32), :] for h in range(2)], 1)

    for s in range(slots):
        pltpu.make_async_copy(window(s), corner_ref.at[s], corner_sem.at[s]).start()

    first = [
        [
            times_left(wx_ref[...], jnp.concatenate([piece(o * 8 + 2 * q), piece(o * 8 + 2 * q + 1)], 0))
            for q in range(4)
        ]
        for o in range(2)
    ]
    stacked = []
    for o in range(2):
        for cy in range(2):
            for yh in range(2):
                part = slice(yh * 128, yh * 128 + 128)
                stacked.append(jnp.concatenate([first[o][cy][:, part], first[o][2 + cy][:, part]], 1))
    lifted = times(jnp.concatenate(stacked, 0), wzh_ref[...], wzl_ref[...])
    stacked = []
    for o in range(2):
        for tz in range(2):
            stacked.append(
                jnp.concatenate(
                    [lifted[(o * 4 + u) * 32 : (o * 4 + u + 1) * 32, tz * 128 : tz * 128 + 128] for u in range(4)],
                    1,
                )
            )
    lifted = times(jnp.concatenate(stacked, 0), wyh_ref[...], wyl_ref[...])
    corner = []
    for o in range(2):
        for tz in range(2):
            for ty in range(2):
                for tx in range(2):
                    at = (o * 2 + tz) * 32 + tx * 16
                    value = lifted[at : at + 16, ty * 256 : ty * 256 + 256]
                    if tx + ty + tz == 0:
                        corner.append(value)
                    else:
                        block_ref[o * 8 + tx + 2 * ty + 4 * tz] = value
    both = times(jnp.concatenate(corner, 0), w23h_ref[...], w23l_ref[...])
    depth = lax.broadcasted_iota(jnp.int32, (16, 128), 0)
    small = (depth < 8) & ((lane & 15) < 8)
    for o in range(2):
        mine = both[o * 16 : o * 16 + 16]
        second = times_left(wx2_ref[...], mine[:, :256])
        third = times_left(wx3_ref[...], mine[:, 256:])
        block_ref[o * 8] = jnp.concatenate(
            [jnp.where(small, third, second[:, :128]), second[:, 128:]], 1
        )

    for s in range(slots):
        pltpu.make_async_copy(window(s), corner_ref.at[s], corner_sem.at[s]).wait()
    placed = (lane & 63) < 16
    for s in range(slots):
        value = block_ref[index_ref[0] + s]
        for t in range(8):
            tile = value[:, (t // 4) * 128 : (t // 4) * 128 + 128]
            if t % 4:
                tile = pltpu.roll(tile, 128 - 16 * (t % 4), 1)
            cols = pl.ds(t * 128, 128)
            corner_ref[s, :, cols] = jnp.where(placed, tile, corner_ref[s, :, cols])
    for s in range(slots):

        @pl.when(s < index_ref[1])
        def _():
            pltpu.make_async_copy(corner_ref.at[s], window(s), out_sem.at[s]).start()

    for s in range(slots):

        @pl.when(s < index_ref[1])
        def _():
            pltpu.make_async_copy(corner_ref.at[s], window(s), out_sem.at[s]).wait()


def coarse_call(index, pieces, fine):
    slots, edge, plane = fine.shape
    m32, m16, m8 = pass_matrix(32), pass_matrix(16), pass_matrix(8)
    deep = np.zeros((16, 16))
    deep[:8] = m8 @ m16[:8]
    eye8, eye16 = np.eye(8), np.eye(16)
    wz = np.zeros((256, 256))
    for cz in range(2):
        for tz in range(2):
            wz[cz * 128 : cz * 128 + 128, tz * 128 : tz * 128 + 128] = np.kron(
                eye8, m32[tz * 16 : tz * 16 + 16, cz * 16 : cz * 16 + 16].T
            )
    lanes = np.arange(256).reshape(2, 4, 2, 16).transpose(0, 2, 1, 3).reshape(-1)
    wy = np.kron(m32.T, eye16)[:, np.concatenate([lanes, 256 + lanes])]
    w23 = np.concatenate([np.kron(m16.T, m16.T)[:, lanes], np.kron(deep.T, deep.T)[:, lanes[:128]]], 1)[lanes]
    weights = [
        left_terms(m32),
        *two_terms(wz),
        *two_terms(wy),
        *two_terms(w23),
        left_terms(m16),
        left_terms(deep),
    ]
    anywhere = pl.BlockSpec(memory_space=pl.ANY)
    vmem = pl.BlockSpec(memory_space=pltpu.VMEM)
    return pl.pallas_call(
        coarse_kernel,
        in_specs=[pl.BlockSpec(memory_space=pltpu.SMEM), vmem] + [vmem] * len(weights) + [anywhere],
        out_specs=anywhere,
        out_shape=jax.ShapeDtypeStruct(fine.shape, F32),
        scratch_shapes=[
            pltpu.VMEM((16, 16, 256), F32),
            pltpu.VMEM((slots, 16, 1024), F32),
            pltpu.SemaphoreType.DMA((slots,)),
            pltpu.SemaphoreType.DMA((slots,)),
        ],
        input_output_aliases={2 + len(weights): 0},
        compiler_params=pltpu.CompilerParams(vmem_limit_bytes=VMEM_SMALL),
        name="coarse",
    )(index, pieces.reshape(-1, 128), *weights, fine)


def exchange(lowpass, slots, token):
    me = lax.axis_index(AXES)
    devices = lax.axis_size(AXES)
    if devices == lowpass.shape[0]:
        got = lax.all_to_all(lowpass, SWAPPED, 0, 0, tiled=True)
        sent, index = route_call(me.reshape(1), got, token, slots, lax.axis_size("dev"))
        return lax.all_to_all(sent, SWAPPED, 0, 0, tiled=True), index
    every = lax.all_gather(lowpass, AXES, axis=0)
    counts = every[:, 0, 7, 0].astype(jnp.int32)
    starts = jnp.cumsum(counts) - counts
    blocks = starts[me] // 8 * 8 + jnp.arange(16, dtype=jnp.int32)
    owners = jnp.sum((starts[None, :] <= blocks[:, None]).astype(jnp.int32), axis=1) - 1
    place = jnp.minimum(blocks - starts[owners], slots - 1)
    pieces = jnp.transpose(every[owners, :, place], (1, 0, 2))
    return pieces, jnp.stack([starts[me] % 8, counts[me]])


def per_device(density, owner_counts):
    slots = density.shape[0]
    early = slots // 3
    lowpass, token = lowpass_call(owner_counts, density)
    fine, token = fine_call(owner_counts, token, density, 0, early)
    pieces, index = exchange(lowpass, slots, token)
    fine, _ = fine_call(owner_counts, index, density, early, slots, fine)
    return coarse_call(index, pieces, fine)


def solution(mesh):
    in_specs = (P(AXES, None, None), P(AXES))
    out_specs = P(AXES, None, None)
    return jax.shard_map(per_device, mesh=mesh, in_specs=in_specs, out_specs=out_specs, check_vma=False)
```
